512 devices in a mesh: lon: 32 (over z_hi, y, core), lat: 16 (over x, z_lo).
Axes of the slice: x: 4, y: 4, z: 16 (z_hi: 4, z_lo: 4; z = z_hi * 4 + z_lo), core: 2. Of those that a mesh axis runs over, the one named last changes fastest.
Arguments:
- zonal_flow_middle: float32 [8, 512, 8192], P(None, 'lat', 'lon'), may hold values from -6 to 6
- meridional_flow_middle: float32 [8, 512, 8192], P(None, 'lat', 'lon'), may hold values from -6 to 6
- heat_content: float32 [8, 512, 8192], P(None, 'lat', 'lon'), may hold values from -6 to 6
- ocean_strata_number: int32 [512, 8192], P('lat', 'lon'), may hold values from 0 to 8
- former_free_elevation: float32 [512, 8192], P('lat', 'lon'), may hold values from -6 to 6
Outputs:
- zonal_new: float32 [8, 512, 8192], P(None, 'lat', 'lon')
- meridional_new: float32 [8, 512, 8192], P(None, 'lat', 'lon')
- temperature_new: float32 [8, 512, 8192], P(None, 'lat', 'lon')
- surface_pressure: float32 [512, 8192], P('lat', 'lon')
The draws below stay inside these ranges and needn't reach their ends.
All inputs are finite; a program needn't handle non-finite values.
Results may differ from the reference program's by a relative error of at most 0.035.
Values sent between devices are 32-bit elements; how exact they have to be, the bound alone decides.
A program may use at most 64 MiB of HBM per device.

```python
import jax
import jax.numpy as jnp
from jax import lax

VERTICAL_STRATA = 8
GRIDS = 3
CYCLES = 3
SWEEPS = 4
MESH_MERID_CELLS = 512
MESH_ZONAL_CELLS = 8192


def with_ends(result, rng, low, top_value):
    longest = result.shape.index(max(result.shape))
    spots = []
    for shift in (0, 1):
        where = [jax.random.randint(jax.random.fold_in(rng, axis), (), 0, length) for axis, length in enumerate(result.shape)]
        where[longest] = (where[longest] + shift) % result.shape[longest]
        spots.append(tuple(where))
    return result.at[spots[0]].set(low).at[spots[1]].set(top_value)


def shard_levels(own_key, extent, cuts, low, high):
    gain = 1.0
    for axis_at, parts in cuts:
        draws = jax.random.uniform(jax.random.fold_in(jax.random.fold_in(own_key, 6), axis_at), (parts,), jnp.float32, low / len(cuts), high / len(cuts))
        gain = gain * jnp.repeat(jnp.exp(draws), extent[axis_at] // parts).reshape((-1,) + (1,) * (len(extent) - 1 - axis_at))
    return gain


def centred(rng, extent, scale, bound, shards=(), held_as=jnp.bfloat16):
    drawn = scale * jax.random.normal(rng, extent, jnp.float32)
    if shards:
        drawn = drawn * shard_levels(rng, extent, shards, -0.22, 0.18)
    return jnp.clip(drawn, -bound, bound).astype(held_as)


def setup_inputs(seed: int = 0) -> dict:
    keys = jax.random.split(jax.random.key(seed), 6)
    return {
        "zonal_flow_middle": centred(keys[0], (VERTICAL_STRATA, MESH_MERID_CELLS, MESH_ZONAL_CELLS), 1.0, 6.0, ((1, 16), (2, 32)), jnp.float32),
        "meridional_flow_middle": centred(keys[1], (VERTICAL_STRATA, MESH_MERID_CELLS, MESH_ZONAL_CELLS), 1.0, 6.0, ((1, 16), (2, 32)), jnp.float32),
        "heat_content": centred(keys[2], (VERTICAL_STRATA, MESH_MERID_CELLS, MESH_ZONAL_CELLS), 1.0, 6.0, ((1, 16), (2, 32)), jnp.float32),
        "ocean_strata_number": with_ends(jax.random.randint(keys[3], (MESH_MERID_CELLS, MESH_ZONAL_CELLS), 0, VERTICAL_STRATA + 1), jax.random.fold_in(keys[3], 1), 0, VERTICAL_STRATA).astype(jnp.int32),
        "former_free_elevation": centred(keys[4], (MESH_MERID_CELLS, MESH_ZONAL_CELLS), 1.0, 6.0, ((0, 16), (1, 32)), jnp.float32),
    }


TIME_STEP = 0.2
VISCOSITY = 1.0
DIFFUSIVITY = 1.0
CORIOLIS = 1.0
MASS_TERM = 0.05
GRAVITY_STEP = 0.5


def neighbours(values):
    eastern = jnp.roll(values, -1, axis=-1)
    western = jnp.roll(values, 1, axis=-1)
    border = jnp.zeros_like(values[..., :1, :])
    northern = jnp.concatenate([values[..., 1:, :], border], axis=-2)
    southern = jnp.concatenate([border, values[..., :-1, :]], axis=-2)
    return eastern, western, northern, southern


def rotation_rate(row_index, total_rows):
    return CORIOLIS * jnp.sin(jnp.pi * ((row_index + 0.5) / total_rows - 0.5))


def baroclinic(layer_index, eastward, northward, tracer, column_depth_count, near_east, near_north, near_tracer, near_depth, rotation):
    wet_cell = (layer_index < column_depth_count).astype(jnp.float32)
    face_open = [wet_cell * (layer_index < beside_depth).astype(jnp.float32) for beside_depth in near_depth]

    def laplace(values, nearby):
        return (face_open[0] * (nearby[0] - values) + face_open[1] * (nearby[1] - values)) + (face_open[2] * (nearby[2] - values) + face_open[3] * (nearby[3] - values))

    east_flow = face_open[0] * (eastward + near_east[0]) * 0.5
    west_flow = face_open[1] * (near_east[1] + eastward) * 0.5
    north_flow = face_open[2] * (northward + near_north[2]) * 0.5
    south_flow = face_open[3] * (near_north[3] + northward) * 0.5
    transport = (east_flow * (tracer + near_tracer[0]) - west_flow * (near_tracer[1] + tracer)) + (north_flow * (tracer + near_tracer[2]) - south_flow * (near_tracer[3] + tracer))
    advected_scalar = wet_cell * (tracer + TIME_STEP * (DIFFUSIVITY * laplace(tracer, near_tracer) - 0.5 * transport))
    zonal_flow_guess = wet_cell * (eastward + TIME_STEP * (VISCOSITY * laplace(eastward, near_east) + rotation * northward))
    meridional_flow_guess = wet_cell * (northward + TIME_STEP * (VISCOSITY * laplace(northward, near_north) - rotation * eastward))
    return zonal_flow_guess, meridional_flow_guess, advected_scalar


def barotropic_source(near_east, near_north, column_depth_count, former_free_elevation):
    spread = 0.5 * ((near_east[0] - near_east[1]) + (near_north[2] - near_north[3]))
    wet_column = (column_depth_count > 0.5).astype(jnp.float32)
    return wet_column * (former_free_elevation - spread)


def fine_coefficients(column_depth_count, near_depth):
    column = column_depth_count * (1.0 / VERTICAL_STRATA)
    weights = [jnp.minimum(column, beside_depth * (1.0 / VERTICAL_STRATA)) for beside_depth in near_depth]
    return (jnp.full_like(column, MASS_TERM), weights[0], weights[1], weights[2], weights[3])


def restrict(values):
    paired = values[..., 0::2, :] + values[..., 1::2, :]
    return paired[..., 0::2] + paired[..., 1::2]


def prolong(values):
    return jnp.repeat(jnp.repeat(values, 2, axis=-2), 2, axis=-1)


def coarse_coefficients(coeffs):
    mass_field, east_weight, west_weight, north_weight, south_weight = coeffs
    return (restrict(mass_field),
            east_weight[0::2, 1::2] + east_weight[1::2, 1::2],
            west_weight[0::2, 0::2] + west_weight[1::2, 0::2],
            north_weight[1::2, 0::2] + north_weight[1::2, 1::2],
            south_weight[0::2, 0::2] + south_weight[0::2, 1::2])


def hierarchy(coeffs):
    grids_list = [coeffs]
    for grid_number in range(GRIDS):
        grids_list.append(coarse_coefficients(grids_list[-1]))
    return grids_list


def apply_operator(coeffs, pressure, nearby):
    mass_field, east_weight, west_weight, north_weight, south_weight = coeffs
    diagonal = mass_field + ((east_weight + west_weight) + (north_weight + south_weight))
    return diagonal * pressure - ((east_weight * nearby[0] + west_weight * nearby[1]) + (north_weight * nearby[2] + south_weight * nearby[3]))


def smooth_sweep(coeffs, pressure, source, nearby):
    mass_field, east_weight, west_weight, north_weight, south_weight = coeffs
    divisor = mass_field + 2.0 * ((east_weight + west_weight) + (north_weight + south_weight))
    if pressure is None:
        return source / divisor
    return pressure + (source - apply_operator(coeffs, pressure, nearby)) / divisor


def coarse_sweeps(coeffs, source, near_fn):
    pressure = smooth_sweep(coeffs, None, source, None)
    for sweep_number in range(SWEEPS - 1):
        pressure = smooth_sweep(coeffs, pressure, source, near_fn(pressure))
    return pressure


def multigrid_cycle(grids_list, grid_number, source, pressure, near_fn, coarse_solve):
    coeffs = grids_list[grid_number]
    if grid_number == len(grids_list) - 1:
        return coarse_solve(coeffs, source)
    pressure = smooth_sweep(coeffs, pressure, source, None if pressure is None else near_fn(pressure))
    residual = source - apply_operator(coeffs, pressure, near_fn(pressure))
    correction = multigrid_cycle(grids_list, grid_number + 1, restrict(residual), None, near_fn, coarse_solve)
    pressure = pressure + prolong(correction)
    return smooth_sweep(coeffs, pressure, source, near_fn(pressure))


def corrected(wet_cell, zonal_flow_guess, meridional_flow_guess, near_surface):
    slope_east = 0.5 * (near_surface[0] - near_surface[1])
    slope_north = 0.5 * (near_surface[2] - near_surface[3])
    return wet_cell * (zonal_flow_guess - GRAVITY_STEP * slope_east), wet_cell * (meridional_flow_guess - GRAVITY_STEP * slope_north)


def reference(zonal_flow_middle, meridional_flow_middle, heat_content, ocean_strata_number, former_free_elevation):
    column_depth_count = ocean_strata_number.astype(jnp.float32)
    near_depth = neighbours(column_depth_count)
    rotation = rotation_rate(jnp.arange(MESH_MERID_CELLS).astype(jnp.float32), MESH_MERID_CELLS)[:, None]

    def lone_stratum(pieces):
        layer_index, eastward, northward, tracer = pieces
        return baroclinic(layer_index.astype(jnp.float32), eastward, northward, tracer, column_depth_count,
                          neighbours(eastward), neighbours(northward), neighbours(tracer), near_depth, rotation)

    zonal_flow_guess, meridional_flow_guess, advected_scalar = lax.map(lone_stratum, (jnp.arange(VERTICAL_STRATA), zonal_flow_middle, meridional_flow_middle, heat_content))
    mean_east = jnp.sum(zonal_flow_guess, axis=0) * (1.0 / VERTICAL_STRATA)
    mean_north = jnp.sum(meridional_flow_guess, axis=0) * (1.0 / VERTICAL_STRATA)
    source = barotropic_source(neighbours(mean_east), neighbours(mean_north), column_depth_count, former_free_elevation)
    grids_list = hierarchy(fine_coefficients(column_depth_count, near_depth))

    def coarse_solve(coeffs, coarse_source):
        return coarse_sweeps(coeffs, coarse_source, neighbours)

    pressure = None
    for cycle_number in range(CYCLES):
        pressure = multigrid_cycle(grids_list, 0, source, pressure, neighbours, coarse_solve)
    layers = jnp.arange(VERTICAL_STRATA).astype(jnp.float32)[:, None, None]
    wet_cell = (layers < column_depth_count).astype(jnp.float32)
    zonal_new, meridional_new = corrected(wet_cell, zonal_flow_guess, meridional_flow_guess, neighbours(pressure))
    return (zonal_new, meridional_new, advected_scalar, pressure)
```

```python
import functools

import jax
import jax.numpy as jnp
from jax import lax
from jax.experimental import pallas as pl
from jax.experimental.pallas import tpu as pltpu
from jax.sharding import PartitionSpec as P

LEVELS = 8
CYCLES = 3
SWEEPS = 4
TIME_STEP = 0.2
VISCOSITY = 1.0
DIFFUSIVITY = 1.0
CORIOLIS = 1.0
MASS_TERM = 0.05
GRAVITY_STEP = 0.5

ROWS = 32
COLS = 256
LANES = 128
WIDE = 512
MESH_IDS = pl.DeviceIdType.MESH

CLASSES = (4, 2, 1, 1)
STEP = (1, 1, 1, 2)
ORIGIN = (72, 40, 24, 16)
HEIGHT = (176, 96, 56, 40)
MASS = tuple(MASS_TERM * 4.0**g for g in range(4))

LAT_MOVES = (1, -1, 2, -2)


def east_of(parts, step):
    turned = pltpu.roll(parts[0], LANES - step, 1)
    return list(parts[1:]) + [turned]


def west_of(parts, step):
    turned = pltpu.roll(parts[-1], step, 1)
    return [turned] + list(parts[:-1])


def each_chunk(first, last, body, unroll=5):
    count = (last - first) // 8
    if count <= unroll:
        for i in range(count):
            body(first + 8 * i)
        return
    while count % unroll:
        unroll -= 1

    def step(i, carry):
        for j in range(unroll):
            body(pl.multiple_of(first + (i * unroll + j) * 8, 8))
        return carry

    lax.fori_loop(0, count // unroll, step, 0)


def split_three(values):
    high = values.astype(jnp.bfloat16)
    rest = values - high.astype(jnp.float32)
    middle = rest.astype(jnp.bfloat16)
    low = (rest - middle.astype(jnp.float32)).astype(jnp.bfloat16)
    return jnp.concatenate([high, middle, low], axis=0)


def exact_select(values, choice):
    count = values.shape[0]
    product = jnp.dot(split_three(values), choice, preferred_element_type=jnp.float32)
    return (product[:count] + product[count : 2 * count]) + product[2 * count :]


def kernel(
    lon_count,
    lat_count,
    u_ref,
    v_ref,
    t_ref,
    depth_ref,
    elevation_ref,
    u_out,
    v_out,
    t_out,
    p_out,
    u_star,
    v_star,
    rows_send,
    rows_got,
    cols_send,
    cols_got,
    mean_send,
    mean_got,
    deep_send,
    deep_got,
    source_send,
    source_got,
    coarse_send,
    coarse_got,
    choice,
    unchoice,
    deep,
    grid_b,
    grid_p,
    grid_q,
    grid_we,
    grid_ww,
    grid_wn,
    grid_dg,
    grid_iv,
    grid_r,
    send_sem,
    recv_sem,
):
    lon = lax.axis_index("lon")
    lat = lax.axis_index("lat")
    sems = iter(range(64))

    def there(lon_move, lat_move):
        return {
            "lon": lax.rem(lon + lon_move + lon_count, lon_count),
            "lat": lax.rem(lat + lat_move + lat_count, lat_count),
        }

    def send(source, target, lon_move, lat_move):
        at = next(sems)
        return pltpu.make_async_remote_copy(
            src_ref=source,
            dst_ref=target,
            send_sem=send_sem.at[at],
            recv_sem=recv_sem.at[at],
            device_id=there(lon_move, lat_move),
            device_id_type=MESH_IDS,
        )

    def inside(lat_move):
        spot = lat + lat_move
        return jnp.where((spot >= 0) & (spot < lat_count), 1.0, 0.0).astype(jnp.float32)

    started = []

    def launch(copies):
        for copy in copies:
            copy.start()
        started.extend(copies)

    barrier = pltpu.get_barrier_semaphore()
    for lon_move, lat_move in [(1, 0), (-1, 0)] + [(0, m) for m in LAT_MOVES]:
        pl.semaphore_signal(
            barrier, inc=1, device_id=there(lon_move, lat_move), device_id_type=MESH_IDS
        )

    depth = depth_ref[...].astype(jnp.float32)
    lane8 = lax.broadcasted_iota(jnp.int32, (8, LANES), 1)
    fields = (u_ref, v_ref, t_ref)
    for side, row in ((0, ROWS - 1), (1, 0)):
        for f, field in enumerate(fields):
            for k in range(LEVELS):
                rows_send[side, 8 * f + k : 8 * f + k + 1, :] = field[
                    k * ROWS + row : k * ROWS + row + 1, :
                ]
        rows_send[side, pl.ds(24, 8), :] = jnp.broadcast_to(depth[row : row + 1, :], (8, COLS))

    def pack(i, carry):
        at_last, at_first = carry
        rows = pl.ds(pl.multiple_of(8 * i, 8), 8)
        for f, field in enumerate(fields):
            here = lane8 == i + 32 * f
            at_last = jnp.where(here, field[rows, COLS - 1 : COLS], at_last)
            at_first = jnp.where(here, field[rows, 0:1], at_first)
        return at_last, at_first

    zero8 = jnp.zeros((8, LANES), jnp.float32)
    at_last, at_first = lax.fori_loop(0, 32, pack, (zero8, zero8), unroll=4)
    elevation = elevation_ref[...]
    for side, edge, tile in ((0, at_last, 1), (1, at_first, 0)):
        cut = slice(tile * LANES, (tile + 1) * LANES)
        cols_send[side, 0:32, :] = depth[:, cut]
        cols_send[side, 32:64, :] = elevation[:, cut]
        cols_send[side, 64:72, :] = edge

    pl.semaphore_wait(barrier, 2 + len(LAT_MOVES))
    first = [
        send(cols_send.at[0], cols_got.at[0], 1, 0),
        send(cols_send.at[1], cols_got.at[1], -1, 0),
        send(rows_send.at[0], rows_got.at[0], 0, 1),
        send(rows_send.at[1], rows_got.at[1], 0, -1),
    ]
    launch(first)

    def order(n):
        return ((((n & 127) + 32) & 127) << 2) + (n >> 7)

    wanted = order(lax.broadcasted_iota(jnp.int32, (1, WIDE), 1))

    def fill(i, carry):
        rows = pl.ds(pl.multiple_of(32 * i, 32), 32)
        k = lax.broadcasted_iota(jnp.int32, (32, WIDE), 0) + 32 * i
        choice[rows, :] = jnp.where(k == wanted, 1.0, 0.0).astype(jnp.bfloat16)
        n = lax.broadcasted_iota(jnp.int32, (32, COLS), 0) + 32 * i
        column = lax.broadcasted_iota(jnp.int32, (32, COLS), 1) + LANES
        unchoice[rows, :] = jnp.where(order(n) == column, 1.0, 0.0).astype(jnp.bfloat16)
        return carry

    lax.fori_loop(0, WIDE // 32, fill, 0)
    for ref in list(grid_p) + list(grid_q) + list(grid_b) + list(grid_wn) + [deep]:
        ref[...] = jnp.zeros_like(ref)
    row_number = lax.broadcasted_iota(jnp.int32, (ROWS, LANES), 0)
    place = (lat * ROWS + row_number).astype(jnp.float32)
    angle = jnp.pi * ((place + 0.5) / (ROWS * lat_count) - 0.5)
    turning = CORIOLIS * jnp.sin(angle)
    rotation = jnp.concatenate([turning, turning], axis=1)

    for copy in first:
        copy.wait_recv()

    west_tile, east_tile = cols_got.at[0], cols_got.at[1]
    depth_wide = jnp.concatenate([west_tile[0:32, :], depth, east_tile[0:32, :]], axis=1)
    by_class = jnp.dot(
        depth_wide.astype(jnp.bfloat16), choice[...], preferred_element_type=jnp.float32
    )
    for c in range(4):
        deep_send[32 * c : 32 * c + 32, :] = by_class[:, LANES * c : LANES * (c + 1)]
    depth_copies = [
        send(deep_send, deep_got.at[i], 0, move) for i, move in enumerate(LAT_MOVES)
    ]
    launch(depth_copies)

    row = lax.broadcasted_iota(jnp.int32, (ROWS, COLS), 0)
    column = lax.broadcasted_iota(jnp.int32, (ROWS, COLS), 1)
    on_east, on_west = column == COLS - 1, column == 0
    on_north, on_south = row == ROWS - 1, row == 0

    def beside(values, east_edge, west_edge, north_edge, south_edge):
        return (
            jnp.where(on_east, east_edge, pltpu.roll(values, COLS - 1, 1)),
            jnp.where(on_west, west_edge, pltpu.roll(values, 1, 1)),
            jnp.where(on_north, north_edge, pltpu.roll(values, ROWS - 1, 0)),
            jnp.where(on_south, south_edge, pltpu.roll(values, 1, 0)),
        )

    depth_near = beside(
        depth,
        east_tile[0:32, 0:1],
        west_tile[0:32, LANES - 1 : LANES],
        rows_got[1, 24:25, :] * inside(1),
        rows_got[0, 24:25, :] * inside(-1),
    )
    open_depth = [jnp.minimum(depth, near) for near in depth_near]
    east_edges = east_tile[64:72, :]
    west_edges = west_tile[64:72, :]

    def near_field(f, field, k):
        values = field[pl.ds(pl.multiple_of(k * ROWS, ROWS), ROWS), :]
        turn = lax.rem(2 * LANES - 32 * f - 4 * k, LANES)
        east_lanes = pltpu.roll(east_edges, turn, 1)
        west_lanes = pltpu.roll(west_edges, turn, 1)
        east_edge = jnp.concatenate([east_lanes[:, g : g + 1] for g in range(4)], axis=0)
        west_edge = jnp.concatenate([west_lanes[:, g : g + 1] for g in range(4)], axis=0)
        north_edge = rows_got[1, pl.ds(8 * f + k, 1), :]
        south_edge = rows_got[0, pl.ds(8 * f + k, 1), :]
        return values, beside(values, east_edge, west_edge, north_edge, south_edge)

    def laplace(faces, values, nearby):
        terms = [jnp.where(face, near - values, 0.0) for face, near in zip(faces, nearby)]
        return (terms[0] + terms[1]) + (terms[2] + terms[3])

    def momentum(k, carry):
        sum_u, sum_v = carry
        level = k.astype(jnp.float32)
        faces = [level < limit for limit in open_depth]
        wet = level < depth
        u, near_u = near_field(0, u_ref, k)
        v, near_v = near_field(1, v_ref, k)
        guess_u = u + TIME_STEP * (VISCOSITY * laplace(faces, u, near_u) + rotation * v)
        guess_v = v + TIME_STEP * (VISCOSITY * laplace(faces, v, near_v) - rotation * u)
        guess_u = jnp.where(wet, guess_u, 0.0)
        guess_v = jnp.where(wet, guess_v, 0.0)
        rows = pl.ds(pl.multiple_of(k * ROWS, ROWS), ROWS)
        u_star[rows, :] = guess_u
        v_star[rows, :] = guess_v
        return sum_u + guess_u, sum_v + guess_v

    zero = jnp.zeros((ROWS, COLS), jnp.float32)
    sum_u, sum_v = lax.fori_loop(0, LEVELS, momentum, (zero, zero))
    mean_u = sum_u * (1.0 / LEVELS)
    mean_v = sum_v * (1.0 / LEVELS)
    for side, tile in ((0, 1), (1, 0)):
        cut = slice(tile * LANES, (tile + 1) * LANES)
        mean_send[side, 0:32, :] = mean_u[:, cut]
        mean_send[side, 32:64, :] = mean_v[:, cut]
    mean_copies = [
        send(mean_send.at[0], mean_got.at[0], 1, 0),
        send(mean_send.at[1], mean_got.at[1], -1, 0),
    ]
    launch(mean_copies)

    def tracer(k, carry):
        level = k.astype(jnp.float32)
        faces = [level < limit for limit in open_depth]
        t, near_t = near_field(2, t_ref, k)
        u, near_u = near_field(0, u_ref, k)
        v, near_v = near_field(1, v_ref, k)
        spread = laplace(faces, t, near_t)
        east = jnp.where(faces[0], (u + near_u[0]) * 0.5, 0.0)
        west = jnp.where(faces[1], (near_u[1] + u) * 0.5, 0.0)
        north = jnp.where(faces[2], (v + near_v[2]) * 0.5, 0.0)
        south = jnp.where(faces[3], (near_v[3] + v) * 0.5, 0.0)
        transport = (east * (t + near_t[0]) - west * (near_t[1] + t)) + (
            north * (t + near_t[2]) - south * (near_t[3] + t)
        )
        result = t + TIME_STEP * (DIFFUSIVITY * spread - 0.5 * transport)
        rows = pl.ds(pl.multiple_of(k * ROWS, ROWS), ROWS)
        t_out[rows, :] = jnp.where(level < depth, result, 0.0)
        return carry

    lax.fori_loop(0, LEVELS, tracer, 0)

    for copy in mean_copies:
        copy.wait_recv()
    west_mean, east_mean = mean_got.at[0], mean_got.at[1]
    wide_u = jnp.concatenate([west_mean[0:32, :], mean_u, east_mean[0:32, :]], axis=1)
    wide_v = jnp.concatenate([west_mean[32:64, :], mean_v, east_mean[32:64, :]], axis=1)
    wide_eta = jnp.concatenate([west_tile[32:64, :], elevation, east_tile[32:64, :]], axis=1)
    wide_row = lax.broadcasted_iota(jnp.int32, (ROWS, WIDE), 0)
    north_v = jnp.where(wide_row == ROWS - 1, 0.0, pltpu.roll(wide_v, ROWS - 1, 0))
    south_v = jnp.where(wide_row == 0, 0.0, pltpu.roll(wide_v, 1, 0))
    across = pltpu.roll(wide_u, WIDE - 1, 1) - pltpu.roll(wide_u, 1, 1)
    source = jnp.where(
        depth_wide > 0.5, wide_eta - 0.5 * (across + (north_v - south_v)), 0.0
    )
    ends = jnp.where(
        lax.broadcasted_iota(jnp.int32, (16, WIDE), 0) == 0, wide_v[0:1, :], wide_v[31:32, :]
    )
    by_class = exact_select(jnp.concatenate([source, ends], axis=0), choice[...])
    for c in range(4):
        cut = slice(LANES * c, LANES * (c + 1))
        source_send[32 * c : 32 * c + 32, :] = by_class[0:32, cut]
        source_send[128 + c : 129 + c, :] = by_class[32:33, cut]
        source_send[132 + c : 133 + c, :] = by_class[33:34, cut]
    source_copies = [
        send(source_send, source_got.at[i], 0, move) for i, move in enumerate(LAT_MOVES)
    ]
    launch(source_copies)

    for copy in depth_copies:
        copy.wait_recv()

    def slot_of(lat_move):
        return LAT_MOVES.index(-lat_move)

    for move in range(-2, 3):
        for c in range(4):
            rows = pl.ds(ORIGIN[0] + 32 * move, 32)
            if move == 0:
                deep[c, rows, :] = deep_send[32 * c : 32 * c + 32, :]
            else:
                deep[c, rows, :] = (
                    deep_got[slot_of(move), 32 * c : 32 * c + 32, :] * inside(move)
                )

    def finish_weights(g, rows):
        we = [grid_we[g][c, rows, :] for c in range(CLASSES[g])]
        ww = west_of(we, STEP[g])
        grid_ww[g][rows, :] = ww[0]
        before = pl.ds(rows.start - 1, 8)
        for c in range(CLASSES[g]):
            near = (we[c] + ww[c]) + (grid_wn[g][c, rows, :] + grid_wn[g][c, before, :])
            grid_dg[g][c, rows, :] = MASS[g] + near
            grid_iv[g][c, rows, :] = 1.0 / (MASS[g] + 2.0 * near)

    def fine_weights(at):
        rows, after = pl.ds(at, 8), pl.ds(at + 1, 8)
        columns = [deep[c, rows, :] * (1.0 / LEVELS) for c in range(4)]
        for c, near in enumerate(east_of(columns, 1)):
            grid_we[0][c, rows, :] = jnp.minimum(columns[c], near)
            north = deep[c, after, :] * (1.0 / LEVELS)
            grid_wn[0][c, rows, :] = jnp.minimum(columns[c], north)

    def whole(g):
        return ORIGIN[g] - (64 >> g), ORIGIN[g] + ((96 >> g) + 7) // 8 * 8

    def pair_lanes(values):
        even = (lax.broadcasted_iota(jnp.int32, values.shape, 1) & 1) == 0
        return even, pltpu.roll(values, LANES - 1, 1), pltpu.roll(values, 1, 1)

    def finer_rows(g, at):
        return 2 * (at - ORIGIN[g]) + ORIGIN[g - 1]

    each_chunk(*whole(0), fine_weights)
    each_chunk(*whole(0), lambda at: finish_weights(0, pl.ds(at, 8)))
    for g in (1, 2, 3):

        def coarse_weights(at, g=g):
            rows = pl.ds(at, 8)
            above = finer_rows(g, at)
            even_rows, odd_rows = pl.ds(above, 8, stride=2), pl.ds(above + 1, 8, stride=2)
            finer_we, finer_wn = grid_we[g - 1], grid_wn[g - 1]
            if g < 3:
                for c in range(CLASSES[g]):
                    grid_we[g][c, rows, :] = (
                        finer_we[2 * c + 1, even_rows, :] + finer_we[2 * c + 1, odd_rows, :]
                    )
                    grid_wn[g][c, rows, :] = (
                        finer_wn[2 * c, odd_rows, :] + finer_wn[2 * c + 1, odd_rows, :]
                    )
            else:
                we = finer_we[0, even_rows, :] + finer_we[0, odd_rows, :]
                even, east, west = pair_lanes(we)
                grid_we[g][0, rows, :] = jnp.where(even, east, we)
                wn = finer_wn[0, odd_rows, :]
                even, east, west = pair_lanes(wn)
                grid_wn[g][0, rows, :] = wn + jnp.where(even, east, west)

        each_chunk(*whole(g), coarse_weights)
        each_chunk(*whole(g), lambda at, g=g: finish_weights(g, pl.ds(at, 8)))

    for copy in source_copies:
        copy.wait_recv()

    def arrived(move):
        return source_send if move == 0 else source_got.at[slot_of(move)]

    rows32 = lax.broadcasted_iota(jnp.int32, (ROWS, LANES), 0)
    for move in range(-2, 3):
        block = arrived(move)
        for c in range(4):
            rows = pl.ds(ORIGIN[0] + 32 * move, 32)
            values = block[32 * c : 32 * c + 32, :]
            if move < 2:
                edge = arrived(move + 1)[128 + c : 129 + c, :] * (0.5 * inside(move + 1))
                values = values - jnp.where(rows32 == ROWS - 1, edge, 0.0)
            if move > -2:
                edge = arrived(move - 1)[132 + c : 133 + c, :] * (0.5 * inside(move - 1))
                values = values + jnp.where(rows32 == 0, edge, 0.0)
            grid_b[0][c, rows, :] = jnp.where(deep[c, rows, :] > 0.5, values, 0.0)

    def operator(g, held, at):
        rows, after, before = pl.ds(at, 8), pl.ds(at + 1, 8), pl.ds(at - 1, 8)
        count = CLASSES[g]
        p = [held[c, rows, :] for c in range(count)]
        we = [grid_we[g][c, rows, :] for c in range(count)]
        ww = [grid_ww[g][rows, :]] + we[:-1]
        pe, pw = east_of(p, STEP[g]), west_of(p, STEP[g])
        residual = []
        for c in range(count):
            pull = (we[c] * pe[c] + ww[c] * pw[c]) + (
                grid_wn[g][c, rows, :] * held[c, after, :]
                + grid_wn[g][c, before, :] * held[c, before, :]
            )
            image = grid_dg[g][c, rows, :] * p[c] - pull
            residual.append(grid_b[g][c, rows, :] - image)
        return p, residual

    def span(g, low, high):
        return ORIGIN[g] + low, ORIGIN[g] + high

    def from_zero(g, low, high, held):
        def body(at):
            rows = pl.ds(at, 8)
            for c in range(CLASSES[g]):
                held[c, rows, :] = grid_b[g][c, rows, :] * grid_iv[g][c, rows, :]

        each_chunk(*span(g, low, high), body)

    def sweep(g, low, high, held, result):
        def body(at):
            rows = pl.ds(at, 8)
            p, residual = operator(g, held, at)
            for c in range(CLASSES[g]):
                result[c, rows, :] = p[c] + residual[c] * grid_iv[g][c, rows, :]

        each_chunk(*span(g, low, high), body)

    def restricted(g, low, high, held):
        def residual_rows(at):
            rows = pl.ds(at, 8)
            _, residual = operator(g, held, at)
            if g < 2:
                for c in range(CLASSES[g] // 2):
                    grid_r[g][c, rows, :] = residual[2 * c] + residual[2 * c + 1]
            else:
                even, east, west = pair_lanes(residual[0])
                grid_r[g][0, rows, :] = residual[0] + jnp.where(even, east, west)

        each_chunk(*span(g, low, high), residual_rows)

        def pair_rows(at):
            above = finer_rows(g + 1, at)
            for c in range(CLASSES[g + 1]):
                grid_b[g + 1][c, pl.ds(at, 8), :] = (
                    grid_r[g][c, pl.ds(above, 8, stride=2), :]
                    + grid_r[g][c, pl.ds(above + 1, 8, stride=2), :]
                )

        top = (high // 2 + 7) // 8 * 8
        each_chunk(*span(g + 1, low // 2 // 8 * 8, top), pair_rows)

    def corrected(g, low, high, held, correction):
        first, last = low // 2 // 8 * 8, (high // 2 + 7) // 8 * 8

        def body(at):
            above = finer_rows(g + 1, at)
            for c in range(CLASSES[g]):
                change = correction[c // 2, pl.ds(at, 8), :]
                for odd in (0, 1):
                    rows = pl.ds(above + odd, 8, stride=2)
                    held[c, rows, :] = held[c, rows, :] + change

        each_chunk(*span(g + 1, first, last), body)

    def coarse_source(reach):
        coarse_send[reach - 1] = grid_b[3][0, pl.ds(ORIGIN[3], 8), :]
        moves = LAT_MOVES[: 2 * reach]
        base = 0 if reach == 2 else 4
        copies = [
            send(coarse_send.at[reach - 1], coarse_got.at[base + i], 0, move)
            for i, move in enumerate(moves)
        ]
        launch(copies)
        for copy in copies:
            copy.wait_recv()
        upper = lax.broadcasted_iota(jnp.int32, (8, LANES), 0) >= 4

        def block(move):
            return coarse_got[base + moves.index(-move)] * inside(move)

        own = coarse_send[reach - 1]
        grid_b[3][0, pl.ds(ORIGIN[3], 8), :] = jnp.where(upper, pltpu.roll(block(1), 4, 0), own)
        lower = pltpu.roll(block(-1), 4, 0)
        if reach == 2:
            lower = jnp.where(upper, lower, block(-2))
            grid_b[3][0, pl.ds(ORIGIN[3] + 8, 8), :] = block(2)
        grid_b[3][0, pl.ds(ORIGIN[3] - 8, 8), :] = lower

    plans = (
        ((-64, 96), (-32, 48), (-16, 24), (-16, 24), (-16, 32), (-24, 56)),
        ((-24, 56), (-16, 32), (-8, 16), (-8, 16), (-8, 24), (-16, 48)),
        ((-16, 48), (-8, 24), (-8, 16), (-8, 16), (-8, 24), (-8, 40)),
    )
    for cycle in range(CYCLES):
        before0, down1, down2, up2, up1, after0 = plans[cycle]
        if cycle == 0:
            from_zero(0, *before0, grid_q[0])
        else:
            sweep(0, *before0, grid_p[0], grid_q[0])
        restricted(0, *before0, grid_q[0])
        from_zero(1, *down1, grid_q[1])
        restricted(1, *down1, grid_q[1])
        from_zero(2, *down2, grid_q[2])
        restricted(2, *down2, grid_q[2])
        if cycle > 0:
            coarse_source(3 - cycle)
        from_zero(3, -8, 16, grid_q[3])
        here, there_ = grid_q[3], grid_p[3]
        for _ in range(SWEEPS - 1):
            sweep(3, -8, 16, here, there_)
            here, there_ = there_, here
        corrected(2, *up2, grid_q[2], here)
        sweep(2, *up2, grid_q[2], grid_p[2])
        corrected(1, *up1, grid_q[1], grid_p[2])
        sweep(1, *up1, grid_q[1], grid_p[1])
        corrected(0, *after0, grid_q[0], grid_p[1])
        sweep(0, *after0, grid_q[0], grid_p[0])

    pressure = grid_p[0]
    own = pl.ds(ORIGIN[0], ROWS)
    p = [pressure[c, own, :] for c in range(4)]
    slope_east = [0.5 * (e - w) for e, w in zip(east_of(p, 1), west_of(p, 1))]
    slope_north = [
        0.5 * (pressure[c, pl.ds(ORIGIN[0] + 1, ROWS), :] - pressure[c, pl.ds(ORIGIN[0] - 1, ROWS), :])
        for c in range(4)
    ]
    stacked = jnp.concatenate(
        [jnp.concatenate(parts, axis=1) for parts in (p, slope_east, slope_north)], axis=0
    )
    ordered = exact_select(stacked, unchoice[...])
    p_out[...] = ordered[0:32]
    push_u = GRAVITY_STEP * ordered[32:64]
    push_v = GRAVITY_STEP * ordered[64:96]

    def finish(k, carry):
        rows = pl.ds(pl.multiple_of(k * ROWS, ROWS), ROWS)
        wet = k.astype(jnp.float32) < depth
        u_out[rows, :] = jnp.where(wet, u_star[rows, :] - push_u, 0.0)
        v_out[rows, :] = jnp.where(wet, v_star[rows, :] - push_v, 0.0)
        return carry

    lax.fori_loop(0, LEVELS, finish, 0)
    for copy in started:
        copy.wait_send()


def shards(lon_count, lat_count, u, v, t, depth, elevation):
    f32 = jnp.float32
    flat = (LEVELS * ROWS, COLS)
    block = pl.BlockSpec(memory_space=pltpu.VMEM)

    def grids(classes=CLASSES):
        return [pltpu.VMEM((c, h, LANES), f32) for c, h in zip(classes, HEIGHT)]

    outs = pl.pallas_call(
        functools.partial(kernel, lon_count, lat_count),
        out_shape=[jax.ShapeDtypeStruct(flat, f32)] * 3
        + [jax.ShapeDtypeStruct((ROWS, COLS), f32)],
        in_specs=[block] * 5,
        out_specs=[block] * 4,
        scratch_shapes=[
            pltpu.VMEM(flat, f32),
            pltpu.VMEM(flat, f32),
            pltpu.VMEM((2, 32, COLS), f32),
            pltpu.VMEM((2, 32, COLS), f32),
            pltpu.VMEM((2, 72, LANES), f32),
            pltpu.VMEM((2, 72, LANES), f32),
            pltpu.VMEM((2, 64, LANES), f32),
            pltpu.VMEM((2, 64, LANES), f32),
            pltpu.VMEM((128, LANES), f32),
            pltpu.VMEM((4, 128, LANES), f32),
            pltpu.VMEM((136, LANES), f32),
            pltpu.VMEM((4, 136, LANES), f32),
            pltpu.VMEM((2, 8, LANES), f32),
            pltpu.VMEM((6, 8, LANES), f32),
            pltpu.VMEM((WIDE, WIDE), jnp.bfloat16),
            pltpu.VMEM((WIDE, COLS), jnp.bfloat16),
            pltpu.VMEM((4, HEIGHT[0], LANES), f32),
            grids(),
            grids(),
            grids(),
            grids(),
            [pltpu.VMEM((h, LANES), f32) for h in HEIGHT],
            grids(),
            grids(),
            grids(),
            grids(),
            pltpu.SemaphoreType.DMA((24,)),
            pltpu.SemaphoreType.DMA((24,)),
        ],
        compiler_params=pltpu.CompilerParams(
            collective_id=0, has_side_effects=True, vmem_limit_bytes=32 << 20
        ),
    )(u.reshape(flat), v.reshape(flat), t.reshape(flat), depth, elevation)
    shape = (LEVELS, ROWS, COLS)
    return outs[0].reshape(shape), outs[1].reshape(shape), outs[2].reshape(shape), outs[3]


def solution(mesh):
    spec3, spec2 = P(None, "lat", "lon"), P("lat", "lon")
    return jax.shard_map(
        functools.partial(shards, mesh.shape["lon"], mesh.shape["lat"]),
        mesh=mesh,
        in_specs=(spec3, spec3, spec3, spec2, spec2),
        out_specs=(spec3, spec3, spec3, spec2),
        check_vma=False,
    )
```

```python
import functools

import jax
import jax.numpy as jnp
from jax import lax
from jax.experimental import pallas as pl
from jax.experimental.pallas import tpu as pltpu
from jax.sharding import PartitionSpec as P

LEVELS = 8
CYCLES = 3
SWEEPS = 4
TIME_STEP = 0.2
VISCOSITY = 1.0
DIFFUSIVITY = 1.0
CORIOLIS = 1.0
MASS_TERM = 0.05
GRAVITY_STEP = 0.5

ROWS = 32
COLS = 256
LANES = 128
WIDE = 512
MESH_IDS = pl.DeviceIdType.MESH

CLASSES = (4, 2, 1, 1)
STEP = (1, 1, 1, 2)
ORIGIN = (48, 32, 24, 16)
HEIGHT = (128, 80, 56, 40)
MASS = tuple(MASS_TERM * 4.0**g for g in range(4))

LAT_MOVES = (1, -1, 2, -2)


def east_of(parts, step):
    turned = pltpu.roll(parts[0], LANES - step, 1)
    return list(parts[1:]) + [turned]


def west_of(parts, step):
    turned = pltpu.roll(parts[-1], step, 1)
    return [turned] + list(parts[:-1])


def each_chunk(first, last, body, unroll=5):
    count = (last - first) // 8
    if count <= unroll:
        for i in range(count):
            body(first + 8 * i)
        return
    while count % unroll:
        unroll -= 1

    def step(i, carry):
        for j in range(unroll):
            body(pl.multiple_of(first + (i * unroll + j) * 8, 8))
        return carry

    lax.fori_loop(0, count // unroll, step, 0)


def split_three(values):
    high = values.astype(jnp.bfloat16)
    rest = values - high.astype(jnp.float32)
    middle = rest.astype(jnp.bfloat16)
    low = (rest - middle.astype(jnp.float32)).astype(jnp.bfloat16)
    return jnp.concatenate([high, middle, low], axis=0)


def exact_select(values, choice):
    count = values.shape[0]
    product = jnp.dot(split_three(values), choice, preferred_element_type=jnp.float32)
    return (product[:count] + product[count : 2 * count]) + product[2 * count :]


def kernel(
    lon_count,
    lat_count,
    u_far,
    v_far,
    t_far,
    depth_far,
    elevation_far,
    u_home,
    v_home,
    t_home,
    p_out,
    push_u_out,
    push_v_out,
    u_ref,
    v_ref,
    t_ref,
    depth_ref,
    elevation_ref,
    u_star,
    v_star,
    t_out,
    rows_send,
    rows_got,
    cols_send,
    cols_got,
    mean_send,
    mean_got,
    deep_send,
    deep_got,
    deep_got_far,
    source_send,
    source_got,
    source_got_far,
    ends_send,
    ends_got,
    weight_send,
    weight_got,
    coarse_send,
    coarse_got,
    choice,
    unchoice,
    deep,
    grid_b,
    grid_p,
    grid_q,
    grid_we,
    grid_ww,
    grid_wn,
    grid_dg,
    grid_iv,
    grid_r,
    load_sem,
    send_sem,
    recv_sem,
):
    lon = lax.axis_index("lon")
    lat = lax.axis_index("lat")
    sems = iter(range(64))

    def there(lon_move, lat_move):
        return {
            "lon": lax.rem(lon + lon_move + lon_count, lon_count),
            "lat": lax.rem(lat + lat_move + lat_count, lat_count),
        }

    def send(source, target, lon_move, lat_move):
        at = next(sems)
        return pltpu.make_async_remote_copy(
            src_ref=source,
            dst_ref=target,
            send_sem=send_sem.at[at],
            recv_sem=recv_sem.at[at],
            device_id=there(lon_move, lat_move),
            device_id_type=MESH_IDS,
        )

    def inside(lat_move):
        spot = lat + lat_move
        return jnp.where((spot >= 0) & (spot < lat_count), 1.0, 0.0).astype(jnp.float32)

    started = []

    def launch(copies):
        for copy in copies:
            copy.start()
        started.extend(copies)

    barrier = pltpu.get_barrier_semaphore()
    for lon_move, lat_move in [(1, 0), (-1, 0)] + [(0, m) for m in LAT_MOVES]:
        pl.semaphore_signal(
            barrier, inc=1, device_id=there(lon_move, lat_move), device_id_type=MESH_IDS
        )

    loads = [
        pltpu.make_async_copy(far, near, load_sem.at[i])
        for i, (far, near) in enumerate(
            (
                (depth_far, depth_ref),
                (elevation_far, elevation_ref),
                (u_far, u_ref),
                (v_far, v_ref),
                (t_far, t_ref),
            )
        )
    ]
    for load in loads:
        load.start()
    for load in loads:
        load.wait()

    depth = depth_ref[...].astype(jnp.float32)
    lane8 = lax.broadcasted_iota(jnp.int32, (8, LANES), 1)
    fields = (u_ref, v_ref, t_ref)
    for side, row in ((0, ROWS - 1), (1, 0)):
        for f, field in enumerate(fields):
            for k in range(LEVELS):
                rows_send[side, 8 * f + k : 8 * f + k + 1, :] = field[
                    k * ROWS + row : k * ROWS + row + 1, :
                ]
        rows_send[side, pl.ds(24, 8), :] = jnp.broadcast_to(depth[row : row + 1, :], (8, COLS))

    def pack(i, carry):
        at_last, at_first = carry
        rows = pl.ds(pl.multiple_of(8 * i, 8), 8)
        for f, field in enumerate(fields):
            here = lane8 == i + 32 * f
            at_last = jnp.where(here, field[rows, COLS - 1 : COLS], at_last)
            at_first = jnp.where(here, field[rows, 0:1], at_first)
        return at_last, at_first

    zero8 = jnp.zeros((8, LANES), jnp.float32)
    at_last, at_first = lax.fori_loop(0, 32, pack, (zero8, zero8), unroll=4)
    elevation = elevation_ref[...]
    deep_send[0] = depth
    for side, edge, tile in ((0, at_last, 1), (1, at_first, 0)):
        cut = slice(tile * LANES, (tile + 1) * LANES)
        cols_send[side, 0:32, :] = depth[:, cut]
        cols_send[side, 32:64, :] = elevation[:, cut]
        cols_send[side, 64:72, :] = edge

    pl.semaphore_wait(barrier, 2 + len(LAT_MOVES))
    first = [
        send(cols_send.at[0], cols_got.at[0], 1, 0),
        send(cols_send.at[1], cols_got.at[1], -1, 0),
        send(rows_send.at[0], rows_got.at[0], 0, 1),
        send(rows_send.at[1], rows_got.at[1], 0, -1),
    ]
    launch(first)

    def depth_sends(part):
        source = deep_send.at[part]
        return [
            send(source, deep_got.at[part, 0], 0, 1),
            send(source, deep_got.at[part, 1], 0, -1),
            send(source.at[pl.ds(ROWS - 8, 8)], deep_got_far.at[part, 0], 0, 2),
            send(source.at[pl.ds(0, 8)], deep_got_far.at[part, 1], 0, -2),
        ]

    depth_copies = depth_sends(0)
    launch(depth_copies)

    def order(n):
        return ((((n & 127) + 32) & 127) << 2) + (n >> 7)

    wanted = order(lax.broadcasted_iota(jnp.int32, (1, WIDE), 1))

    def fill(i, carry):
        rows = pl.ds(pl.multiple_of(32 * i, 32), 32)
        k = lax.broadcasted_iota(jnp.int32, (32, WIDE), 0) + 32 * i
        choice[rows, :] = jnp.where(k == wanted, 1.0, 0.0).astype(jnp.bfloat16)
        n = lax.broadcasted_iota(jnp.int32, (32, COLS), 0) + 32 * i
        column = lax.broadcasted_iota(jnp.int32, (32, COLS), 1) + LANES
        unchoice[rows, :] = jnp.where(order(n) == column, 1.0, 0.0).astype(jnp.bfloat16)
        return carry

    lax.fori_loop(0, WIDE // 32, fill, 0)
    for ref in list(grid_p) + list(grid_q) + list(grid_b) + list(grid_wn) + [deep]:
        ref[...] = jnp.zeros_like(ref)
    row_number = lax.broadcasted_iota(jnp.int32, (ROWS, LANES), 0)
    place = (lat * ROWS + row_number).astype(jnp.float32)
    angle = jnp.pi * ((place + 0.5) / (ROWS * lat_count) - 0.5)
    turning = CORIOLIS * jnp.sin(angle)
    rotation = jnp.concatenate([turning, turning], axis=1)

    for copy in first:
        copy.wait_recv()

    west_tile, east_tile = cols_got.at[0], cols_got.at[1]
    deep_send[1, :, 0:LANES] = west_tile[0:32, :]
    deep_send[1, :, LANES:COLS] = east_tile[0:32, :]
    more_depth = depth_sends(1)
    launch(more_depth)
    depth_copies = depth_copies + more_depth

    row = lax.broadcasted_iota(jnp.int32, (ROWS, COLS), 0)
    column = lax.broadcasted_iota(jnp.int32, (ROWS, COLS), 1)
    on_east, on_west = column == COLS - 1, column == 0
    on_north, on_south = row == ROWS - 1, row == 0

    def beside(values, east_edge, west_edge, north_edge, south_edge):
        return (
            jnp.where(on_east, east_edge, pltpu.roll(values, COLS - 1, 1)),
            jnp.where(on_west, west_edge, pltpu.roll(values, 1, 1)),
            jnp.where(on_north, north_edge, pltpu.roll(values, ROWS - 1, 0)),
            jnp.where(on_south, south_edge, pltpu.roll(values, 1, 0)),
        )

    depth_near = beside(
        depth,
        east_tile[0:32, 0:1],
        west_tile[0:32, LANES - 1 : LANES],
        rows_got[1, 24:25, :] * inside(1),
        rows_got[0, 24:25, :] * inside(-1),
    )
    open_depth = [jnp.minimum(depth, near) for near in depth_near]
    east_edges = east_tile[64:72, :]
    west_edges = west_tile[64:72, :]

    def near_field(f, field, k):
        values = field[pl.ds(pl.multiple_of(k * ROWS, ROWS), ROWS), :]
        turn = lax.rem(2 * LANES - 32 * f - 4 * k, LANES)
        east_lanes = pltpu.roll(east_edges, turn, 1)
        west_lanes = pltpu.roll(west_edges, turn, 1)
        east_edge = jnp.concatenate([east_lanes[:, g : g + 1] for g in range(4)], axis=0)
        west_edge = jnp.concatenate([west_lanes[:, g : g + 1] for g in range(4)], axis=0)
        north_edge = rows_got[1, pl.ds(8 * f + k, 1), :]
        south_edge = rows_got[0, pl.ds(8 * f + k, 1), :]
        return values, beside(values, east_edge, west_edge, north_edge, south_edge)

    def laplace(faces, values, nearby):
        terms = [jnp.where(face, near - values, 0.0) for face, near in zip(faces, nearby)]
        return (terms[0] + terms[1]) + (terms[2] + terms[3])

    def momentum(k, carry):
        sum_u, sum_v = carry
        level = k.astype(jnp.float32)
        faces = [level < limit for limit in open_depth]
        wet = level < depth
        u, near_u = near_field(0, u_ref, k)
        v, near_v = near_field(1, v_ref, k)
        guess_u = u + TIME_STEP * (VISCOSITY * laplace(faces, u, near_u) + rotation * v)
        guess_v = v + TIME_STEP * (VISCOSITY * laplace(faces, v, near_v) - rotation * u)
        guess_u = jnp.where(wet, guess_u, 0.0)
        guess_v = jnp.where(wet, guess_v, 0.0)
        rows = pl.ds(pl.multiple_of(k * ROWS, ROWS), ROWS)
        u_star[rows, :] = guess_u
        v_star[rows, :] = guess_v
        return sum_u + guess_u, sum_v + guess_v

    zero = jnp.zeros((ROWS, COLS), jnp.float32)
    sum_u, sum_v = lax.fori_loop(0, LEVELS, momentum, (zero, zero))
    mean_u = sum_u * (1.0 / LEVELS)
    mean_v = sum_v * (1.0 / LEVELS)
    for side, tile in ((0, 1), (1, 0)):
        cut = slice(tile * LANES, (tile + 1) * LANES)
        mean_send[side, 0:32, :] = mean_u[:, cut]
        mean_send[side, 32:64, :] = mean_v[:, cut]
    mean_copies = [
        send(mean_send.at[0], mean_got.at[0], 1, 0),
        send(mean_send.at[1], mean_got.at[1], -1, 0),
    ]
    launch(mean_copies)

    def tracer(k, carry):
        level = k.astype(jnp.float32)
        faces = [level < limit for limit in open_depth]
        t, near_t = near_field(2, t_ref, k)
        u, near_u = near_field(0, u_ref, k)
        v, near_v = near_field(1, v_ref, k)
        spread = laplace(faces, t, near_t)
        east = jnp.where(faces[0], (u + near_u[0]) * 0.5, 0.0)
        west = jnp.where(faces[1], (near_u[1] + u) * 0.5, 0.0)
        north = jnp.where(faces[2], (v + near_v[2]) * 0.5, 0.0)
        south = jnp.where(faces[3], (near_v[3] + v) * 0.5, 0.0)
        transport = (east * (t + near_t[0]) - west * (near_t[1] + t)) + (
            north * (t + near_t[2]) - south * (near_t[3] + t)
        )
        result = t + TIME_STEP * (DIFFUSIVITY * spread - 0.5 * transport)
        rows = pl.ds(pl.multiple_of(k * ROWS, ROWS), ROWS)
        t_out[rows, :] = jnp.where(level < depth, result, 0.0)
        return carry

    lax.fori_loop(0, LEVELS, tracer, 0)
    stores = [
        pltpu.make_async_copy(near, far, load_sem.at[i])
        for i, (near, far) in enumerate(
            ((u_star, u_home), (v_star, v_home), (t_out, t_home))
        )
    ]
    for store in stores:
        store.start()

    for copy in mean_copies:
        copy.wait_recv()
    west_mean, east_mean = mean_got.at[0], mean_got.at[1]
    wide_u = jnp.concatenate([west_mean[0:32, :], mean_u, east_mean[0:32, :]], axis=1)
    wide_v = jnp.concatenate([west_mean[32:64, :], mean_v, east_mean[32:64, :]], axis=1)
    wide_eta = jnp.concatenate([west_tile[32:64, :], elevation, east_tile[32:64, :]], axis=1)
    wide_row = lax.broadcasted_iota(jnp.int32, (ROWS, WIDE), 0)
    north_v = jnp.where(wide_row == ROWS - 1, 0.0, pltpu.roll(wide_v, ROWS - 1, 0))
    south_v = jnp.where(wide_row == 0, 0.0, pltpu.roll(wide_v, 1, 0))
    across = pltpu.roll(wide_u, WIDE - 1, 1) - pltpu.roll(wide_u, 1, 1)
    depth_wide = jnp.concatenate([west_tile[0:32, :], depth, east_tile[0:32, :]], axis=1)
    source = jnp.where(
        depth_wide > 0.5, wide_eta - 0.5 * (across + (north_v - south_v)), 0.0
    )
    ends = jnp.where(
        lax.broadcasted_iota(jnp.int32, (16, WIDE), 0) == 0, wide_v[0:1, :], wide_v[31:32, :]
    )
    by_class = exact_select(jnp.concatenate([source, ends], axis=0), choice[...])
    for c in range(4):
        cut = slice(LANES * c, LANES * (c + 1))
        source_send[c] = by_class[0:32, cut]
        ends_send[c : c + 1, :] = by_class[32:33, cut]
        ends_send[4 + c : 5 + c, :] = by_class[33:34, cut]
    source_copies = [
        send(ends_send, ends_got.at[i], 0, move) for i, move in enumerate(LAT_MOVES)
    ] + [
        send(source_send, source_got.at[0], 0, 1),
        send(source_send, source_got.at[1], 0, -1),
        send(source_send.at[:, pl.ds(ROWS - 8, 8)], source_got_far.at[0], 0, 2),
        send(source_send.at[:, pl.ds(0, 8)], source_got_far.at[1], 0, -2),
    ]
    launch(source_copies)

    for copy in depth_copies:
        copy.wait_recv()

    def slot_of(lat_move):
        return LAT_MOVES.index(-lat_move)

    def wide_depth(own, halo, mask):
        return mask * jnp.concatenate([halo[:, 0:LANES], own, halo[:, LANES:COLS]], axis=1)

    blocks = [
        wide_depth(deep_got_far[0, 0], deep_got_far[1, 0], inside(-2)),
        wide_depth(deep_got[0, 0], deep_got[1, 0], inside(-1)),
        wide_depth(deep_send[0], deep_send[1], 1.0),
        wide_depth(deep_got[0, 1], deep_got[1, 1], inside(1)),
        wide_depth(deep_got_far[0, 1], deep_got_far[1, 1], inside(2)),
    ]
    by_class = jnp.dot(
        jnp.concatenate(blocks, axis=0).astype(jnp.bfloat16),
        choice[...],
        preferred_element_type=jnp.float32,
    )
    for c in range(4):
        deep[c, pl.ds(ORIGIN[0] - 40, 112), :] = by_class[:, LANES * c : LANES * (c + 1)]

    def finish_weights(g, rows):
        we = [grid_we[g][c, rows, :] for c in range(CLASSES[g])]
        ww = west_of(we, STEP[g])
        grid_ww[g][rows, :] = ww[0]
        before = pl.ds(rows.start - 1, 8)
        for c in range(CLASSES[g]):
            near = (we[c] + ww[c]) + (grid_wn[g][c, rows, :] + grid_wn[g][c, before, :])
            grid_dg[g][c, rows, :] = MASS[g] + near
            grid_iv[g][c, rows, :] = 1.0 / (MASS[g] + 2.0 * near)

    def fine_weights(at):
        rows, after = pl.ds(at, 8), pl.ds(at + 1, 8)
        columns = [deep[c, rows, :] * (1.0 / LEVELS) for c in range(4)]
        for c, near in enumerate(east_of(columns, 1)):
            grid_we[0][c, rows, :] = jnp.minimum(columns[c], near)
            north = deep[c, after, :] * (1.0 / LEVELS)
            grid_wn[0][c, rows, :] = jnp.minimum(columns[c], north)

    def whole(g):
        return tuple(ORIGIN[g] + end for end in ((-40, 72), (-24, 40), (-16, 24), (0, 8))[g])

    def pair_lanes(values):
        even = (lax.broadcasted_iota(jnp.int32, values.shape, 1) & 1) == 0
        return even, pltpu.roll(values, LANES - 1, 1), pltpu.roll(values, 1, 1)

    def finer_rows(g, at):
        return 2 * (at - ORIGIN[g]) + ORIGIN[g - 1]

    each_chunk(*whole(0), fine_weights)
    each_chunk(*whole(0), lambda at: finish_weights(0, pl.ds(at, 8)))
    for g in (1, 2, 3):

        def coarse_weights(at, g=g):
            rows = pl.ds(at, 8)
            above = finer_rows(g, at)
            even_rows, odd_rows = pl.ds(above, 8, stride=2), pl.ds(above + 1, 8, stride=2)
            finer_we, finer_wn = grid_we[g - 1], grid_wn[g - 1]
            if g < 3:
                for c in range(CLASSES[g]):
                    grid_we[g][c, rows, :] = (
                        finer_we[2 * c + 1, even_rows, :] + finer_we[2 * c + 1, odd_rows, :]
                    )
                    grid_wn[g][c, rows, :] = (
                        finer_wn[2 * c, odd_rows, :] + finer_wn[2 * c + 1, odd_rows, :]
                    )
            else:
                we = finer_we[0, even_rows, :] + finer_we[0, odd_rows, :]
                even, east, west = pair_lanes(we)
                grid_we[g][0, rows, :] = jnp.where(even, east, we)
                wn = finer_wn[0, odd_rows, :]
                even, east, west = pair_lanes(wn)
                grid_wn[g][0, rows, :] = wn + jnp.where(even, east, west)

        each_chunk(*whole(g), coarse_weights)
        if g < 3:
            each_chunk(*whole(g), lambda at, g=g: finish_weights(g, pl.ds(at, 8)))

    upper = lax.broadcasted_iota(jnp.int32, (8, LANES), 0) >= 4

    def around(held, own, got, moves):
        def block(move):
            return got[moves.index(-move)][...] * inside(move)

        held[0, pl.ds(ORIGIN[3], 8), :] = jnp.where(upper, pltpu.roll(block(1), 4, 0), own)
        lower = pltpu.roll(block(-1), 4, 0)
        if len(moves) == 4:
            lower = jnp.where(upper, lower, block(-2))
            held[0, pl.ds(ORIGIN[3] + 8, 8), :] = block(2)
        held[0, pl.ds(ORIGIN[3] - 8, 8), :] = lower

    weight_send[0:8, :] = grid_we[3][0, pl.ds(ORIGIN[3], 8), :]
    weight_send[8:16, :] = grid_wn[3][0, pl.ds(ORIGIN[3], 8), :]
    weight_copies = [
        send(weight_send, weight_got.at[i], 0, move) for i, move in enumerate(LAT_MOVES)
    ]
    launch(weight_copies)

    for copy in source_copies:
        copy.wait_recv()

    rows32 = lax.broadcasted_iota(jnp.int32, (ROWS, LANES), 0)

    def ends(move, spot):
        held = ends_send if move == 0 else ends_got.at[slot_of(move)]
        return held[spot : spot + 1, :] * (0.5 * inside(move))

    def place_source(c, move, first, values):
        rows = pl.ds(ORIGIN[0] + first, values.shape[0])
        at = rows32[: values.shape[0]] + (first - 32 * move)
        if move < 2:
            values = values - jnp.where(at == ROWS - 1, ends(move + 1, c), 0.0)
        if move > -2:
            values = values + jnp.where(at == 0, ends(move - 1, 4 + c), 0.0)
        grid_b[0][c, rows, :] = jnp.where(deep[c, rows, :] > 0.5, values, 0.0)

    for c in range(4):
        place_source(c, -2, -40, source_got_far[0, c])
        place_source(c, -1, -32, source_got[0, c])
        place_source(c, 0, 0, source_send[c])
        place_source(c, 1, 32, source_got[1, c])
        place_source(c, 2, 64, source_got_far[1, c])

    def operator(g, held, at):
        rows, after, before = pl.ds(at, 8), pl.ds(at + 1, 8), pl.ds(at - 1, 8)
        count = CLASSES[g]
        p = [held[c, rows, :] for c in range(count)]
        we = [grid_we[g][c, rows, :] for c in range(count)]
        ww = [grid_ww[g][rows, :]] + we[:-1]
        pe, pw = east_of(p, STEP[g]), west_of(p, STEP[g])
        residual = []
        for c in range(count):
            pull = (we[c] * pe[c] + ww[c] * pw[c]) + (
                grid_wn[g][c, rows, :] * held[c, after, :]
                + grid_wn[g][c, before, :] * held[c, before, :]
            )
            image = grid_dg[g][c, rows, :] * p[c] - pull
            residual.append(grid_b[g][c, rows, :] - image)
        return p, residual

    def span(g, low, high):
        return ORIGIN[g] + low, ORIGIN[g] + high

    def from_zero(g, low, high, held):
        def body(at):
            rows = pl.ds(at, 8)
            for c in range(CLASSES[g]):
                held[c, rows, :] = grid_b[g][c, rows, :] * grid_iv[g][c, rows, :]

        each_chunk(*span(g, low, high), body)

    def sweep(g, low, high, held, result):
        def body(at):
            rows = pl.ds(at, 8)
            p, residual = operator(g, held, at)
            for c in range(CLASSES[g]):
                result[c, rows, :] = p[c] + residual[c] * grid_iv[g][c, rows, :]

        each_chunk(*span(g, low, high), body)

    def restricted(g, low, high, held):
        def residual_rows(at):
            rows = pl.ds(at, 8)
            _, residual = operator(g, held, at)
            if g < 2:
                for c in range(CLASSES[g] // 2):
                    grid_r[g][c, rows, :] = residual[2 * c] + residual[2 * c + 1]
            else:
                even, east, west = pair_lanes(residual[0])
                grid_r[g][0, rows, :] = residual[0] + jnp.where(even, east, west)

        each_chunk(*span(g, low, high), residual_rows)

        def pair_rows(at):
            above = finer_rows(g + 1, at)
            for c in range(CLASSES[g + 1]):
                grid_b[g + 1][c, pl.ds(at, 8), :] = (
                    grid_r[g][c, pl.ds(above, 8, stride=2), :]
                    + grid_r[g][c, pl.ds(above + 1, 8, stride=2), :]
                )

        top = (high // 2 + 7) // 8 * 8
        each_chunk(*span(g + 1, low // 2 // 8 * 8, top), pair_rows)

    def corrected(g, low, high, held, correction):
        first, last = low // 2 // 8 * 8, (high // 2 + 7) // 8 * 8

        def body(at):
            above = finer_rows(g + 1, at)
            for c in range(CLASSES[g]):
                change = correction[c // 2, pl.ds(at, 8), :]
                for odd in (0, 1):
                    rows = pl.ds(above + odd, 8, stride=2)
                    held[c, rows, :] = held[c, rows, :] + change

        each_chunk(*span(g + 1, first, last), body)

    def coarse_source(cycle, reach):
        coarse_send[cycle] = grid_b[3][0, pl.ds(ORIGIN[3], 8), :]
        moves = LAT_MOVES[: 2 * reach]
        got = coarse_got.at[pl.ds(4 * cycle, 2 * reach)]
        copies = [
            send(coarse_send.at[cycle], got.at[i], 0, move) for i, move in enumerate(moves)
        ]
        launch(copies)
        if cycle == 0:
            for copy in weight_copies:
                copy.wait_recv()
            for held, first in ((grid_we[3], 0), (grid_wn[3], 8)):
                cut = pl.ds(first, 8)
                around(held, weight_send[cut, :], [weight_got.at[i, cut] for i in range(4)], LAT_MOVES)
            each_chunk(ORIGIN[3] - 8, ORIGIN[3] + 16, lambda at: finish_weights(3, pl.ds(at, 8)))
        for copy in copies:
            copy.wait_recv()
        around(grid_b[3], coarse_send[cycle], [got.at[i] for i in range(2 * reach)], moves)

    plans = (
        ((-40, 72), (-24, 40), (-16, 24), (-8, 16), (-16, 32), (-24, 56)),
        ((-24, 56), (-16, 32), (-8, 16), (-8, 16), (-8, 24), (-16, 48)),
        ((-16, 48), (-8, 24), (-8, 16), (-8, 16), (-8, 24), (-8, 40)),
    )
    for cycle in range(CYCLES):
        before0, down1, down2, up2, up1, after0 = plans[cycle]
        if cycle == 0:
            from_zero(0, *before0, grid_q[0])
        else:
            sweep(0, *before0, grid_p[0], grid_q[0])
        restricted(0, *before0, grid_q[0])
        from_zero(1, *down1, grid_q[1])
        restricted(1, *down1, grid_q[1])
        from_zero(2, *down2, grid_q[2])
        restricted(2, -8, 16, grid_q[2])
        coarse_source(cycle, 1 if cycle == 2 else 2)
        from_zero(3, -8, 16, grid_q[3])
        here, there_ = grid_q[3], grid_p[3]
        for _ in range(SWEEPS - 1):
            sweep(3, -8, 16, here, there_)
            here, there_ = there_, here
        corrected(2, *up2, grid_q[2], here)
        sweep(2, *up2, grid_q[2], grid_p[2])
        corrected(1, *up1, grid_q[1], grid_p[2])
        sweep(1, *up1, grid_q[1], grid_p[1])
        corrected(0, *after0, grid_q[0], grid_p[1])
        sweep(0, *after0, grid_q[0], grid_p[0])

    pressure = grid_p[0]
    own = pl.ds(ORIGIN[0], ROWS)
    p = [pressure[c, own, :] for c in range(4)]
    slope_east = [0.5 * (e - w) for e, w in zip(east_of(p, 1), west_of(p, 1))]
    slope_north = [
        0.5 * (pressure[c, pl.ds(ORIGIN[0] + 1, ROWS), :] - pressure[c, pl.ds(ORIGIN[0] - 1, ROWS), :])
        for c in range(4)
    ]
    stacked = jnp.concatenate(
        [jnp.concatenate(parts, axis=1) for parts in (p, slope_east, slope_north)], axis=0
    )
    ordered = exact_select(stacked, unchoice[...])
    p_out[...] = ordered[0:32]
    push_u_out[...] = GRAVITY_STEP * ordered[32:64]
    push_v_out[...] = GRAVITY_STEP * ordered[64:96]
    for store in stores:
        store.wait()
    for copy in started:
        copy.wait_send()


def finish(u_star, v_star, t, p, push_u, push_v, depth_ref, u_out, v_out, t_out, p_out):
    depth = depth_ref[...]
    p_out[...] = p[...]
    t_out[...] = t[...]
    for k in range(LEVELS):
        rows = slice(k * ROWS, (k + 1) * ROWS)
        wet = depth > k
        u_out[rows, :] = jnp.where(wet, u_star[rows, :] - push_u[...], 0.0)
        v_out[rows, :] = jnp.where(wet, v_star[rows, :] - push_v[...], 0.0)


def shards(lon_count, lat_count, u, v, t, depth, elevation):
    f32 = jnp.float32
    flat = (LEVELS * ROWS, COLS)
    block = pl.BlockSpec(memory_space=pltpu.VMEM)

    def grids(classes=CLASSES):
        return [pltpu.VMEM((c, h, LANES), f32) for c, h in zip(classes, HEIGHT)]

    anywhere = pl.BlockSpec(memory_space=pl.ANY)
    held = pl.pallas_call(
        functools.partial(kernel, lon_count, lat_count),
        out_shape=[jax.ShapeDtypeStruct(flat, f32)] * 3
        + [jax.ShapeDtypeStruct((ROWS, COLS), f32)] * 3,
        in_specs=[anywhere] * 5,
        out_specs=[anywhere] * 3 + [block] * 3,
        scratch_shapes=[
            pltpu.VMEM(flat, f32),
            pltpu.VMEM(flat, f32),
            pltpu.VMEM(flat, f32),
            pltpu.VMEM((ROWS, COLS), jnp.int32),
            pltpu.VMEM((ROWS, COLS), f32),
            pltpu.VMEM(flat, f32),
            pltpu.VMEM(flat, f32),
            pltpu.VMEM(flat, f32),
            pltpu.VMEM((2, 32, COLS), f32),
            pltpu.VMEM((2, 32, COLS), f32),
            pltpu.VMEM((2, 72, LANES), f32),
            pltpu.VMEM((2, 72, LANES), f32),
            pltpu.VMEM((2, 64, LANES), f32),
            pltpu.VMEM((2, 64, LANES), f32),
            pltpu.VMEM((2, ROWS, COLS), f32),
            pltpu.VMEM((2, 2, ROWS, COLS), f32),
            pltpu.VMEM((2, 2, 8, COLS), f32),
            pltpu.VMEM((4, ROWS, LANES), f32),
            pltpu.VMEM((2, 4, ROWS, LANES), f32),
            pltpu.VMEM((2, 4, 8, LANES), f32),
            pltpu.VMEM((8, LANES), f32),
            pltpu.VMEM((4, 8, LANES), f32),
            pltpu.VMEM((16, LANES), f32),
            pltpu.VMEM((4, 16, LANES), f32),
            pltpu.VMEM((CYCLES, 8, LANES), f32),
            pltpu.VMEM((10, 8, LANES), f32),
            pltpu.VMEM((WIDE, WIDE), jnp.bfloat16),
            pltpu.VMEM((WIDE, COLS), jnp.bfloat16),
            pltpu.VMEM((4, HEIGHT[0], LANES), f32),
            grids(),
            grids(),
            grids(),
            grids(),
            [pltpu.VMEM((h, LANES), f32) for h in HEIGHT],
            grids(),
            grids(),
            grids(),
            grids(),
            pltpu.SemaphoreType.DMA((5,)),
            pltpu.SemaphoreType.DMA((40,)),
            pltpu.SemaphoreType.DMA((40,)),
        ],
        compiler_params=pltpu.CompilerParams(
            collective_id=0, has_side_effects=True, vmem_limit_bytes=60 << 20
        ),
    )(u.reshape(flat), v.reshape(flat), t.reshape(flat), depth, elevation)
    outs = pl.pallas_call(
        finish,
        out_shape=[jax.ShapeDtypeStruct(flat, f32)] * 3
        + [jax.ShapeDtypeStruct((ROWS, COLS), f32)],
        in_specs=[block] * 7,
        out_specs=[block] * 4,
        compiler_params=pltpu.CompilerParams(vmem_limit_bytes=60 << 20),
    )(*held, depth)
    shape = (LEVELS, ROWS, COLS)
    return outs[0].reshape(shape), outs[1].reshape(shape), outs[2].reshape(shape), outs[3]


def solution(mesh):
    spec3, spec2 = P(None, "lat", "lon"), P("lat", "lon")
    return jax.shard_map(
        functools.partial(shards, mesh.shape["lon"], mesh.shape["lat"]),
        mesh=mesh,
        in_specs=(spec3, spec3, spec3, spec2, spec2),
        out_specs=(spec3, spec3, spec3, spec2),
        check_vma=False,
    )
```

```python
import functools

import jax
import jax.numpy as jnp
from jax import lax
from jax.experimental import pallas as pl
from jax.experimental.pallas import tpu as pltpu
from jax.sharding import PartitionSpec as P

LEVELS = 8
CYCLES = 3
SWEEPS = 4
TIME_STEP = 0.2
VISCOSITY = 1.0
DIFFUSIVITY = 1.0
CORIOLIS = 1.0
MASS_TERM = 0.05
GRAVITY_STEP = 0.5

ROWS = 32
COLS = 256
LANES = 128
WIDE = 512
MESH_IDS = pl.DeviceIdType.MESH

CLASSES = (4, 2, 1, 1)
STEP = (1, 1, 1, 2)
ORIGIN = (48, 32, 24, 16)
HEIGHT = (128, 80, 56, 40)
MASS = tuple(MASS_TERM * 4.0**g for g in range(4))

LAT_MOVES = (1, -1, 2, -2)
EARLY_LEVELS = 3


def east_of(parts, step):
    turned = pltpu.roll(parts[0], LANES - step, 1)
    return list(parts[1:]) + [turned]


def west_of(parts, step):
    turned = pltpu.roll(parts[-1], step, 1)
    return [turned] + list(parts[:-1])


def each_chunk(first, last, body, unroll=5):
    count = (last - first) // 8
    if count <= unroll:
        for i in range(count):
            body(first + 8 * i)
        return
    while count % unroll:
        unroll -= 1

    def step(i, carry):
        for j in range(unroll):
            body(pl.multiple_of(first + (i * unroll + j) * 8, 8))
        return carry

    lax.fori_loop(0, count // unroll, step, 0)


def split_three(values):
    high = values.astype(jnp.bfloat16)
    rest = values - high.astype(jnp.float32)
    middle = rest.astype(jnp.bfloat16)
    low = (rest - middle.astype(jnp.float32)).astype(jnp.bfloat16)
    return jnp.concatenate([high, middle, low], axis=0)


def exact_select(values, choice):
    count = values.shape[0]
    product = jnp.dot(split_three(values), choice, preferred_element_type=jnp.float32)
    return (product[:count] + product[count : 2 * count]) + product[2 * count :]


def kernel(
    lon_count,
    lat_count,
    u_far,
    v_far,
    t_far,
    depth_far,
    elevation_far,
    u_home,
    v_home,
    t_home,
    p_out,
    push_u_out,
    push_v_out,
    u_ref,
    v_ref,
    t_ref,
    depth_ref,
    elevation_ref,
    u_star,
    v_star,
    t_out,
    rows_send,
    rows_got,
    cols_send,
    cols_got,
    mean_send,
    mean_got,
    deep_send,
    deep_got,
    deep_got_far,
    source_send,
    source_got,
    source_got_far,
    ends_send,
    ends_got,
    weight_send,
    weight_got,
    coarse_send,
    coarse_got,
    choice,
    unchoice,
    deep,
    grid_b,
    grid_p,
    grid_q,
    grid_we,
    grid_ww,
    grid_wn,
    grid_dg,
    grid_iv,
    grid_r,
    load_sem,
    send_sem,
    recv_sem,
):
    lon = lax.axis_index("lon")
    lat = lax.axis_index("lat")
    sems = iter(range(64))

    def there(lon_move, lat_move):
        return {
            "lon": lax.rem(lon + lon_move + lon_count, lon_count),
            "lat": lax.rem(lat + lat_move + lat_count, lat_count),
        }

    def send(source, target, lon_move, lat_move):
        at = next(sems)
        return pltpu.make_async_remote_copy(
            src_ref=source,
            dst_ref=target,
            send_sem=send_sem.at[at],
            recv_sem=recv_sem.at[at],
            device_id=there(lon_move, lat_move),
            device_id_type=MESH_IDS,
        )

    def inside(lat_move):
        spot = lat + lat_move
        return jnp.where((spot >= 0) & (spot < lat_count), 1.0, 0.0).astype(jnp.float32)

    started = []

    def launch(copies):
        for copy in copies:
            copy.start()
        started.extend(copies)

    barrier = pltpu.get_barrier_semaphore()
    for lon_move, lat_move in [(1, 0), (-1, 0)] + [(0, m) for m in LAT_MOVES]:
        pl.semaphore_signal(
            barrier, inc=1, device_id=there(lon_move, lat_move), device_id_type=MESH_IDS
        )

    loads = [
        pltpu.make_async_copy(far, near, load_sem.at[i])
        for i, (far, near) in enumerate(
            (
                (depth_far, depth_ref),
                (elevation_far, elevation_ref),
                (u_far, u_ref),
                (v_far, v_ref),
                (t_far, t_ref),
            )
        )
    ]
    for load in loads:
        load.start()
    for load in loads:
        load.wait()

    depth = depth_ref[...].astype(jnp.float32)
    lane8 = lax.broadcasted_iota(jnp.int32, (8, LANES), 1)
    fields = (u_ref, v_ref, t_ref)
    for side, row in ((0, ROWS - 1), (1, 0)):
        for f, field in enumerate(fields):
            for k in range(LEVELS):
                rows_send[side, 8 * f + k : 8 * f + k + 1, :] = field[
                    k * ROWS + row : k * ROWS + row + 1, :
                ]
        rows_send[side, pl.ds(24, 8), :] = jnp.broadcast_to(depth[row : row + 1, :], (8, COLS))

    def pack(i, carry):
        at_last, at_first = carry
        rows = pl.ds(pl.multiple_of(8 * i, 8), 8)
        for f, field in enumerate(fields):
            here = lane8 == i + 32 * f
            at_last = jnp.where(here, field[rows, COLS - 1 : COLS], at_last)
            at_first = jnp.where(here, field[rows, 0:1], at_first)
        return at_last, at_first

    zero8 = jnp.zeros((8, LANES), jnp.float32)
    at_last, at_first = lax.fori_loop(0, 32, pack, (zero8, zero8), unroll=4)
    elevation = elevation_ref[...]
    deep_send[0] = depth
    for side, edge, tile in ((0, at_last, 1), (1, at_first, 0)):
        cut = slice(tile * LANES, (tile + 1) * LANES)
        cols_send[side, 0:32, :] = depth[:, cut]
        cols_send[side, 32:64, :] = elevation[:, cut]
        cols_send[side, 64:72, :] = edge

    pl.semaphore_wait(barrier, 2 + len(LAT_MOVES))
    row_copies = [
        send(rows_send.at[0], rows_got.at[0], 0, 1),
        send(rows_send.at[1], rows_got.at[1], 0, -1),
    ]
    column_copies = [
        send(cols_send.at[0], cols_got.at[0], 1, 0),
        send(cols_send.at[1], cols_got.at[1], -1, 0),
    ]
    launch(column_copies + row_copies)

    def depth_sends(part):
        source = deep_send.at[part]
        return [
            send(source, deep_got.at[part, 0], 0, 1),
            send(source, deep_got.at[part, 1], 0, -1),
            send(source.at[pl.ds(ROWS - 8, 8)], deep_got_far.at[part, 0], 0, 2),
            send(source.at[pl.ds(0, 8)], deep_got_far.at[part, 1], 0, -2),
        ]

    depth_copies = depth_sends(0)
    launch(depth_copies)

    row_number = lax.broadcasted_iota(jnp.int32, (ROWS, LANES), 0)
    place = (lat * ROWS + row_number).astype(jnp.float32)
    angle = jnp.pi * ((place + 0.5) / (ROWS * lat_count) - 0.5)
    turning = CORIOLIS * jnp.sin(angle)
    rotation = jnp.concatenate([turning, turning], axis=1)

    row = lax.broadcasted_iota(jnp.int32, (ROWS, COLS), 0)
    column = lax.broadcasted_iota(jnp.int32, (ROWS, COLS), 1)
    on_east, on_west = column == COLS - 1, column == 0
    on_north, on_south = row == ROWS - 1, row == 0

    def beside(values, east_edge, west_edge, north_edge, south_edge):
        return (
            jnp.where(on_east, east_edge, pltpu.roll(values, COLS - 1, 1)),
            jnp.where(on_west, west_edge, pltpu.roll(values, 1, 1)),
            jnp.where(on_north, north_edge, pltpu.roll(values, ROWS - 1, 0)),
            jnp.where(on_south, south_edge, pltpu.roll(values, 1, 0)),
        )

    def laplace(faces, values, nearby):
        terms = [jnp.where(face, near - values, 0.0) for face, near in zip(faces, nearby)]
        return (terms[0] + terms[1]) + (terms[2] + terms[3])

    def momentum(faces, u, near_u, v, near_v):
        guess_u = u + TIME_STEP * (VISCOSITY * laplace(faces, u, near_u) + rotation * v)
        guess_v = v + TIME_STEP * (VISCOSITY * laplace(faces, v, near_v) - rotation * u)
        return guess_u, guess_v

    inner_depth = [jnp.minimum(depth, near) for near in beside(depth, 0.0, 0.0, 0.0, 0.0)]

    def inner(k, carry):
        sum_u, sum_v = carry
        level = k.astype(jnp.float32)
        faces = [level < limit for limit in inner_depth]
        rows = pl.ds(pl.multiple_of(k * ROWS, ROWS), ROWS)
        u, v = u_ref[rows, :], v_ref[rows, :]
        near_u, near_v = beside(u, 0.0, 0.0, 0.0, 0.0), beside(v, 0.0, 0.0, 0.0, 0.0)
        guess_u, guess_v = momentum(faces, u, near_u, v, near_v)
        wet = level < depth
        return sum_u + jnp.where(wet, guess_u, 0.0), sum_v + jnp.where(wet, guess_v, 0.0)

    zero = jnp.zeros((ROWS, COLS), jnp.float32)
    sum_u, sum_v = lax.fori_loop(0, LEVELS, inner, (zero, zero))
    gain = TIME_STEP * VISCOSITY / LEVELS

    for copy in row_copies:
        copy.wait_recv()
    north_depth = rows_got[1, 24:25, :] * inside(1)
    south_depth = rows_got[0, 24:25, :] * inside(-1)
    level8 = lax.broadcasted_iota(jnp.int32, (LEVELS, COLS), 0).astype(jnp.float32)

    def row_flux(f, side, limit):
        step = rows_got[side, 8 * f : 8 * f + 8, :] - rows_send[1 - side, 8 * f : 8 * f + 8, :]
        return gain * jnp.sum(jnp.where(level8 < limit, step, 0.0), axis=0, keepdims=True)

    north_limit = jnp.minimum(depth[ROWS - 1 : ROWS, :], north_depth)
    south_limit = jnp.minimum(depth[0:1, :], south_depth)

    def mean(f, total):
        return (
            total * (1.0 / LEVELS)
            + jnp.where(on_north, row_flux(f, 1, north_limit), 0.0)
            + jnp.where(on_south, row_flux(f, 0, south_limit), 0.0)
        )

    mean_u, mean_v = mean(0, sum_u), mean(1, sum_v)
    for side, tile in ((0, 1), (1, 0)):
        cut = slice(tile * LANES, (tile + 1) * LANES)
        mean_send[side, 0:32, :] = mean_u[:, cut]
        mean_send[side, 32:64, :] = mean_v[:, cut]
    mean_copies = [
        send(mean_send.at[0], mean_got.at[0], 1, 0),
        send(mean_send.at[1], mean_got.at[1], -1, 0),
    ]
    launch(mean_copies)

    def order(n):
        return ((((n & 127) + 32) & 127) << 2) + (n >> 7)

    wanted = order(lax.broadcasted_iota(jnp.int32, (1, WIDE), 1))

    def fill(i, carry):
        rows = pl.ds(pl.multiple_of(32 * i, 32), 32)
        k = lax.broadcasted_iota(jnp.int32, (32, WIDE), 0) + 32 * i
        choice[rows, :] = jnp.where(k == wanted, 1.0, 0.0).astype(jnp.bfloat16)
        n = lax.broadcasted_iota(jnp.int32, (32, COLS), 0) + 32 * i
        column = lax.broadcasted_iota(jnp.int32, (32, COLS), 1) + LANES
        unchoice[rows, :] = jnp.where(order(n) == column, 1.0, 0.0).astype(jnp.bfloat16)
        return carry

    lax.fori_loop(0, WIDE // 32, fill, 0)
    for ref in list(grid_p) + list(grid_q) + list(grid_b) + list(grid_wn) + [deep]:
        ref[...] = jnp.zeros_like(ref)
    for copy in column_copies:
        copy.wait_recv()

    west_tile, east_tile = cols_got.at[0], cols_got.at[1]
    deep_send[1, :, 0:LANES] = west_tile[0:32, :]
    deep_send[1, :, LANES:COLS] = east_tile[0:32, :]
    more_depth = depth_sends(1)
    launch(more_depth)
    depth_copies = depth_copies + more_depth

    lane_row = lane8 & 3
    lane_level = ((lane8 >> 2) & 7).astype(jnp.float32)

    def packed(values, column):
        result = zero8
        for g in range(4):
            result = jnp.where(lane_row == g, values[8 * g : 8 * g + 8, column : column + 1], result)
        return result

    def column_flux(own, other, own_depth, other_depth):
        limit = jnp.minimum(own_depth, other_depth)
        flux = jnp.where(lane_level < limit, other - own, 0.0)
        for turn in (4, 8, 16):
            flux = flux + pltpu.roll(flux, turn, 1)
        flux = gain * flux
        return [
            jnp.concatenate([flux[:, at + g : at + g + 1] for g in range(4)], axis=0)
            for at in (28, 60)
        ]

    east_flux = column_flux(
        cols_send[0, 64:72, :],
        east_tile[64:72, :],
        packed(depth, COLS - 1),
        packed(east_tile[0:32, :], 0),
    )
    west_flux = column_flux(
        cols_send[1, 64:72, :],
        west_tile[64:72, :],
        packed(depth, 0),
        packed(west_tile[0:32, :], LANES - 1),
    )

    depth_near = beside(
        depth,
        east_tile[0:32, 0:1],
        west_tile[0:32, LANES - 1 : LANES],
        north_depth,
        south_depth,
    )
    open_depth = [jnp.minimum(depth, near) for near in depth_near]
    east_edges = east_tile[64:72, :]
    west_edges = west_tile[64:72, :]

    def near_field(f, field, k):
        values = field[pl.ds(pl.multiple_of(k * ROWS, ROWS), ROWS), :]
        turn = lax.rem(2 * LANES - 32 * f - 4 * k, LANES)
        east_lanes = pltpu.roll(east_edges, turn, 1)
        west_lanes = pltpu.roll(west_edges, turn, 1)
        east_edge = jnp.concatenate([east_lanes[:, g : g + 1] for g in range(4)], axis=0)
        west_edge = jnp.concatenate([west_lanes[:, g : g + 1] for g in range(4)], axis=0)
        north_edge = rows_got[1, pl.ds(8 * f + k, 1), :]
        south_edge = rows_got[0, pl.ds(8 * f + k, 1), :]
        return values, beside(values, east_edge, west_edge, north_edge, south_edge)

    def layer(k, carry):
        level = k.astype(jnp.float32)
        faces = [level < limit for limit in open_depth]
        t, near_t = near_field(2, t_ref, k)
        u, near_u = near_field(0, u_ref, k)
        v, near_v = near_field(1, v_ref, k)
        spread = laplace(faces, t, near_t)
        east = jnp.where(faces[0], (u + near_u[0]) * 0.5, 0.0)
        west = jnp.where(faces[1], (near_u[1] + u) * 0.5, 0.0)
        north = jnp.where(faces[2], (v + near_v[2]) * 0.5, 0.0)
        south = jnp.where(faces[3], (near_v[3] + v) * 0.5, 0.0)
        transport = (east * (t + near_t[0]) - west * (near_t[1] + t)) + (
            north * (t + near_t[2]) - south * (near_t[3] + t)
        )
        result = t + TIME_STEP * (DIFFUSIVITY * spread - 0.5 * transport)
        guess_u, guess_v = momentum(faces, u, near_u, v, near_v)
        wet = level < depth
        rows = pl.ds(pl.multiple_of(k * ROWS, ROWS), ROWS)
        u_star[rows, :] = jnp.where(wet, guess_u, 0.0)
        v_star[rows, :] = jnp.where(wet, guess_v, 0.0)
        t_out[rows, :] = jnp.where(wet, result, 0.0)
        return carry

    lax.fori_loop(0, EARLY_LEVELS, layer, 0)

    for copy in mean_copies:
        copy.wait_recv()
    west_mean, east_mean = mean_got.at[0], mean_got.at[1]
    tile_lane = lax.broadcasted_iota(jnp.int32, (ROWS, LANES), 1)
    tile_first, tile_last = tile_lane == 0, tile_lane == LANES - 1

    def window(f, values):
        cut = slice(32 * f, 32 * f + 32)
        return jnp.concatenate(
            [
                west_mean[cut, :] - jnp.where(tile_last, west_flux[f], 0.0),
                values[:, 0:LANES] + jnp.where(tile_first, west_flux[f], 0.0),
                values[:, LANES:COLS] + jnp.where(tile_last, east_flux[f], 0.0),
                east_mean[cut, :] - jnp.where(tile_first, east_flux[f], 0.0),
            ],
            axis=1,
        )

    wide_u, wide_v = window(0, mean_u), window(1, mean_v)
    wide_eta = jnp.concatenate([west_tile[32:64, :], elevation, east_tile[32:64, :]], axis=1)
    wide_row = lax.broadcasted_iota(jnp.int32, (ROWS, WIDE), 0)
    north_v = jnp.where(wide_row == ROWS - 1, 0.0, pltpu.roll(wide_v, ROWS - 1, 0))
    south_v = jnp.where(wide_row == 0, 0.0, pltpu.roll(wide_v, 1, 0))
    across = pltpu.roll(wide_u, WIDE - 1, 1) - pltpu.roll(wide_u, 1, 1)
    depth_wide = jnp.concatenate([west_tile[0:32, :], depth, east_tile[0:32, :]], axis=1)
    source = jnp.where(
        depth_wide > 0.5, wide_eta - 0.5 * (across + (north_v - south_v)), 0.0
    )
    ends = jnp.where(
        lax.broadcasted_iota(jnp.int32, (16, WIDE), 0) == 0, wide_v[0:1, :], wide_v[31:32, :]
    )
    by_class = exact_select(jnp.concatenate([source, ends], axis=0), choice[...])
    for c in range(4):
        cut = slice(LANES * c, LANES * (c + 1))
        source_send[c] = by_class[0:32, cut]
        ends_send[c : c + 1, :] = by_class[32:33, cut]
        ends_send[4 + c : 5 + c, :] = by_class[33:34, cut]
    source_copies = [
        send(ends_send, ends_got.at[i], 0, move) for i, move in enumerate(LAT_MOVES)
    ] + [
        send(source_send, source_got.at[0], 0, 1),
        send(source_send, source_got.at[1], 0, -1),
        send(source_send.at[:, pl.ds(ROWS - 8, 8)], source_got_far.at[0], 0, 2),
        send(source_send.at[:, pl.ds(0, 8)], source_got_far.at[1], 0, -2),
    ]
    launch(source_copies)

    for copy in depth_copies:
        copy.wait_recv()

    def slot_of(lat_move):
        return LAT_MOVES.index(-lat_move)

    def wide_depth(own, halo, mask):
        return mask * jnp.concatenate([halo[:, 0:LANES], own, halo[:, LANES:COLS]], axis=1)

    blocks = [
        wide_depth(deep_got_far[0, 0], deep_got_far[1, 0], inside(-2)),
        wide_depth(deep_got[0, 0], deep_got[1, 0], inside(-1)),
        wide_depth(deep_send[0], deep_send[1], 1.0),
        wide_depth(deep_got[0, 1], deep_got[1, 1], inside(1)),
        wide_depth(deep_got_far[0, 1], deep_got_far[1, 1], inside(2)),
    ]
    by_class = jnp.dot(
        jnp.concatenate(blocks, axis=0).astype(jnp.bfloat16),
        choice[...],
        preferred_element_type=jnp.float32,
    )
    for c in range(4):
        deep[c, pl.ds(ORIGIN[0] - 40, 112), :] = by_class[:, LANES * c : LANES * (c + 1)]

    def finish_weights(g, rows):
        we = [grid_we[g][c, rows, :] for c in range(CLASSES[g])]
        ww = west_of(we, STEP[g])
        grid_ww[g][rows, :] = ww[0]
        before = pl.ds(rows.start - 1, 8)
        for c in range(CLASSES[g]):
            near = (we[c] + ww[c]) + (grid_wn[g][c, rows, :] + grid_wn[g][c, before, :])
            grid_dg[g][c, rows, :] = MASS[g] + near
            grid_iv[g][c, rows, :] = 1.0 / (MASS[g] + 2.0 * near)

    def fine_weights(at):
        rows, after = pl.ds(at, 8), pl.ds(at + 1, 8)
        columns = [deep[c, rows, :] * (1.0 / LEVELS) for c in range(4)]
        for c, near in enumerate(east_of(columns, 1)):
            grid_we[0][c, rows, :] = jnp.minimum(columns[c], near)
            north = deep[c, after, :] * (1.0 / LEVELS)
            grid_wn[0][c, rows, :] = jnp.minimum(columns[c], north)

    def whole(g):
        return tuple(ORIGIN[g] + end for end in ((-40, 72), (-24, 40), (-16, 24), (0, 8))[g])

    def pair_lanes(values):
        even = (lax.broadcasted_iota(jnp.int32, values.shape, 1) & 1) == 0
        return even, pltpu.roll(values, LANES - 1, 1), pltpu.roll(values, 1, 1)

    def finer_rows(g, at):
        return 2 * (at - ORIGIN[g]) + ORIGIN[g - 1]

    each_chunk(*whole(0), fine_weights)
    each_chunk(*whole(0), lambda at: finish_weights(0, pl.ds(at, 8)))
    for g in (1, 2, 3):

        def coarse_weights(at, g=g):
            rows = pl.ds(at, 8)
            above = finer_rows(g, at)
            even_rows, odd_rows = pl.ds(above, 8, stride=2), pl.ds(above + 1, 8, stride=2)
            finer_we, finer_wn = grid_we[g - 1], grid_wn[g - 1]
            if g < 3:
                for c in range(CLASSES[g]):
                    grid_we[g][c, rows, :] = (
                        finer_we[2 * c + 1, even_rows, :] + finer_we[2 * c + 1, odd_rows, :]
                    )
                    grid_wn[g][c, rows, :] = (
                        finer_wn[2 * c, odd_rows, :] + finer_wn[2 * c + 1, odd_rows, :]
                    )
            else:
                we = finer_we[0, even_rows, :] + finer_we[0, odd_rows, :]
                even, east, west = pair_lanes(we)
                grid_we[g][0, rows, :] = jnp.where(even, east, we)
                wn = finer_wn[0, odd_rows, :]
                even, east, west = pair_lanes(wn)
                grid_wn[g][0, rows, :] = wn + jnp.where(even, east, west)

        each_chunk(*whole(g), coarse_weights)
        if g < 3:
            each_chunk(*whole(g), lambda at, g=g: finish_weights(g, pl.ds(at, 8)))

    upper = lax.broadcasted_iota(jnp.int32, (8, LANES), 0) >= 4

    def around(held, own, got, moves):
        def block(move):
            return got[moves.index(-move)][...] * inside(move)

        held[0, pl.ds(ORIGIN[3], 8), :] = jnp.where(upper, pltpu.roll(block(1), 4, 0), own)
        lower = pltpu.roll(block(-1), 4, 0)
        if len(moves) == 4:
            lower = jnp.where(upper, lower, block(-2))
            held[0, pl.ds(ORIGIN[3] + 8, 8), :] = block(2)
        held[0, pl.ds(ORIGIN[3] - 8, 8), :] = lower

    weight_send[0:8, :] = grid_we[3][0, pl.ds(ORIGIN[3], 8), :]
    weight_send[8:16, :] = grid_wn[3][0, pl.ds(ORIGIN[3], 8), :]
    weight_copies = [
        send(weight_send, weight_got.at[i], 0, move) for i, move in enumerate(LAT_MOVES)
    ]
    launch(weight_copies)

    lax.fori_loop(EARLY_LEVELS, LEVELS, layer, 0)
    stores = [
        pltpu.make_async_copy(near, far, load_sem.at[i])
        for i, (near, far) in enumerate(
            ((u_star, u_home), (v_star, v_home), (t_out, t_home))
        )
    ]
    for store in stores:
        store.start()


    for copy in source_copies:
        copy.wait_recv()

    rows32 = lax.broadcasted_iota(jnp.int32, (ROWS, LANES), 0)

    def ends(move, spot):
        held = ends_send if move == 0 else ends_got.at[slot_of(move)]
        return held[spot : spot + 1, :] * (0.5 * inside(move))

    def place_source(c, move, first, values):
        rows = pl.ds(ORIGIN[0] + first, values.shape[0])
        at = rows32[: values.shape[0]] + (first - 32 * move)
        if move < 2:
            values = values - jnp.where(at == ROWS - 1, ends(move + 1, c), 0.0)
        if move > -2:
            values = values + jnp.where(at == 0, ends(move - 1, 4 + c), 0.0)
        grid_b[0][c, rows, :] = jnp.where(deep[c, rows, :] > 0.5, values, 0.0)

    for c in range(4):
        place_source(c, -2, -40, source_got_far[0, c])
        place_source(c, -1, -32, source_got[0, c])
        place_source(c, 0, 0, source_send[c])
        place_source(c, 1, 32, source_got[1, c])
        place_source(c, 2, 64, source_got_far[1, c])

    def operator(g, held, at):
        rows, after, before = pl.ds(at, 8), pl.ds(at + 1, 8), pl.ds(at - 1, 8)
        count = CLASSES[g]
        p = [held[c, rows, :] for c in range(count)]
        we = [grid_we[g][c, rows, :] for c in range(count)]
        ww = [grid_ww[g][rows, :]] + we[:-1]
        pe, pw = east_of(p, STEP[g]), west_of(p, STEP[g])
        residual = []
        for c in range(count):
            pull = (we[c] * pe[c] + ww[c] * pw[c]) + (
                grid_wn[g][c, rows, :] * held[c, after, :]
                + grid_wn[g][c, before, :] * held[c, before, :]
            )
            image = grid_dg[g][c, rows, :] * p[c] - pull
            residual.append(grid_b[g][c, rows, :] - image)
        return p, residual

    def span(g, low, high):
        return ORIGIN[g] + low, ORIGIN[g] + high

    def from_zero(g, low, high, held):
        def body(at):
            rows = pl.ds(at, 8)
            for c in range(CLASSES[g]):
                held[c, rows, :] = grid_b[g][c, rows, :] * grid_iv[g][c, rows, :]

        each_chunk(*span(g, low, high), body)

    def sweep(g, low, high, held, result):
        def body(at):
            rows = pl.ds(at, 8)
            p, residual = operator(g, held, at)
            for c in range(CLASSES[g]):
                result[c, rows, :] = p[c] + residual[c] * grid_iv[g][c, rows, :]

        each_chunk(*span(g, low, high), body)

    def restricted(g, low, high, held):
        def residual_rows(at):
            rows = pl.ds(at, 8)
            _, residual = operator(g, held, at)
            if g < 2:
                for c in range(CLASSES[g] // 2):
                    grid_r[g][c, rows, :] = residual[2 * c] + residual[2 * c + 1]
            else:
                even, east, west = pair_lanes(residual[0])
                grid_r[g][0, rows, :] = residual[0] + jnp.where(even, east, west)

        each_chunk(*span(g, low, high), residual_rows)

        def pair_rows(at):
            above = finer_rows(g + 1, at)
            for c in range(CLASSES[g + 1]):
                grid_b[g + 1][c, pl.ds(at, 8), :] = (
                    grid_r[g][c, pl.ds(above, 8, stride=2), :]
                    + grid_r[g][c, pl.ds(above + 1, 8, stride=2), :]
                )

        top = (high // 2 + 7) // 8 * 8
        each_chunk(*span(g + 1, low // 2 // 8 * 8, top), pair_rows)

    def corrected(g, low, high, held, correction):
        first, last = low // 2 // 8 * 8, (high // 2 + 7) // 8 * 8

        def body(at):
            above = finer_rows(g + 1, at)
            for c in range(CLASSES[g]):
                change = correction[c // 2, pl.ds(at, 8), :]
                for odd in (0, 1):
                    rows = pl.ds(above + odd, 8, stride=2)
                    held[c, rows, :] = held[c, rows, :] + change

        each_chunk(*span(g + 1, first, last), body)

    def coarse_source(cycle, reach):
        coarse_send[cycle] = grid_b[3][0, pl.ds(ORIGIN[3], 8), :]
        moves = LAT_MOVES[: 2 * reach]
        got = coarse_got.at[pl.ds(4 * cycle, 2 * reach)]
        copies = [
            send(coarse_send.at[cycle], got.at[i], 0, move) for i, move in enumerate(moves)
        ]
        launch(copies)
        if cycle == 0:
            for copy in weight_copies:
                copy.wait_recv()
            for held, first in ((grid_we[3], 0), (grid_wn[3], 8)):
                cut = pl.ds(first, 8)
                around(held, weight_send[cut, :], [weight_got.at[i, cut] for i in range(4)], LAT_MOVES)
            each_chunk(ORIGIN[3] - 8, ORIGIN[3] + 16, lambda at: finish_weights(3, pl.ds(at, 8)))
        for copy in copies:
            copy.wait_recv()
        around(grid_b[3], coarse_send[cycle], [got.at[i] for i in range(2 * reach)], moves)

    plans = (
        ((-40, 72), (-24, 40), (-16, 24), (-8, 16), (-16, 32), (-24, 56)),
        ((-24, 56), (-16, 32), (-8, 16), (-8, 16), (-8, 24), (-16, 48)),
        ((-16, 48), (-8, 24), (-8, 16), (-8, 16), (-8, 24), (-8, 40)),
    )
    for cycle in range(CYCLES):
        before0, down1, down2, up2, up1, after0 = plans[cycle]
        if cycle == 0:
            from_zero(0, *before0, grid_q[0])
        else:
            sweep(0, *before0, grid_p[0], grid_q[0])
        restricted(0, *before0, grid_q[0])
        from_zero(1, *down1, grid_q[1])
        restricted(1, *down1, grid_q[1])
        from_zero(2, *down2, grid_q[2])
        restricted(2, -8, 16, grid_q[2])
        coarse_source(cycle, 1 if cycle == 2 else 2)
        from_zero(3, -8, 16, grid_q[3])
        here, there_ = grid_q[3], grid_p[3]
        for _ in range(SWEEPS - 1):
            sweep(3, -8, 16, here, there_)
            here, there_ = there_, here
        corrected(2, *up2, grid_q[2], here)
        sweep(2, *up2, grid_q[2], grid_p[2])
        corrected(1, *up1, grid_q[1], grid_p[2])
        sweep(1, *up1, grid_q[1], grid_p[1])
        corrected(0, *after0, grid_q[0], grid_p[1])
        sweep(0, *after0, grid_q[0], grid_p[0])

    pressure = grid_p[0]
    own = pl.ds(ORIGIN[0], ROWS)
    p = [pressure[c, own, :] for c in range(4)]
    slope_east = [0.5 * (e - w) for e, w in zip(east_of(p, 1), west_of(p, 1))]
    slope_north = [
        0.5 * (pressure[c, pl.ds(ORIGIN[0] + 1, ROWS), :] - pressure[c, pl.ds(ORIGIN[0] - 1, ROWS), :])
        for c in range(4)
    ]
    stacked = jnp.concatenate(
        [jnp.concatenate(parts, axis=1) for parts in (p, slope_east, slope_north)], axis=0
    )
    ordered = exact_select(stacked, unchoice[...])
    p_out[...] = ordered[0:32]
    push_u_out[...] = GRAVITY_STEP * ordered[32:64]
    push_v_out[...] = GRAVITY_STEP * ordered[64:96]
    for store in stores:
        store.wait()
    for copy in started:
        copy.wait_send()


def finish(u_star, v_star, t, p, push_u, push_v, depth_ref, u_out, v_out, t_out, p_out):
    depth = depth_ref[...]
    p_out[...] = p[...]
    t_out[...] = t[...]
    for k in range(LEVELS):
        rows = slice(k * ROWS, (k + 1) * ROWS)
        wet = depth > k
        u_out[rows, :] = jnp.where(wet, u_star[rows, :] - push_u[...], 0.0)
        v_out[rows, :] = jnp.where(wet, v_star[rows, :] - push_v[...], 0.0)


def shards(lon_count, lat_count, u, v, t, depth, elevation):
    f32 = jnp.float32
    flat = (LEVELS * ROWS, COLS)
    block = pl.BlockSpec(memory_space=pltpu.VMEM)

    def grids(classes=CLASSES):
        return [pltpu.VMEM((c, h, LANES), f32) for c, h in zip(classes, HEIGHT)]

    anywhere = pl.BlockSpec(memory_space=pl.ANY)
    held = pl.pallas_call(
        functools.partial(kernel, lon_count, lat_count),
        out_shape=[jax.ShapeDtypeStruct(flat, f32)] * 3
        + [jax.ShapeDtypeStruct((ROWS, COLS), f32)] * 3,
        in_specs=[anywhere] * 5,
        out_specs=[anywhere] * 3 + [block] * 3,
        scratch_shapes=[
            pltpu.VMEM(flat, f32),
            pltpu.VMEM(flat, f32),
            pltpu.VMEM(flat, f32),
            pltpu.VMEM((ROWS, COLS), jnp.int32),
            pltpu.VMEM((ROWS, COLS), f32),
            pltpu.VMEM(flat, f32),
            pltpu.VMEM(flat, f32),
            pltpu.VMEM(flat, f32),
            pltpu.VMEM((2, 32, COLS), f32),
            pltpu.VMEM((2, 32, COLS), f32),
            pltpu.VMEM((2, 72, LANES), f32),
            pltpu.VMEM((2, 72, LANES), f32),
            pltpu.VMEM((2, 64, LANES), f32),
            pltpu.VMEM((2, 64, LANES), f32),
            pltpu.VMEM((2, ROWS, COLS), f32),
            pltpu.VMEM((2, 2, ROWS, COLS), f32),
            pltpu.VMEM((2, 2, 8, COLS), f32),
            pltpu.VMEM((4, ROWS, LANES), f32),
            pltpu.VMEM((2, 4, ROWS, LANES), f32),
            pltpu.VMEM((2, 4, 8, LANES), f32),
            pltpu.VMEM((8, LANES), f32),
            pltpu.VMEM((4, 8, LANES), f32),
            pltpu.VMEM((16, LANES), f32),
            pltpu.VMEM((4, 16, LANES), f32),
            pltpu.VMEM((CYCLES, 8, LANES), f32),
            pltpu.VMEM((10, 8, LANES), f32),
            pltpu.VMEM((WIDE, WIDE), jnp.bfloat16),
            pltpu.VMEM((WIDE, COLS), jnp.bfloat16),
            pltpu.VMEM((4, HEIGHT[0], LANES), f32),
            grids(),
            grids(),
            grids(),
            grids(),
            [pltpu.VMEM((h, LANES), f32) for h in HEIGHT],
            grids(),
            grids(),
            grids(),
            grids(),
            pltpu.SemaphoreType.DMA((5,)),
            pltpu.SemaphoreType.DMA((40,)),
            pltpu.SemaphoreType.DMA((40,)),
        ],
        compiler_params=pltpu.CompilerParams(
            collective_id=0, has_side_effects=True, vmem_limit_bytes=60 << 20
        ),
    )(u.reshape(flat), v.reshape(flat), t.reshape(flat), depth, elevation)
    outs = pl.pallas_call(
        finish,
        out_shape=[jax.ShapeDtypeStruct(flat, f32)] * 3
        + [jax.ShapeDtypeStruct((ROWS, COLS), f32)],
        in_specs=[block] * 7,
        out_specs=[block] * 4,
        compiler_params=pltpu.CompilerParams(vmem_limit_bytes=60 << 20),
    )(*held, depth)
    shape = (LEVELS, ROWS, COLS)
    return outs[0].reshape(shape), outs[1].reshape(shape), outs[2].reshape(shape), outs[3]


def solution(mesh):
    spec3, spec2 = P(None, "lat", "lon"), P("lat", "lon")
    return jax.shard_map(
        functools.partial(shards, mesh.shape["lon"], mesh.shape["lat"]),
        mesh=mesh,
        in_specs=(spec3, spec3, spec3, spec2, spec2),
        out_specs=(spec3, spec3, spec3, spec2),
        check_vma=False,
    )
```

```python
import functools

import jax
import jax.numpy as jnp
from jax import lax
from jax.experimental import pallas as pl
from jax.experimental.pallas import tpu as pltpu
from jax.sharding import PartitionSpec as P

LEVELS = 8
CYCLES = 3
SWEEPS = 4
TIME_STEP = 0.2
VISCOSITY = 1.0
DIFFUSIVITY = 1.0
CORIOLIS = 1.0
MASS_TERM = 0.05
GRAVITY_STEP = 0.5

ROWS = 32
COLS = 256
LANES = 128
WIDE = 512
MESH_IDS = pl.DeviceIdType.MESH

CLASSES = (4, 2, 1, 1)
STEP = (1, 1, 1, 2)
ORIGIN = (48, 32, 24, 16)
HEIGHT = (128, 80, 56, 40)
MASS = tuple(MASS_TERM * 4.0**g for g in range(4))

LAT_MOVES = (1, -1, 2, -2)
EARLY_LEVELS = 3


def east_of(parts, step):
    turned = pltpu.roll(parts[0], LANES - step, 1)
    return list(parts[1:]) + [turned]


def west_of(parts, step):
    turned = pltpu.roll(parts[-1], step, 1)
    return [turned] + list(parts[:-1])


def each_chunk(first, last, body, unroll=5):
    count = (last - first) // 8
    if count <= unroll:
        for i in range(count):
            body(first + 8 * i)
        return
    while count % unroll:
        unroll -= 1

    def step(i, carry):
        for j in range(unroll):
            body(pl.multiple_of(first + (i * unroll + j) * 8, 8))
        return carry

    lax.fori_loop(0, count // unroll, step, 0)


def split_three(values):
    high = values.astype(jnp.bfloat16)
    rest = values - high.astype(jnp.float32)
    middle = rest.astype(jnp.bfloat16)
    low = (rest - middle.astype(jnp.float32)).astype(jnp.bfloat16)
    return jnp.concatenate([high, middle, low], axis=0)


def exact_select(values, choice):
    count = values.shape[0]
    product = jnp.dot(split_three(values), choice, preferred_element_type=jnp.float32)
    return (product[:count] + product[count : 2 * count]) + product[2 * count :]


class Link:
    def __init__(self, copy, leaves, comes):
        self.copy, self.leaves, self.comes = copy, leaves, comes

    def start(self):
        if self.leaves is None:
            self.copy.start()
        else:
            pl.when(self.leaves)(self.copy.start)

    def wait_send(self):
        if self.leaves is None:
            self.copy.wait_send()
        else:
            pl.when(self.leaves)(self.copy.wait_send)

    def wait_recv(self):
        if self.comes is None:
            self.copy.wait_recv()
        else:
            pl.when(self.comes)(self.copy.wait_recv)


def kernel(
    lon_count,
    lat_count,
    u_far,
    v_far,
    t_far,
    depth_far,
    elevation_far,
    u_out,
    v_out,
    t_out,
    p_out,
    u_ref,
    v_ref,
    t_ref,
    depth_ref,
    elevation_ref,
    u_star,
    v_star,
    rows_send,
    rows_got,
    cols_send,
    cols_got,
    mean_send,
    mean_got,
    deep_send,
    deep_got,
    deep_got_far,
    source_send,
    source_got,
    source_got_far,
    ends_send,
    ends_got,
    weight_send,
    weight_got,
    coarse_send,
    coarse_got,
    choice,
    unchoice,
    deep,
    grid_b,
    grid_p,
    grid_q,
    grid_we,
    grid_ww,
    grid_wn,
    grid_dg,
    grid_iv,
    grid_r,
    load_sem,
    send_sem,
    recv_sem,
):
    lon = lax.axis_index("lon")
    lat = lax.axis_index("lat")
    sems = iter(range(64))

    def there(lon_move, lat_move):
        return {
            "lon": lax.rem(lon + lon_move + lon_count, lon_count),
            "lat": lax.rem(lat + lat_move + lat_count, lat_count),
        }

    def send(source, target, lon_move, lat_move):
        at = next(sems)
        copy = pltpu.make_async_remote_copy(
            src_ref=source,
            dst_ref=target,
            send_sem=send_sem.at[at],
            recv_sem=recv_sem.at[at],
            device_id=there(lon_move, lat_move),
            device_id_type=MESH_IDS,
        )
        if lat_move == 0:
            return Link(copy, None, None)
        return Link(copy, inside(lat_move), inside(-lat_move))

    def inside(lat_move):
        return (lat + lat_move >= 0) & (lat + lat_move < lat_count)

    def kept(lat_move, values):
        if lat_move == 0:
            return values
        return jnp.where(inside(lat_move), values, jnp.zeros_like(values))

    started = []

    def launch(copies):
        for copy in copies:
            copy.start()
        started.extend(copies)

    barrier = pltpu.get_barrier_semaphore()
    for lon_move in (1, -1):
        pl.semaphore_signal(
            barrier, inc=1, device_id=there(lon_move, 0), device_id_type=MESH_IDS
        )
    beside_count = jnp.int32(2)
    for lat_move in LAT_MOVES:
        beside_count = beside_count + inside(lat_move).astype(jnp.int32)

        @pl.when(inside(lat_move))
        def _(lat_move=lat_move):
            pl.semaphore_signal(
                barrier, inc=1, device_id=there(0, lat_move), device_id_type=MESH_IDS
            )


    loads = [
        pltpu.make_async_copy(far, near, load_sem.at[i])
        for i, (far, near) in enumerate(
            (
                (depth_far, depth_ref),
                (elevation_far, elevation_ref),
                (u_far, u_ref),
                (v_far, v_ref),
                (t_far, t_ref),
            )
        )
    ]
    for load in loads:
        load.start()
    for load in loads:
        load.wait()

    depth = depth_ref[...].astype(jnp.float32)
    lane8 = lax.broadcasted_iota(jnp.int32, (8, LANES), 1)
    fields = (u_ref, v_ref, t_ref)
    for side, row in ((0, ROWS - 1), (1, 0)):
        for f, field in enumerate(fields):
            for k in range(LEVELS):
                rows_send[side, 8 * f + k : 8 * f + k + 1, :] = field[
                    k * ROWS + row : k * ROWS + row + 1, :
                ]
        rows_send[side, pl.ds(24, 8), :] = jnp.broadcast_to(depth[row : row + 1, :], (8, COLS))

    def pack(i, carry):
        at_last, at_first = carry
        rows = pl.ds(pl.multiple_of(8 * i, 8), 8)
        for f, field in enumerate(fields):
            here = lane8 == i + 32 * f
            at_last = jnp.where(here, field[rows, COLS - 1 : COLS], at_last)
            at_first = jnp.where(here, field[rows, 0:1], at_first)
        return at_last, at_first

    zero8 = jnp.zeros((8, LANES), jnp.float32)
    at_last, at_first = lax.fori_loop(0, 32, pack, (zero8, zero8), unroll=4)
    elevation = elevation_ref[...]
    deep_send[0] = depth
    for side, edge, tile in ((0, at_last, 1), (1, at_first, 0)):
        cut = slice(tile * LANES, (tile + 1) * LANES)
        cols_send[side, 0:32, :] = depth[:, cut]
        cols_send[side, 32:64, :] = elevation[:, cut]
        cols_send[side, 64:72, :] = edge

    pl.semaphore_wait(barrier, beside_count)
    row_copies = [
        send(rows_send.at[0], rows_got.at[0], 0, 1),
        send(rows_send.at[1], rows_got.at[1], 0, -1),
    ]
    column_copies = [
        send(cols_send.at[0], cols_got.at[0], 1, 0),
        send(cols_send.at[1], cols_got.at[1], -1, 0),
    ]
    launch(column_copies + row_copies)

    def depth_sends(part):
        source = deep_send.at[part]
        return [
            send(source, deep_got.at[part, 0], 0, 1),
            send(source, deep_got.at[part, 1], 0, -1),
            send(source.at[pl.ds(ROWS - 8, 8)], deep_got_far.at[part, 0], 0, 2),
            send(source.at[pl.ds(0, 8)], deep_got_far.at[part, 1], 0, -2),
        ]

    depth_copies = depth_sends(0)
    launch(depth_copies)

    row_number = lax.broadcasted_iota(jnp.int32, (ROWS, LANES), 0)
    place = (lat * ROWS + row_number).astype(jnp.float32)
    angle = jnp.pi * ((place + 0.5) / (ROWS * lat_count) - 0.5)
    turning = CORIOLIS * jnp.sin(angle)
    rotation = jnp.concatenate([turning, turning], axis=1)

    row = lax.broadcasted_iota(jnp.int32, (ROWS, COLS), 0)
    column = lax.broadcasted_iota(jnp.int32, (ROWS, COLS), 1)
    on_east, on_west = column == COLS - 1, column == 0
    on_north, on_south = row == ROWS - 1, row == 0

    def beside(values, east_edge, west_edge, north_edge, south_edge):
        return (
            jnp.where(on_east, east_edge, pltpu.roll(values, COLS - 1, 1)),
            jnp.where(on_west, west_edge, pltpu.roll(values, 1, 1)),
            jnp.where(on_north, north_edge, pltpu.roll(values, ROWS - 1, 0)),
            jnp.where(on_south, south_edge, pltpu.roll(values, 1, 0)),
        )

    def laplace(faces, values, nearby):
        terms = [jnp.where(face, near - values, 0.0) for face, near in zip(faces, nearby)]
        return (terms[0] + terms[1]) + (terms[2] + terms[3])

    def momentum(faces, u, near_u, v, near_v):
        guess_u = u + TIME_STEP * (VISCOSITY * laplace(faces, u, near_u) + rotation * v)
        guess_v = v + TIME_STEP * (VISCOSITY * laplace(faces, v, near_v) - rotation * u)
        return guess_u, guess_v

    inner_depth = [jnp.minimum(depth, near) for near in beside(depth, 0.0, 0.0, 0.0, 0.0)]

    def inner(k, carry):
        sum_u, sum_v = carry
        level = k.astype(jnp.float32)
        faces = [level < limit for limit in inner_depth]
        rows = pl.ds(pl.multiple_of(k * ROWS, ROWS), ROWS)
        u, v = u_ref[rows, :], v_ref[rows, :]
        near_u, near_v = beside(u, 0.0, 0.0, 0.0, 0.0), beside(v, 0.0, 0.0, 0.0, 0.0)
        guess_u, guess_v = momentum(faces, u, near_u, v, near_v)
        wet = level < depth
        return sum_u + jnp.where(wet, guess_u, 0.0), sum_v + jnp.where(wet, guess_v, 0.0)

    zero = jnp.zeros((ROWS, COLS), jnp.float32)
    sum_u, sum_v = lax.fori_loop(0, LEVELS, inner, (zero, zero))
    gain = TIME_STEP * VISCOSITY / LEVELS

    for copy in row_copies:
        copy.wait_recv()
    north_depth = kept(1, rows_got[1, 24:25, :])
    south_depth = kept(-1, rows_got[0, 24:25, :])
    level8 = lax.broadcasted_iota(jnp.int32, (LEVELS, COLS), 0).astype(jnp.float32)

    def row_flux(f, side, limit):
        step = rows_got[side, 8 * f : 8 * f + 8, :] - rows_send[1 - side, 8 * f : 8 * f + 8, :]
        return gain * jnp.sum(jnp.where(level8 < limit, step, 0.0), axis=0, keepdims=True)

    north_limit = jnp.minimum(depth[ROWS - 1 : ROWS, :], north_depth)
    south_limit = jnp.minimum(depth[0:1, :], south_depth)

    def mean(f, total):
        return (
            total * (1.0 / LEVELS)
            + jnp.where(on_north, row_flux(f, 1, north_limit), 0.0)
            + jnp.where(on_south, row_flux(f, 0, south_limit), 0.0)
        )

    mean_u, mean_v = mean(0, sum_u), mean(1, sum_v)
    for side, tile in ((0, 1), (1, 0)):
        cut = slice(tile * LANES, (tile + 1) * LANES)
        mean_send[side, 0:32, :] = mean_u[:, cut]
        mean_send[side, 32:64, :] = mean_v[:, cut]
    mean_copies = [
        send(mean_send.at[0], mean_got.at[0], 1, 0),
        send(mean_send.at[1], mean_got.at[1], -1, 0),
    ]
    launch(mean_copies)

    def order(n):
        return ((((n & 127) + 32) & 127) << 2) + (n >> 7)

    wanted = order(lax.broadcasted_iota(jnp.int32, (1, WIDE), 1))

    def fill(i, carry):
        rows = pl.ds(pl.multiple_of(32 * i, 32), 32)
        k = lax.broadcasted_iota(jnp.int32, (32, WIDE), 0) + 32 * i
        choice[rows, :] = jnp.where(k == wanted, 1.0, 0.0).astype(jnp.bfloat16)
        n = lax.broadcasted_iota(jnp.int32, (32, COLS), 0) + 32 * i
        column = lax.broadcasted_iota(jnp.int32, (32, COLS), 1) + LANES
        unchoice[rows, :] = jnp.where(order(n) == column, 1.0, 0.0).astype(jnp.bfloat16)
        return carry

    lax.fori_loop(0, WIDE // 32, fill, 0)
    for ref in list(grid_p) + list(grid_q) + list(grid_b) + list(grid_wn) + [deep]:
        ref[...] = jnp.zeros_like(ref)
    for copy in column_copies:
        copy.wait_recv()

    west_tile, east_tile = cols_got.at[0], cols_got.at[1]
    deep_send[1, :, 0:LANES] = west_tile[0:32, :]
    deep_send[1, :, LANES:COLS] = east_tile[0:32, :]
    more_depth = depth_sends(1)
    launch(more_depth)
    depth_copies = depth_copies + more_depth

    lane_row = lane8 & 3
    lane_level = ((lane8 >> 2) & 7).astype(jnp.float32)

    def packed(values, column):
        result = zero8
        for g in range(4):
            result = jnp.where(lane_row == g, values[8 * g : 8 * g + 8, column : column + 1], result)
        return result

    def column_flux(own, other, own_depth, other_depth):
        limit = jnp.minimum(own_depth, other_depth)
        flux = jnp.where(lane_level < limit, other - own, 0.0)
        for turn in (4, 8, 16):
            flux = flux + pltpu.roll(flux, turn, 1)
        flux = gain * flux
        return [
            jnp.concatenate([flux[:, at + g : at + g + 1] for g in range(4)], axis=0)
            for at in (28, 60)
        ]

    east_flux = column_flux(
        cols_send[0, 64:72, :],
        east_tile[64:72, :],
        packed(depth, COLS - 1),
        packed(east_tile[0:32, :], 0),
    )
    west_flux = column_flux(
        cols_send[1, 64:72, :],
        west_tile[64:72, :],
        packed(depth, 0),
        packed(west_tile[0:32, :], LANES - 1),
    )

    depth_near = beside(
        depth,
        east_tile[0:32, 0:1],
        west_tile[0:32, LANES - 1 : LANES],
        north_depth,
        south_depth,
    )
    open_depth = [jnp.minimum(depth, near) for near in depth_near]
    east_edges = east_tile[64:72, :]
    west_edges = west_tile[64:72, :]

    def near_field(f, field, k):
        values = field[pl.ds(pl.multiple_of(k * ROWS, ROWS), ROWS), :]
        turn = lax.rem(2 * LANES - 32 * f - 4 * k, LANES)
        east_lanes = pltpu.roll(east_edges, turn, 1)
        west_lanes = pltpu.roll(west_edges, turn, 1)
        east_edge = jnp.concatenate([east_lanes[:, g : g + 1] for g in range(4)], axis=0)
        west_edge = jnp.concatenate([west_lanes[:, g : g + 1] for g in range(4)], axis=0)
        north_edge = kept(1, rows_got[1, pl.ds(8 * f + k, 1), :])
        south_edge = kept(-1, rows_got[0, pl.ds(8 * f + k, 1), :])
        return values, beside(values, east_edge, west_edge, north_edge, south_edge)

    def layer(k, carry):
        level = k.astype(jnp.float32)
        faces = [level < limit for limit in open_depth]
        t, near_t = near_field(2, t_ref, k)
        u, near_u = near_field(0, u_ref, k)
        v, near_v = near_field(1, v_ref, k)
        spread = laplace(faces, t, near_t)
        east = jnp.where(faces[0], (u + near_u[0]) * 0.5, 0.0)
        west = jnp.where(faces[1], (near_u[1] + u) * 0.5, 0.0)
        north = jnp.where(faces[2], (v + near_v[2]) * 0.5, 0.0)
        south = jnp.where(faces[3], (near_v[3] + v) * 0.5, 0.0)
        transport = (east * (t + near_t[0]) - west * (near_t[1] + t)) + (
            north * (t + near_t[2]) - south * (near_t[3] + t)
        )
        result = t + TIME_STEP * (DIFFUSIVITY * spread - 0.5 * transport)
        guess_u, guess_v = momentum(faces, u, near_u, v, near_v)
        wet = level < depth
        rows = pl.ds(pl.multiple_of(k * ROWS, ROWS), ROWS)
        u_star[rows, :] = jnp.where(wet, guess_u, 0.0)
        v_star[rows, :] = jnp.where(wet, guess_v, 0.0)
        t_out[rows, :] = jnp.where(wet, result, 0.0)
        return carry

    lax.fori_loop(0, EARLY_LEVELS, layer, 0)

    for copy in mean_copies:
        copy.wait_recv()
    west_mean, east_mean = mean_got.at[0], mean_got.at[1]
    tile_lane = lax.broadcasted_iota(jnp.int32, (ROWS, LANES), 1)
    tile_first, tile_last = tile_lane == 0, tile_lane == LANES - 1

    def window(f, values):
        cut = slice(32 * f, 32 * f + 32)
        return jnp.concatenate(
            [
                west_mean[cut, :] - jnp.where(tile_last, west_flux[f], 0.0),
                values[:, 0:LANES] + jnp.where(tile_first, west_flux[f], 0.0),
                values[:, LANES:COLS] + jnp.where(tile_last, east_flux[f], 0.0),
                east_mean[cut, :] - jnp.where(tile_first, east_flux[f], 0.0),
            ],
            axis=1,
        )

    wide_u, wide_v = window(0, mean_u), window(1, mean_v)
    wide_eta = jnp.concatenate([west_tile[32:64, :], elevation, east_tile[32:64, :]], axis=1)
    wide_row = lax.broadcasted_iota(jnp.int32, (ROWS, WIDE), 0)
    north_v = jnp.where(wide_row == ROWS - 1, 0.0, pltpu.roll(wide_v, ROWS - 1, 0))
    south_v = jnp.where(wide_row == 0, 0.0, pltpu.roll(wide_v, 1, 0))
    across = pltpu.roll(wide_u, WIDE - 1, 1) - pltpu.roll(wide_u, 1, 1)
    depth_wide = jnp.concatenate([west_tile[0:32, :], depth, east_tile[0:32, :]], axis=1)
    source = jnp.where(
        depth_wide > 0.5, wide_eta - 0.5 * (across + (north_v - south_v)), 0.0
    )
    ends = jnp.where(
        lax.broadcasted_iota(jnp.int32, (16, WIDE), 0) == 0, wide_v[0:1, :], wide_v[31:32, :]
    )
    by_class = exact_select(jnp.concatenate([source, ends], axis=0), choice[...])
    for c in range(4):
        cut = slice(LANES * c, LANES * (c + 1))
        source_send[c] = by_class[0:32, cut]
        ends_send[c : c + 1, :] = by_class[32:33, cut]
        ends_send[4 + c : 5 + c, :] = by_class[33:34, cut]
    source_copies = [
        send(ends_send, ends_got.at[i], 0, move) for i, move in enumerate(LAT_MOVES)
    ] + [
        send(source_send.at[:, pl.ds(24, 8)], source_got.at[0, :, pl.ds(24, 8)], 0, 1),
        send(source_send.at[:, pl.ds(0, 8)], source_got.at[1, :, pl.ds(0, 8)], 0, -1),
    ]
    far_copies = [
        send(source_send.at[:, pl.ds(0, 24)], source_got.at[0, :, pl.ds(0, 24)], 0, 1),
        send(source_send.at[:, pl.ds(8, 24)], source_got.at[1, :, pl.ds(8, 24)], 0, -1),
        send(source_send.at[:, pl.ds(ROWS - 8, 8)], source_got_far.at[0], 0, 2),
        send(source_send.at[:, pl.ds(0, 8)], source_got_far.at[1], 0, -2),
    ]
    launch(source_copies + far_copies)

    for copy in depth_copies:
        copy.wait_recv()

    def slot_of(lat_move):
        return LAT_MOVES.index(-lat_move)

    def wide_depth(own, halo, move):
        return kept(move, jnp.concatenate([halo[:, 0:LANES], own, halo[:, LANES:COLS]], axis=1))

    blocks = [
        wide_depth(deep_got_far[0, 0], deep_got_far[1, 0], -2),
        wide_depth(deep_got[0, 0], deep_got[1, 0], -1),
        wide_depth(deep_send[0], deep_send[1], 0),
        wide_depth(deep_got[0, 1], deep_got[1, 1], 1),
        wide_depth(deep_got_far[0, 1], deep_got_far[1, 1], 2),
    ]
    by_class = jnp.dot(
        jnp.concatenate(blocks, axis=0).astype(jnp.bfloat16),
        choice[...],
        preferred_element_type=jnp.float32,
    )
    for c in range(4):
        deep[c, pl.ds(ORIGIN[0] - 40, 112), :] = by_class[:, LANES * c : LANES * (c + 1)]

    def finish_weights(g, rows):
        we = [grid_we[g][c, rows, :] for c in range(CLASSES[g])]
        ww = west_of(we, STEP[g])
        grid_ww[g][rows, :] = ww[0]
        before = pl.ds(rows.start - 1, 8)
        for c in range(CLASSES[g]):
            near = (we[c] + ww[c]) + (grid_wn[g][c, rows, :] + grid_wn[g][c, before, :])
            grid_dg[g][c, rows, :] = MASS[g] + near
            grid_iv[g][c, rows, :] = 1.0 / (MASS[g] + 2.0 * near)

    def fine_weights(at):
        rows, after = pl.ds(at, 8), pl.ds(at + 1, 8)
        columns = [deep[c, rows, :] * (1.0 / LEVELS) for c in range(4)]
        for c, near in enumerate(east_of(columns, 1)):
            grid_we[0][c, rows, :] = jnp.minimum(columns[c], near)
            north = deep[c, after, :] * (1.0 / LEVELS)
            grid_wn[0][c, rows, :] = jnp.minimum(columns[c], north)

    def whole(g):
        return tuple(ORIGIN[g] + end for end in ((-40, 72), (-24, 40), (-16, 24), (0, 8))[g])

    def pair_lanes(values):
        even = (lax.broadcasted_iota(jnp.int32, values.shape, 1) & 1) == 0
        return even, pltpu.roll(values, LANES - 1, 1), pltpu.roll(values, 1, 1)

    def finer_rows(g, at):
        return 2 * (at - ORIGIN[g]) + ORIGIN[g - 1]

    each_chunk(*whole(0), fine_weights)
    each_chunk(*whole(0), lambda at: finish_weights(0, pl.ds(at, 8)))
    for g in (1, 2, 3):

        def coarse_weights(at, g=g):
            rows = pl.ds(at, 8)
            above = finer_rows(g, at)
            even_rows, odd_rows = pl.ds(above, 8, stride=2), pl.ds(above + 1, 8, stride=2)
            finer_we, finer_wn = grid_we[g - 1], grid_wn[g - 1]
            if g < 3:
                for c in range(CLASSES[g]):
                    grid_we[g][c, rows, :] = (
                        finer_we[2 * c + 1, even_rows, :] + finer_we[2 * c + 1, odd_rows, :]
                    )
                    grid_wn[g][c, rows, :] = (
                        finer_wn[2 * c, odd_rows, :] + finer_wn[2 * c + 1, odd_rows, :]
                    )
            else:
                we = finer_we[0, even_rows, :] + finer_we[0, odd_rows, :]
                even, east, west = pair_lanes(we)
                grid_we[g][0, rows, :] = jnp.where(even, east, we)
                wn = finer_wn[0, odd_rows, :]
                even, east, west = pair_lanes(wn)
                grid_wn[g][0, rows, :] = wn + jnp.where(even, east, west)

        each_chunk(*whole(g), coarse_weights)
        if g < 3:
            each_chunk(*whole(g), lambda at, g=g: finish_weights(g, pl.ds(at, 8)))

    upper = lax.broadcasted_iota(jnp.int32, (8, LANES), 0) >= 4

    def around(held, own, got, moves):
        def block(move):
            return kept(move, got[moves.index(-move)][...])

        held[0, pl.ds(ORIGIN[3], 8), :] = jnp.where(upper, pltpu.roll(block(1), 4, 0), own)
        lower = pltpu.roll(block(-1), 4, 0)
        if len(moves) == 4:
            lower = jnp.where(upper, lower, block(-2))
            held[0, pl.ds(ORIGIN[3] + 8, 8), :] = block(2)
        held[0, pl.ds(ORIGIN[3] - 8, 8), :] = lower

    weight_send[0:8, :] = grid_we[3][0, pl.ds(ORIGIN[3], 8), :]
    weight_send[8:16, :] = grid_wn[3][0, pl.ds(ORIGIN[3], 8), :]
    weight_copies = [
        send(weight_send, weight_got.at[i], 0, move) for i, move in enumerate(LAT_MOVES)
    ]
    launch(weight_copies)

    lax.fori_loop(EARLY_LEVELS, LEVELS, layer, 0)
    for copy in source_copies:
        copy.wait_recv()

    rows32 = lax.broadcasted_iota(jnp.int32, (ROWS, LANES), 0)

    def ends(move, spot):
        held = ends_send if move == 0 else ends_got.at[slot_of(move)]
        return 0.5 * kept(move, held[spot : spot + 1, :])

    def place_source(move, low, high, held):
        at = rows32[: high - low] + low
        for c in range(4):
            rows = pl.ds(ORIGIN[0] + 32 * move + low, high - low)
            values = held[c]
            if move < 2 and high == ROWS:
                values = values - jnp.where(at == ROWS - 1, ends(move + 1, c), 0.0)
            if move > -2 and low == 0:
                values = values + jnp.where(at == 0, ends(move - 1, 4 + c), 0.0)
            grid_b[0][c, rows, :] = jnp.where(deep[c, rows, :] > 0.5, values, 0.0)

    place_source(-1, 24, 32, source_got.at[0, :, pl.ds(24, 8)])
    place_source(0, 0, 32, source_send)
    place_source(1, 0, 8, source_got.at[1, :, pl.ds(0, 8)])

    def place_far_source():
        for copy in far_copies:
            copy.wait_recv()
        place_source(-2, 24, 32, source_got_far.at[0])
        place_source(-1, 0, 24, source_got.at[0, :, pl.ds(0, 24)])
        place_source(1, 8, 32, source_got.at[1, :, pl.ds(8, 24)])
        place_source(2, 0, 8, source_got_far.at[1])

    def operator(g, held, at):
        rows, after, before = pl.ds(at, 8), pl.ds(at + 1, 8), pl.ds(at - 1, 8)
        count = CLASSES[g]
        p = [held[c, rows, :] for c in range(count)]
        we = [grid_we[g][c, rows, :] for c in range(count)]
        ww = [grid_ww[g][rows, :]] + we[:-1]
        pe, pw = east_of(p, STEP[g]), west_of(p, STEP[g])
        residual = []
        for c in range(count):
            pull = (we[c] * pe[c] + ww[c] * pw[c]) + (
                grid_wn[g][c, rows, :] * held[c, after, :]
                + grid_wn[g][c, before, :] * held[c, before, :]
            )
            image = grid_dg[g][c, rows, :] * p[c] - pull
            residual.append(grid_b[g][c, rows, :] - image)
        return p, residual

    def span(g, low, high):
        return ORIGIN[g] + low, ORIGIN[g] + high

    def from_zero(g, low, high, held):
        def body(at):
            rows = pl.ds(at, 8)
            for c in range(CLASSES[g]):
                held[c, rows, :] = grid_b[g][c, rows, :] * grid_iv[g][c, rows, :]

        each_chunk(*span(g, low, high), body)

    def sweep(g, low, high, held, result):
        def body(at):
            rows = pl.ds(at, 8)
            p, residual = operator(g, held, at)
            for c in range(CLASSES[g]):
                result[c, rows, :] = p[c] + residual[c] * grid_iv[g][c, rows, :]

        each_chunk(*span(g, low, high), body)

    def restricted(g, low, high, held):
        def residual_rows(at):
            rows = pl.ds(at, 8)
            _, residual = operator(g, held, at)
            if g < 2:
                for c in range(CLASSES[g] // 2):
                    grid_r[g][c, rows, :] = residual[2 * c] + residual[2 * c + 1]
            else:
                even, east, west = pair_lanes(residual[0])
                grid_r[g][0, rows, :] = residual[0] + jnp.where(even, east, west)

        each_chunk(*span(g, low, high), residual_rows)

        def pair_rows(at):
            above = finer_rows(g + 1, at)
            for c in range(CLASSES[g + 1]):
                grid_b[g + 1][c, pl.ds(at, 8), :] = (
                    grid_r[g][c, pl.ds(above, 8, stride=2), :]
                    + grid_r[g][c, pl.ds(above + 1, 8, stride=2), :]
                )

        top = (high // 2 + 7) // 8 * 8
        each_chunk(*span(g + 1, low // 2 // 8 * 8, top), pair_rows)

    def corrected(g, low, high, held, correction):
        first, last = low // 2 // 8 * 8, (high // 2 + 7) // 8 * 8

        def body(at):
            above = finer_rows(g + 1, at)
            for c in range(CLASSES[g]):
                change = correction[c // 2, pl.ds(at, 8), :]
                for odd in (0, 1):
                    rows = pl.ds(above + odd, 8, stride=2)
                    held[c, rows, :] = held[c, rows, :] + change

        each_chunk(*span(g + 1, first, last), body)

    def coarse_links(cycle, reach):
        coarse_send[cycle] = grid_b[3][0, pl.ds(ORIGIN[3], 8), :]
        moves = LAT_MOVES[: 2 * reach]
        copies = [
            send(coarse_send.at[cycle], coarse_got.at[4 * cycle + i], 0, move)
            for i, move in enumerate(moves)
        ]
        launch(copies)
        return copies, moves

    def coarse_weights_around():
        for copy in weight_copies:
            copy.wait_recv()
        for held, first in ((grid_we[3], 0), (grid_wn[3], 8)):
            cut = pl.ds(first, 8)
            around(held, weight_send[cut, :], [weight_got.at[i, cut] for i in range(4)], LAT_MOVES)
        each_chunk(ORIGIN[3] - 8, ORIGIN[3] + 16, lambda at: finish_weights(3, pl.ds(at, 8)))

    def coarse_source(cycle, copies, moves):
        for copy in copies:
            copy.wait_recv()
        got = [coarse_got.at[4 * cycle + i] for i in range(len(moves))]
        around(grid_b[3], coarse_send[cycle], got, moves)

    plans = (
        ((-40, 72), (-24, 40), (-16, 24), (-8, 16), (-16, 32), (-24, 56)),
        ((-24, 56), (-16, 32), (-8, 16), (-8, 16), (-8, 24), (-16, 48)),
        ((-16, 48), (-8, 24), (-8, 16), (-8, 16), (-8, 24), (-8, 40)),
    )
    for cycle in range(CYCLES):
        before0, down1, down2, up2, up1, after0 = plans[cycle]

        def first_leg(before0, down1, down2, cycle=cycle):
            if cycle == 0:
                from_zero(0, *before0, grid_q[0])
            else:
                sweep(0, *before0, grid_p[0], grid_q[0])
            restricted(0, *before0, grid_q[0])
            from_zero(1, *down1, grid_q[1])
            restricted(1, *down1, grid_q[1])
            from_zero(2, *down2, grid_q[2])

        if cycle == 0:
            first_leg((-8, 40), (-8, 24), (-8, 16))
        else:
            first_leg(before0, down1, down2)
        restricted(2, -8, 16, grid_q[2])
        links = coarse_links(cycle, 1 if cycle == 2 else 2)
        if cycle == 0:
            place_far_source()
            first_leg(before0, down1, down2)
            coarse_weights_around()
        coarse_source(cycle, *links)
        from_zero(3, -8, 16, grid_q[3])
        here, there_ = grid_q[3], grid_p[3]
        for _ in range(SWEEPS - 1):
            sweep(3, -8, 16, here, there_)
            here, there_ = there_, here
        corrected(2, *up2, grid_q[2], here)
        sweep(2, *up2, grid_q[2], grid_p[2])
        corrected(1, *up1, grid_q[1], grid_p[2])
        sweep(1, *up1, grid_q[1], grid_p[1])
        corrected(0, *after0, grid_q[0], grid_p[1])
        sweep(0, *after0, grid_q[0], grid_p[0])

    pressure = grid_p[0]
    own = pl.ds(ORIGIN[0], ROWS)
    p = [pressure[c, own, :] for c in range(4)]
    slope_east = [0.5 * (e - w) for e, w in zip(east_of(p, 1), west_of(p, 1))]
    slope_north = [
        0.5 * (pressure[c, pl.ds(ORIGIN[0] + 1, ROWS), :] - pressure[c, pl.ds(ORIGIN[0] - 1, ROWS), :])
        for c in range(4)
    ]
    stacked = jnp.concatenate(
        [jnp.concatenate(parts, axis=1) for parts in (p, slope_east, slope_north)], axis=0
    )
    ordered = exact_select(stacked, unchoice[...])
    p_out[...] = ordered[0:32]
    push_u = GRAVITY_STEP * ordered[32:64]
    push_v = GRAVITY_STEP * ordered[64:96]
    for k in range(LEVELS):
        rows = slice(k * ROWS, (k + 1) * ROWS)
        wet = depth > k
        u_out[rows, :] = jnp.where(wet, u_star[rows, :] - push_u, 0.0)
        v_out[rows, :] = jnp.where(wet, v_star[rows, :] - push_v, 0.0)
    for copy in started:
        copy.wait_send()


def deliver(*refs):
    held, outs, sem = refs[:4], refs[4:8], refs[8]
    copies = [pltpu.make_async_copy(held[i], outs[i], sem.at[i]) for i in range(4)]
    for copy in copies:
        copy.start()
    for copy in copies:
        copy.wait()


def shards(lon_count, lat_count, u, v, t, depth, elevation):
    f32 = jnp.float32
    flat = (LEVELS * ROWS, COLS)
    block = pl.BlockSpec(memory_space=pltpu.VMEM)

    def grids(classes=CLASSES):
        return [pltpu.VMEM((c, h, LANES), f32) for c, h in zip(classes, HEIGHT)]

    shapes = [flat] * 3 + [(ROWS, COLS)]
    anywhere = pl.BlockSpec(memory_space=pl.ANY)
    held = pl.pallas_call(
        functools.partial(kernel, lon_count, lat_count),
        out_shape=[pltpu.VMEM(shape, f32) for shape in shapes],
        in_specs=[anywhere] * 5,
        out_specs=[block] * 4,
        scratch_shapes=[
            pltpu.VMEM(flat, f32),
            pltpu.VMEM(flat, f32),
            pltpu.VMEM(flat, f32),
            pltpu.VMEM((ROWS, COLS), jnp.int32),
            pltpu.VMEM((ROWS, COLS), f32),
            pltpu.VMEM(flat, f32),
            pltpu.VMEM(flat, f32),
            pltpu.VMEM((2, 32, COLS), f32),
            pltpu.VMEM((2, 32, COLS), f32),
            pltpu.VMEM((2, 72, LANES), f32),
            pltpu.VMEM((2, 72, LANES), f32),
            pltpu.VMEM((2, 64, LANES), f32),
            pltpu.VMEM((2, 64, LANES), f32),
            pltpu.VMEM((2, ROWS, COLS), f32),
            pltpu.VMEM((2, 2, ROWS, COLS), f32),
            pltpu.VMEM((2, 2, 8, COLS), f32),
            pltpu.VMEM((4, ROWS, LANES), f32),
            pltpu.VMEM((2, 4, ROWS, LANES), f32),
            pltpu.VMEM((2, 4, 8, LANES), f32),
            pltpu.VMEM((8, LANES), f32),
            pltpu.VMEM((4, 8, LANES), f32),
            pltpu.VMEM((16, LANES), f32),
            pltpu.VMEM((4, 16, LANES), f32),
            pltpu.VMEM((CYCLES, 8, LANES), f32),
            pltpu.VMEM((10, 8, LANES), f32),
            pltpu.VMEM((WIDE, WIDE), jnp.bfloat16),
            pltpu.VMEM((WIDE, COLS), jnp.bfloat16),
            pltpu.VMEM((4, HEIGHT[0], LANES), f32),
            grids(),
            grids(),
            grids(),
            grids(),
            [pltpu.VMEM((h, LANES), f32) for h in HEIGHT],
            grids(),
            grids(),
            grids(),
            grids(),
            pltpu.SemaphoreType.DMA((5,)),
            pltpu.SemaphoreType.DMA((40,)),
            pltpu.SemaphoreType.DMA((40,)),
        ],
        compiler_params=pltpu.CompilerParams(
            collective_id=0, has_side_effects=True, vmem_limit_bytes=32 << 20
        ),
    )(
        *[
            pltpu.with_memory_space_constraint(x, pltpu.HBM)
            for x in (u.reshape(flat), v.reshape(flat), t.reshape(flat), depth, elevation)
        ]
    )
    outs = pl.pallas_call(
        deliver,
        out_shape=[jax.ShapeDtypeStruct(shape, f32) for shape in shapes],
        in_specs=[block] * 4,
        out_specs=[anywhere] * 4,
        scratch_shapes=[pltpu.SemaphoreType.DMA((4,))],
    )(*[pltpu.with_memory_space_constraint(x, pltpu.VMEM) for x in held])
    shape = (LEVELS, ROWS, COLS)
    return outs[0].reshape(shape), outs[1].reshape(shape), outs[2].reshape(shape), outs[3]


def solution(mesh):
    spec3, spec2 = P(None, "lat", "lon"), P("lat", "lon")
    return jax.shard_map(
        functools.partial(shards, mesh.shape["lon"], mesh.shape["lat"]),
        mesh=mesh,
        in_specs=(spec3, spec3, spec3, spec2, spec2),
        out_specs=(spec3, spec3, spec3, spec2),
        check_vma=False,
    )
```

```python
import functools

import jax
import jax.numpy as jnp
from jax import lax
from jax.experimental import pallas as pl
from jax.experimental.pallas import tpu as pltpu
from jax.sharding import PartitionSpec as P

LEVELS = 8
CYCLES = 3
SWEEPS = 4
TIME_STEP = 0.2
VISCOSITY = 1.0
DIFFUSIVITY = 1.0
CORIOLIS = 1.0
MASS_TERM = 0.05
GRAVITY_STEP = 0.5

ROWS = 32
COLS = 256
LANES = 128
WIDE = 512
MESH_IDS = pl.DeviceIdType.MESH

CLASSES = (4, 2, 1, 1)
STEP = (1, 1, 1, 2)
ORIGIN = (48, 32, 24, 16)
HEIGHT = (128, 80, 56, 40)
MASS = tuple(MASS_TERM * 4.0**g for g in range(4))

LAT_MOVES = (1, -1, 2, -2)
EARLY_LEVELS = 5


def east_of(parts, step):
    turned = pltpu.roll(parts[0], LANES - step, 1)
    return list(parts[1:]) + [turned]


def west_of(parts, step):
    turned = pltpu.roll(parts[-1], step, 1)
    return [turned] + list(parts[:-1])


def each_chunk(first, last, body, unroll=5):
    count = (last - first) // 8
    if count <= unroll:
        for i in range(count):
            body(first + 8 * i)
        return
    while count % unroll:
        unroll -= 1

    def step(i, carry):
        for j in range(unroll):
            body(pl.multiple_of(first + (i * unroll + j) * 8, 8))
        return carry

    lax.fori_loop(0, count // unroll, step, 0)


def split_three(values):
    high = values.astype(jnp.bfloat16)
    rest = values - high.astype(jnp.float32)
    middle = rest.astype(jnp.bfloat16)
    low = (rest - middle.astype(jnp.float32)).astype(jnp.bfloat16)
    return jnp.concatenate([high, middle, low], axis=0)


def exact_select(values, choice):
    count = values.shape[0]
    product = jnp.dot(split_three(values), choice, preferred_element_type=jnp.float32)
    return (product[:count] + product[count : 2 * count]) + product[2 * count :]


class Link:
    def __init__(self, copy, leaves, comes):
        self.copy, self.leaves, self.comes = copy, leaves, comes

    def start(self):
        if self.leaves is None:
            self.copy.start()
        else:
            pl.when(self.leaves)(self.copy.start)

    def wait_send(self):
        if self.leaves is None:
            self.copy.wait_send()
        else:
            pl.when(self.leaves)(self.copy.wait_send)

    def wait_recv(self):
        if self.comes is None:
            self.copy.wait_recv()
        else:
            pl.when(self.comes)(self.copy.wait_recv)


def kernel(
    lon_count,
    lat_count,
    u_far,
    v_far,
    t_far,
    depth_far,
    elevation_far,
    u_out,
    v_out,
    t_out,
    p_out,
    u_ref,
    v_ref,
    t_ref,
    depth_ref,
    elevation_ref,
    u_star,
    v_star,
    rows_send,
    rows_got,
    cols_send,
    cols_got,
    mean_send,
    mean_got,
    deep_send,
    deep_got,
    deep_got_far,
    source_send,
    source_got,
    source_got_far,
    close_send,
    close_got,
    weight_send,
    weight_got,
    coarse_send,
    coarse_got,
    choice,
    unchoice,
    deep,
    grid_b,
    grid_p,
    grid_q,
    grid_we,
    grid_ww,
    grid_wn,
    grid_dg,
    grid_iv,
    grid_r,
    grid_s,
    load_sem,
    send_sem,
    recv_sem,
):
    lon = lax.axis_index("lon")
    lat = lax.axis_index("lat")
    sems = iter(range(64))

    def there(lon_move, lat_move):
        return {
            "lon": lax.rem(lon + lon_move + lon_count, lon_count),
            "lat": lax.rem(lat + lat_move + lat_count, lat_count),
        }

    def send(source, target, lon_move, lat_move):
        at = next(sems)
        copy = pltpu.make_async_remote_copy(
            src_ref=source,
            dst_ref=target,
            send_sem=send_sem.at[at],
            recv_sem=recv_sem.at[at],
            device_id=there(lon_move, lat_move),
            device_id_type=MESH_IDS,
        )
        if lat_move == 0:
            return Link(copy, None, None)
        return Link(copy, inside(lat_move), inside(-lat_move))

    def inside(lat_move):
        return (lat + lat_move >= 0) & (lat + lat_move < lat_count)

    def kept(lat_move, values):
        if lat_move == 0:
            return values
        return jnp.where(inside(lat_move), values, jnp.zeros_like(values))

    started = []

    def launch(copies):
        for copy in copies:
            copy.start()
        started.extend(copies)

    barrier = pltpu.get_barrier_semaphore()
    for lon_move in (1, -1):
        pl.semaphore_signal(
            barrier, inc=1, device_id=there(lon_move, 0), device_id_type=MESH_IDS
        )
    beside_count = jnp.int32(2)
    for lat_move in LAT_MOVES:
        beside_count = beside_count + inside(lat_move).astype(jnp.int32)

        @pl.when(inside(lat_move))
        def _(lat_move=lat_move):
            pl.semaphore_signal(
                barrier, inc=1, device_id=there(0, lat_move), device_id_type=MESH_IDS
            )


    loads = [
        pltpu.make_async_copy(far, near, load_sem.at[i])
        for i, (far, near) in enumerate(
            (
                (depth_far, depth_ref),
                (elevation_far, elevation_ref),
                (u_far, u_ref),
                (v_far, v_ref),
                (t_far, t_ref),
            )
        )
    ]
    for load in loads:
        load.start()
    for load in loads:
        load.wait()

    depth = depth_ref[...].astype(jnp.float32)
    lane8 = lax.broadcasted_iota(jnp.int32, (8, LANES), 1)
    fields = (u_ref, v_ref, t_ref)
    for side, row in ((0, ROWS - 1), (1, 0)):
        for f, field in enumerate(fields):
            for k in range(LEVELS):
                rows_send[side, 8 * f + k : 8 * f + k + 1, :] = field[
                    k * ROWS + row : k * ROWS + row + 1, :
                ]
        rows_send[side, pl.ds(24, 8), :] = jnp.broadcast_to(depth[row : row + 1, :], (8, COLS))

    def pack(i, carry):
        at_last, at_first = carry
        rows = pl.ds(pl.multiple_of(8 * i, 8), 8)
        for f, field in enumerate(fields):
            here = lane8 == i + 32 * f
            at_last = jnp.where(here, field[rows, COLS - 1 : COLS], at_last)
            at_first = jnp.where(here, field[rows, 0:1], at_first)
        return at_last, at_first

    zero8 = jnp.zeros((8, LANES), jnp.float32)
    at_last, at_first = lax.fori_loop(0, 32, pack, (zero8, zero8), unroll=4)
    elevation = elevation_ref[...]
    deep_send[0] = depth
    for side, edge, tile in ((0, at_last, 1), (1, at_first, 0)):
        cut = slice(tile * LANES, (tile + 1) * LANES)
        cols_send[side, 0:32, :] = depth[:, cut]
        cols_send[side, 32:64, :] = elevation[:, cut]
        cols_send[side, 64:72, :] = edge

    pl.semaphore_wait(barrier, beside_count)
    row_copies = [
        send(rows_send.at[0], rows_got.at[0], 0, 1),
        send(rows_send.at[1], rows_got.at[1], 0, -1),
    ]
    column_copies = [
        send(cols_send.at[0], cols_got.at[0], 1, 0),
        send(cols_send.at[1], cols_got.at[1], -1, 0),
    ]
    launch(column_copies + row_copies)

    def depth_sends(part):
        source = deep_send.at[part]
        return [
            send(source, deep_got.at[part, 0], 0, 1),
            send(source, deep_got.at[part, 1], 0, -1),
            send(source.at[pl.ds(ROWS - 8, 8)], deep_got_far.at[part, 0], 0, 2),
            send(source.at[pl.ds(0, 8)], deep_got_far.at[part, 1], 0, -2),
        ]

    depth_copies = depth_sends(0)
    launch(depth_copies)

    row_number = lax.broadcasted_iota(jnp.int32, (ROWS, LANES), 0)
    place = (lat * ROWS + row_number).astype(jnp.float32)
    angle = jnp.pi * ((place + 0.5) / (ROWS * lat_count) - 0.5)
    turning = CORIOLIS * jnp.sin(angle)
    rotation = jnp.concatenate([turning, turning], axis=1)

    row = lax.broadcasted_iota(jnp.int32, (ROWS, COLS), 0)
    column = lax.broadcasted_iota(jnp.int32, (ROWS, COLS), 1)
    on_east, on_west = column == COLS - 1, column == 0
    on_north, on_south = row == ROWS - 1, row == 0

    def beside(values, east_edge, west_edge, north_edge, south_edge):
        return (
            jnp.where(on_east, east_edge, pltpu.roll(values, COLS - 1, 1)),
            jnp.where(on_west, west_edge, pltpu.roll(values, 1, 1)),
            jnp.where(on_north, north_edge, pltpu.roll(values, ROWS - 1, 0)),
            jnp.where(on_south, south_edge, pltpu.roll(values, 1, 0)),
        )

    def laplace(faces, values, nearby):
        terms = [jnp.where(face, near - values, 0.0) for face, near in zip(faces, nearby)]
        return (terms[0] + terms[1]) + (terms[2] + terms[3])

    def momentum(faces, u, near_u, v, near_v):
        guess_u = u + TIME_STEP * (VISCOSITY * laplace(faces, u, near_u) + rotation * v)
        guess_v = v + TIME_STEP * (VISCOSITY * laplace(faces, v, near_v) - rotation * u)
        return guess_u, guess_v

    inner_depth = [jnp.minimum(depth, near) for near in beside(depth, 0.0, 0.0, 0.0, 0.0)]

    def inner(k, carry):
        sum_u, sum_v = carry
        level = k.astype(jnp.float32)
        faces = [level < limit for limit in inner_depth]
        rows = pl.ds(pl.multiple_of(k * ROWS, ROWS), ROWS)
        u, v = u_ref[rows, :], v_ref[rows, :]
        near_u, near_v = beside(u, 0.0, 0.0, 0.0, 0.0), beside(v, 0.0, 0.0, 0.0, 0.0)
        guess_u, guess_v = momentum(faces, u, near_u, v, near_v)
        wet = level < depth
        return sum_u + jnp.where(wet, guess_u, 0.0), sum_v + jnp.where(wet, guess_v, 0.0)

    zero = jnp.zeros((ROWS, COLS), jnp.float32)
    sum_u, sum_v = lax.fori_loop(0, LEVELS, inner, (zero, zero))
    gain = TIME_STEP * VISCOSITY / LEVELS

    for copy in row_copies:
        copy.wait_recv()
    north_depth = kept(1, rows_got[1, 24:25, :])
    south_depth = kept(-1, rows_got[0, 24:25, :])
    level8 = lax.broadcasted_iota(jnp.int32, (LEVELS, COLS), 0).astype(jnp.float32)

    def row_flux(f, side, limit):
        step = rows_got[side, 8 * f : 8 * f + 8, :] - rows_send[1 - side, 8 * f : 8 * f + 8, :]
        return gain * jnp.sum(jnp.where(level8 < limit, step, 0.0), axis=0, keepdims=True)

    north_limit = jnp.minimum(depth[ROWS - 1 : ROWS, :], north_depth)
    south_limit = jnp.minimum(depth[0:1, :], south_depth)

    def mean(f, total):
        return (
            total * (1.0 / LEVELS)
            + jnp.where(on_north, row_flux(f, 1, north_limit), 0.0)
            + jnp.where(on_south, row_flux(f, 0, south_limit), 0.0)
        )

    mean_u, mean_v = mean(0, sum_u), mean(1, sum_v)
    for side, tile in ((0, 1), (1, 0)):
        cut = slice(tile * LANES, (tile + 1) * LANES)
        mean_send[side, 0:32, :] = mean_u[:, cut]
        mean_send[side, 32:64, :] = mean_v[:, cut]
    mean_copies = [
        send(mean_send.at[0], mean_got.at[0], 1, 0),
        send(mean_send.at[1], mean_got.at[1], -1, 0),
    ]
    launch(mean_copies)

    def order(n):
        return ((((n & 127) + 32) & 127) << 2) + (n >> 7)

    wanted = order(lax.broadcasted_iota(jnp.int32, (1, WIDE), 1))

    def fill(i, carry):
        rows = pl.ds(pl.multiple_of(32 * i, 32), 32)
        k = lax.broadcasted_iota(jnp.int32, (32, WIDE), 0) + 32 * i
        choice[rows, :] = jnp.where(k == wanted, 1.0, 0.0).astype(jnp.bfloat16)
        n = lax.broadcasted_iota(jnp.int32, (32, COLS), 0) + 32 * i
        column = lax.broadcasted_iota(jnp.int32, (32, COLS), 1) + LANES
        unchoice[rows, :] = jnp.where(order(n) == column, 1.0, 0.0).astype(jnp.bfloat16)
        return carry

    lax.fori_loop(0, WIDE // 32, fill, 0)
    for ref in list(grid_p) + list(grid_q) + list(grid_b) + list(grid_wn) + [deep, grid_s]:
        ref[...] = jnp.zeros_like(ref)
    for copy in column_copies:
        copy.wait_recv()

    west_tile, east_tile = cols_got.at[0], cols_got.at[1]
    deep_send[1, :, 0:LANES] = west_tile[0:32, :]
    deep_send[1, :, LANES:COLS] = east_tile[0:32, :]
    more_depth = depth_sends(1)
    launch(more_depth)
    depth_copies = depth_copies + more_depth

    lane_row = lane8 & 3
    lane_level = ((lane8 >> 2) & 7).astype(jnp.float32)

    def packed(values, column):
        result = zero8
        for g in range(4):
            result = jnp.where(lane_row == g, values[8 * g : 8 * g + 8, column : column + 1], result)
        return result

    def column_flux(own, other, own_depth, other_depth):
        limit = jnp.minimum(own_depth, other_depth)
        flux = jnp.where(lane_level < limit, other - own, 0.0)
        for turn in (4, 8, 16):
            flux = flux + pltpu.roll(flux, turn, 1)
        flux = gain * flux
        return [
            jnp.concatenate([flux[:, at + g : at + g + 1] for g in range(4)], axis=0)
            for at in (28, 60)
        ]

    east_flux = column_flux(
        cols_send[0, 64:72, :],
        east_tile[64:72, :],
        packed(depth, COLS - 1),
        packed(east_tile[0:32, :], 0),
    )
    west_flux = column_flux(
        cols_send[1, 64:72, :],
        west_tile[64:72, :],
        packed(depth, 0),
        packed(west_tile[0:32, :], LANES - 1),
    )

    depth_near = beside(
        depth,
        east_tile[0:32, 0:1],
        west_tile[0:32, LANES - 1 : LANES],
        north_depth,
        south_depth,
    )
    open_depth = [jnp.minimum(depth, near) for near in depth_near]
    east_edges = east_tile[64:72, :]
    west_edges = west_tile[64:72, :]

    def near_field(f, field, k):
        values = field[pl.ds(pl.multiple_of(k * ROWS, ROWS), ROWS), :]
        turn = lax.rem(2 * LANES - 32 * f - 4 * k, LANES)
        east_lanes = pltpu.roll(east_edges, turn, 1)
        west_lanes = pltpu.roll(west_edges, turn, 1)
        east_edge = jnp.concatenate([east_lanes[:, g : g + 1] for g in range(4)], axis=0)
        west_edge = jnp.concatenate([west_lanes[:, g : g + 1] for g in range(4)], axis=0)
        north_edge = kept(1, rows_got[1, pl.ds(8 * f + k, 1), :])
        south_edge = kept(-1, rows_got[0, pl.ds(8 * f + k, 1), :])
        return values, beside(values, east_edge, west_edge, north_edge, south_edge)

    def layer(k, carry):
        level = k.astype(jnp.float32)
        faces = [level < limit for limit in open_depth]
        t, near_t = near_field(2, t_ref, k)
        u, near_u = near_field(0, u_ref, k)
        v, near_v = near_field(1, v_ref, k)
        spread = laplace(faces, t, near_t)
        east = jnp.where(faces[0], (u + near_u[0]) * 0.5, 0.0)
        west = jnp.where(faces[1], (near_u[1] + u) * 0.5, 0.0)
        north = jnp.where(faces[2], (v + near_v[2]) * 0.5, 0.0)
        south = jnp.where(faces[3], (near_v[3] + v) * 0.5, 0.0)
        transport = (east * (t + near_t[0]) - west * (near_t[1] + t)) + (
            north * (t + near_t[2]) - south * (near_t[3] + t)
        )
        result = t + TIME_STEP * (DIFFUSIVITY * spread - 0.5 * transport)
        guess_u, guess_v = momentum(faces, u, near_u, v, near_v)
        wet = level < depth
        rows = pl.ds(pl.multiple_of(k * ROWS, ROWS), ROWS)
        u_star[rows, :] = jnp.where(wet, guess_u, 0.0)
        v_star[rows, :] = jnp.where(wet, guess_v, 0.0)
        t_out[rows, :] = jnp.where(wet, result, 0.0)
        return carry

    lax.fori_loop(0, EARLY_LEVELS, layer, 0)

    for copy in mean_copies:
        copy.wait_recv()
    west_mean, east_mean = mean_got.at[0], mean_got.at[1]
    tile_lane = lax.broadcasted_iota(jnp.int32, (ROWS, LANES), 1)
    tile_first, tile_last = tile_lane == 0, tile_lane == LANES - 1

    def window(f, values):
        cut = slice(32 * f, 32 * f + 32)
        return jnp.concatenate(
            [
                west_mean[cut, :] - jnp.where(tile_last, west_flux[f], 0.0),
                values[:, 0:LANES] + jnp.where(tile_first, west_flux[f], 0.0),
                values[:, LANES:COLS] + jnp.where(tile_last, east_flux[f], 0.0),
                east_mean[cut, :] - jnp.where(tile_first, east_flux[f], 0.0),
            ],
            axis=1,
        )

    wide_u, wide_v = window(0, mean_u), window(1, mean_v)
    wide_eta = jnp.concatenate([west_tile[32:64, :], elevation, east_tile[32:64, :]], axis=1)
    wide_row = lax.broadcasted_iota(jnp.int32, (ROWS, WIDE), 0)
    north_v = jnp.where(wide_row == ROWS - 1, 0.0, pltpu.roll(wide_v, ROWS - 1, 0))
    south_v = jnp.where(wide_row == 0, 0.0, pltpu.roll(wide_v, 1, 0))
    across = pltpu.roll(wide_u, WIDE - 1, 1) - pltpu.roll(wide_u, 1, 1)
    depth_wide = jnp.concatenate([west_tile[0:32, :], depth, east_tile[0:32, :]], axis=1)
    source = jnp.where(
        depth_wide > 0.5, wide_eta - 0.5 * (across + (north_v - south_v)), 0.0
    )
    ends = jnp.where(
        lax.broadcasted_iota(jnp.int32, (16, WIDE), 0) == 0, wide_v[0:1, :], wide_v[31:32, :]
    )
    by_class = exact_select(jnp.concatenate([source, ends], axis=0), choice[...])
    for c in range(4):
        cut = slice(LANES * c, LANES * (c + 1))
        source_send[c] = by_class[0:32, cut]
        close_send[0, c] = by_class[24:32, cut]
        close_send[1, c] = by_class[0:8, cut]
        for side in (0, 1):
            close_send[side, 4, c : c + 1, :] = by_class[32:33, cut]
            close_send[side, 4, 4 + c : 5 + c, :] = by_class[33:34, cut]
    source_copies = [
        send(close_send.at[0], close_got.at[0], 0, 1),
        send(close_send.at[1], close_got.at[1], 0, -1),
    ]
    far_copies = [
        send(close_send.at[0, 4], close_got.at[2, 4], 0, 2),
        send(close_send.at[1, 4], close_got.at[3, 4], 0, -2),
        send(source_send.at[:, pl.ds(0, 24)], source_got.at[0, :, pl.ds(0, 24)], 0, 1),
        send(source_send.at[:, pl.ds(8, 24)], source_got.at[1, :, pl.ds(8, 24)], 0, -1),
        send(source_send.at[:, pl.ds(ROWS - 8, 8)], source_got_far.at[0], 0, 2),
        send(source_send.at[:, pl.ds(0, 8)], source_got_far.at[1], 0, -2),
    ]
    launch(source_copies + far_copies)

    for copy in depth_copies:
        copy.wait_recv()

    def slot_of(lat_move):
        return LAT_MOVES.index(-lat_move)

    def wide_depth(own, halo, move):
        return kept(move, jnp.concatenate([halo[:, 0:LANES], own, halo[:, LANES:COLS]], axis=1))

    blocks = [
        wide_depth(deep_got_far[0, 0], deep_got_far[1, 0], -2),
        wide_depth(deep_got[0, 0], deep_got[1, 0], -1),
        wide_depth(deep_send[0], deep_send[1], 0),
        wide_depth(deep_got[0, 1], deep_got[1, 1], 1),
        wide_depth(deep_got_far[0, 1], deep_got_far[1, 1], 2),
    ]
    by_class = jnp.dot(
        jnp.concatenate(blocks, axis=0).astype(jnp.bfloat16),
        choice[...],
        preferred_element_type=jnp.float32,
    )
    for c in range(4):
        deep[c, pl.ds(ORIGIN[0] - 40, 112), :] = by_class[:, LANES * c : LANES * (c + 1)]

    def finish_weights(g, rows):
        we = [grid_we[g][c, rows, :] for c in range(CLASSES[g])]
        ww = west_of(we, STEP[g])
        grid_ww[g][rows, :] = ww[0]
        before = pl.ds(rows.start - 1, 8)
        for c in range(CLASSES[g]):
            near = (we[c] + ww[c]) + (grid_wn[g][c, rows, :] + grid_wn[g][c, before, :])
            grid_dg[g][c, rows, :] = MASS[g] + near
            grid_iv[g][c, rows, :] = 1.0 / (MASS[g] + 2.0 * near)

    def fine_weights(at):
        rows, after = pl.ds(at, 8), pl.ds(at + 1, 8)
        columns = [deep[c, rows, :] * (1.0 / LEVELS) for c in range(4)]
        for c, near in enumerate(east_of(columns, 1)):
            grid_we[0][c, rows, :] = jnp.minimum(columns[c], near)
            north = deep[c, after, :] * (1.0 / LEVELS)
            grid_wn[0][c, rows, :] = jnp.minimum(columns[c], north)

    def whole(g):
        return tuple(ORIGIN[g] + end for end in ((-40, 72), (-24, 40), (-16, 24), (0, 8))[g])

    def pair_lanes(values):
        even = (lax.broadcasted_iota(jnp.int32, values.shape, 1) & 1) == 0
        return even, pltpu.roll(values, LANES - 1, 1), pltpu.roll(values, 1, 1)

    def finer_rows(g, at):
        return 2 * (at - ORIGIN[g]) + ORIGIN[g - 1]

    each_chunk(*whole(0), fine_weights)
    each_chunk(*whole(0), lambda at: finish_weights(0, pl.ds(at, 8)))
    for g in (1, 2, 3):

        def coarse_weights(at, g=g):
            rows = pl.ds(at, 8)
            above = finer_rows(g, at)
            even_rows, odd_rows = pl.ds(above, 8, stride=2), pl.ds(above + 1, 8, stride=2)
            finer_we, finer_wn = grid_we[g - 1], grid_wn[g - 1]
            if g < 3:
                for c in range(CLASSES[g]):
                    grid_we[g][c, rows, :] = (
                        finer_we[2 * c + 1, even_rows, :] + finer_we[2 * c + 1, odd_rows, :]
                    )
                    grid_wn[g][c, rows, :] = (
                        finer_wn[2 * c, odd_rows, :] + finer_wn[2 * c + 1, odd_rows, :]
                    )
            else:
                we = finer_we[0, even_rows, :] + finer_we[0, odd_rows, :]
                even, east, west = pair_lanes(we)
                grid_we[g][0, rows, :] = jnp.where(even, east, we)
                wn = finer_wn[0, odd_rows, :]
                even, east, west = pair_lanes(wn)
                grid_wn[g][0, rows, :] = wn + jnp.where(even, east, west)

        each_chunk(*whole(g), coarse_weights)
        if g < 3:
            each_chunk(*whole(g), lambda at, g=g: finish_weights(g, pl.ds(at, 8)))

    upper = lax.broadcasted_iota(jnp.int32, (8, LANES), 0) >= 4

    def around(held, own, got, moves):
        def block(move):
            return kept(move, got[moves.index(-move)][...])

        held[0, pl.ds(ORIGIN[3], 8), :] = jnp.where(upper, pltpu.roll(block(1), 4, 0), own)
        lower = pltpu.roll(block(-1), 4, 0)
        if len(moves) == 4:
            lower = jnp.where(upper, lower, block(-2))
            held[0, pl.ds(ORIGIN[3] + 8, 8), :] = block(2)
        held[0, pl.ds(ORIGIN[3] - 8, 8), :] = lower

    weight_send[0:8, :] = grid_we[3][0, pl.ds(ORIGIN[3], 8), :]
    weight_send[8:16, :] = grid_wn[3][0, pl.ds(ORIGIN[3], 8), :]
    weight_copies = [
        send(weight_send, weight_got.at[i], 0, move) for i, move in enumerate(LAT_MOVES)
    ]
    launch(weight_copies)

    lax.fori_loop(EARLY_LEVELS, LEVELS, layer, 0)
    for copy in source_copies:
        copy.wait_recv()

    rows32 = lax.broadcasted_iota(jnp.int32, (ROWS, LANES), 0)

    def ends(move, spot):
        held = close_send.at[0, 4] if move == 0 else close_got.at[slot_of(move), 4]
        return 0.5 * kept(move, held[spot : spot + 1, :])

    def place_source(move, low, high, held):
        at = rows32[: high - low] + low
        for c in range(4):
            rows = pl.ds(ORIGIN[0] + 32 * move + low, high - low)
            values = held[c]
            if move < 2 and high == ROWS:
                values = values - jnp.where(at == ROWS - 1, ends(move + 1, c), 0.0)
            if move > -2 and low == 0:
                values = values + jnp.where(at == 0, ends(move - 1, 4 + c), 0.0)
            grid_b[0][c, rows, :] = jnp.where(deep[c, rows, :] > 0.5, values, 0.0)

    place_source(-1, 24, 32, close_got.at[0])
    place_source(0, 0, 32, source_send)
    place_source(1, 0, 8, close_got.at[1])

    def place_far_source():
        for copy in far_copies:
            copy.wait_recv()
        place_source(-2, 24, 32, source_got_far.at[0])
        place_source(-1, 0, 24, source_got.at[0, :, pl.ds(0, 24)])
        place_source(1, 8, 32, source_got.at[1, :, pl.ds(8, 24)])
        place_source(2, 0, 8, source_got_far.at[1])

    def operator(g, held, at):
        rows, after, before = pl.ds(at, 8), pl.ds(at + 1, 8), pl.ds(at - 1, 8)
        count = CLASSES[g]
        p = [held[c, rows, :] for c in range(count)]
        we = [grid_we[g][c, rows, :] for c in range(count)]
        ww = [grid_ww[g][rows, :]] + we[:-1]
        pe, pw = east_of(p, STEP[g]), west_of(p, STEP[g])
        residual = []
        for c in range(count):
            pull = (we[c] * pe[c] + ww[c] * pw[c]) + (
                grid_wn[g][c, rows, :] * held[c, after, :]
                + grid_wn[g][c, before, :] * held[c, before, :]
            )
            image = grid_dg[g][c, rows, :] * p[c] - pull
            residual.append(grid_b[g][c, rows, :] - image)
        return p, residual

    def span(g, low, high):
        return ORIGIN[g] + low, ORIGIN[g] + high

    def from_zero(g, low, high, held):
        def body(at):
            rows = pl.ds(at, 8)
            for c in range(CLASSES[g]):
                held[c, rows, :] = grid_b[g][c, rows, :] * grid_iv[g][c, rows, :]

        each_chunk(*span(g, low, high), body)

    def sweep(g, low, high, held, result):
        def body(at):
            rows = pl.ds(at, 8)
            p, residual = operator(g, held, at)
            for c in range(CLASSES[g]):
                result[c, rows, :] = p[c] + residual[c] * grid_iv[g][c, rows, :]

        each_chunk(*span(g, low, high), body)

    def restricted(g, low, high, held):
        def residual_rows(at):
            rows = pl.ds(at, 8)
            _, residual = operator(g, held, at)
            if g < 2:
                for c in range(CLASSES[g] // 2):
                    grid_r[g][c, rows, :] = residual[2 * c] + residual[2 * c + 1]
            else:
                even, east, west = pair_lanes(residual[0])
                grid_r[g][0, rows, :] = residual[0] + jnp.where(even, east, west)

        each_chunk(*span(g, low, high), residual_rows)

        def pair_rows(at):
            above = finer_rows(g + 1, at)
            for c in range(CLASSES[g + 1]):
                grid_b[g + 1][c, pl.ds(at, 8), :] = (
                    grid_r[g][c, pl.ds(above, 8, stride=2), :]
                    + grid_r[g][c, pl.ds(above + 1, 8, stride=2), :]
                )

        top = (high // 2 + 7) // 8 * 8
        each_chunk(*span(g + 1, low // 2 // 8 * 8, top), pair_rows)

    def corrected(g, low, high, held, correction):
        first, last = low // 2 // 8 * 8, (high // 2 + 7) // 8 * 8

        def body(at):
            above = finer_rows(g + 1, at)
            for c in range(CLASSES[g]):
                change = correction[c // 2, pl.ds(at, 8), :]
                for odd in (0, 1):
                    rows = pl.ds(above + odd, 8, stride=2)
                    held[c, rows, :] = held[c, rows, :] + change

        each_chunk(*span(g + 1, first, last), body)

    def coarse_links(cycle, reach):
        coarse_send[cycle] = grid_b[3][0, pl.ds(ORIGIN[3], 8), :]
        moves = LAT_MOVES[: 2 * reach]
        copies = [
            send(coarse_send.at[cycle], coarse_got.at[4 * cycle + i], 0, move)
            for i, move in enumerate(moves)
        ]
        launch(copies)
        return copies, moves

    def coarse_weights_around():
        for copy in weight_copies:
            copy.wait_recv()
        for held, first in ((grid_we[3], 0), (grid_wn[3], 8)):
            cut = pl.ds(first, 8)
            around(held, weight_send[cut, :], [weight_got.at[i, cut] for i in range(4)], LAT_MOVES)
        each_chunk(ORIGIN[3] - 8, ORIGIN[3] + 16, lambda at: finish_weights(3, pl.ds(at, 8)))

    def coarse_source(cycle, copies, moves):
        for copy in copies:
            copy.wait_recv()
        got = [coarse_got.at[4 * cycle + i] for i in range(len(moves))]
        around(grid_b[3], coarse_send[cycle], got, moves)

    reach_before = (
        ((-40, 72), (-24, 40), (-16, 24)),
        ((-24, 56), (-16, 32), (-8, 16)),
        ((-16, 48), (-8, 24), (-8, 16)),
    )
    reach_after = ((-24, 56), (-16, 48), (-8, 40))
    up_rows = ((-16, 32), (-8, 24), (-8, 24))
    smoothed = (grid_q[0], grid_s, grid_q[0])
    pressure = grid_p[0]

    def descend(cycle, ranges):
        for low, high in ranges[0]:
            restricted(0, low, high, smoothed[cycle])
        for low, high in ranges[1]:
            from_zero(1, low, high, grid_q[1])
        for low, high in ranges[1]:
            restricted(1, low, high, grid_q[1])
        for low, high in ranges[2]:
            from_zero(2, low, high, grid_q[2])

    def send_coarse(cycle):
        descend(cycle, (((-8, 40),), ((-8, 24),), ((-8, 16),)))
        restricted(2, -8, 16, grid_q[2])
        return coarse_links(cycle, 1 if cycle == 2 else 2)

    def outer(cycle):
        parts = [((low, 0), (32 >> g, high)) for g, (low, high) in enumerate(reach_before[cycle])]
        if cycle == 0:
            for low, high in parts[0]:
                from_zero(0, low, high, smoothed[0])
        else:
            for low, high in parts[0]:
                sweep(0, low, high, pressure, smoothed[cycle])
        descend(cycle, parts)

    from_zero(0, -8, 40, smoothed[0])
    links = send_coarse(0)
    place_far_source()
    outer(0)
    coarse_weights_around()
    for cycle in range(CYCLES):
        coarse_source(cycle, *links)
        from_zero(3, -8, 16, grid_q[3])
        here, there_ = grid_q[3], grid_p[3]
        for _ in range(SWEEPS - 1):
            sweep(3, -8, 16, here, there_)
            here, there_ = there_, here
        corrected(2, -8, 16, grid_q[2], here)
        sweep(2, -8, 16, grid_q[2], grid_p[2])
        corrected(1, *up_rows[cycle], grid_q[1], grid_p[2])
        sweep(1, *up_rows[cycle], grid_q[1], grid_p[1])
        corrected(0, -16, 48, smoothed[cycle], grid_p[1])
        sweep(0, -8, 40, smoothed[cycle], pressure)
        if cycle + 1 < CYCLES:
            sweep(0, -8, 40, pressure, smoothed[cycle + 1])
            links = send_coarse(cycle + 1)
            low, high = reach_after[cycle]
            if cycle == 0:
                corrected(0, -32, -16, smoothed[0], grid_p[1])
                corrected(0, 48, 64, smoothed[0], grid_p[1])
            sweep(0, low, -8, smoothed[cycle], pressure)
            sweep(0, 40, high, smoothed[cycle], pressure)
            outer(cycle + 1)

    own = pl.ds(ORIGIN[0], ROWS)
    p = [pressure[c, own, :] for c in range(4)]
    slope_east = [0.5 * (e - w) for e, w in zip(east_of(p, 1), west_of(p, 1))]
    slope_north = [
        0.5 * (pressure[c, pl.ds(ORIGIN[0] + 1, ROWS), :] - pressure[c, pl.ds(ORIGIN[0] - 1, ROWS), :])
        for c in range(4)
    ]
    stacked = jnp.concatenate(
        [jnp.concatenate(parts, axis=1) for parts in (p, slope_east, slope_north)], axis=0
    )
    ordered = exact_select(stacked, unchoice[...])
    p_out[...] = ordered[0:32]
    push_u = GRAVITY_STEP * ordered[32:64]
    push_v = GRAVITY_STEP * ordered[64:96]
    for k in range(LEVELS):
        rows = slice(k * ROWS, (k + 1) * ROWS)
        wet = depth > k
        u_out[rows, :] = jnp.where(wet, u_star[rows, :] - push_u, 0.0)
        v_out[rows, :] = jnp.where(wet, v_star[rows, :] - push_v, 0.0)
    for copy in started:
        copy.wait_send()


def deliver(*refs):
    held, outs, sem = refs[:4], refs[4:8], refs[8]
    copies = [pltpu.make_async_copy(held[i], outs[i], sem.at[i]) for i in range(4)]
    for copy in copies:
        copy.start()
    for copy in copies:
        copy.wait()


def shards(lon_count, lat_count, u, v, t, depth, elevation):
    f32 = jnp.float32
    flat = (LEVELS * ROWS, COLS)
    block = pl.BlockSpec(memory_space=pltpu.VMEM)

    def grids(classes=CLASSES):
        return [pltpu.VMEM((c, h, LANES), f32) for c, h in zip(classes, HEIGHT)]

    shapes = [flat] * 3 + [(ROWS, COLS)]
    anywhere = pl.BlockSpec(memory_space=pl.ANY)
    held = pl.pallas_call(
        functools.partial(kernel, lon_count, lat_count),
        out_shape=[pltpu.VMEM(shape, f32) for shape in shapes],
        in_specs=[anywhere] * 5,
        out_specs=[block] * 4,
        scratch_shapes=[
            pltpu.VMEM(flat, f32),
            pltpu.VMEM(flat, f32),
            pltpu.VMEM(flat, f32),
            pltpu.VMEM((ROWS, COLS), jnp.int32),
            pltpu.VMEM((ROWS, COLS), f32),
            pltpu.VMEM(flat, f32),
            pltpu.VMEM(flat, f32),
            pltpu.VMEM((2, 32, COLS), f32),
            pltpu.VMEM((2, 32, COLS), f32),
            pltpu.VMEM((2, 72, LANES), f32),
            pltpu.VMEM((2, 72, LANES), f32),
            pltpu.VMEM((2, 64, LANES), f32),
            pltpu.VMEM((2, 64, LANES), f32),
            pltpu.VMEM((2, ROWS, COLS), f32),
            pltpu.VMEM((2, 2, ROWS, COLS), f32),
            pltpu.VMEM((2, 2, 8, COLS), f32),
            pltpu.VMEM((4, ROWS, LANES), f32),
            pltpu.VMEM((2, 4, ROWS, LANES), f32),
            pltpu.VMEM((2, 4, 8, LANES), f32),
            pltpu.VMEM((2, 5, 8, LANES), f32),
            pltpu.VMEM((4, 5, 8, LANES), f32),
            pltpu.VMEM((16, LANES), f32),
            pltpu.VMEM((4, 16, LANES), f32),
            pltpu.VMEM((CYCLES, 8, LANES), f32),
            pltpu.VMEM((10, 8, LANES), f32),
            pltpu.VMEM((WIDE, WIDE), jnp.bfloat16),
            pltpu.VMEM((WIDE, COLS), jnp.bfloat16),
            pltpu.VMEM((4, HEIGHT[0], LANES), f32),
            grids(),
            grids(),
            grids(),
            grids(),
            [pltpu.VMEM((h, LANES), f32) for h in HEIGHT],
            grids(),
            grids(),
            grids(),
            grids(),
            pltpu.VMEM((4, HEIGHT[0], LANES), f32),
            pltpu.SemaphoreType.DMA((5,)),
            pltpu.SemaphoreType.DMA((40,)),
            pltpu.SemaphoreType.DMA((40,)),
        ],
        compiler_params=pltpu.CompilerParams(
            collective_id=0, has_side_effects=True, vmem_limit_bytes=32 << 20
        ),
    )(
        *[
            pltpu.with_memory_space_constraint(x, pltpu.HBM)
            for x in (u.reshape(flat), v.reshape(flat), t.reshape(flat), depth, elevation)
        ]
    )
    outs = pl.pallas_call(
        deliver,
        out_shape=[jax.ShapeDtypeStruct(shape, f32) for shape in shapes],
        in_specs=[block] * 4,
        out_specs=[anywhere] * 4,
        scratch_shapes=[pltpu.SemaphoreType.DMA((4,))],
    )(*[pltpu.with_memory_space_constraint(x, pltpu.VMEM) for x in held])
    shape = (LEVELS, ROWS, COLS)
    return outs[0].reshape(shape), outs[1].reshape(shape), outs[2].reshape(shape), outs[3]


def solution(mesh):
    spec3, spec2 = P(None, "lat", "lon"), P("lat", "lon")
    return jax.shard_map(
        functools.partial(shards, mesh.shape["lon"], mesh.shape["lat"]),
        mesh=mesh,
        in_specs=(spec3, spec3, spec3, spec2, spec2),
        out_specs=(spec3, spec3, spec3, spec2),
        check_vma=False,
    )
```

```python
import functools

import jax
import jax.numpy as jnp
from jax import lax
from jax.experimental import pallas as pl
from jax.experimental.pallas import tpu as pltpu
from jax.sharding import PartitionSpec as P

LEVELS = 8
CYCLES = 3
SWEEPS = 4
TIME_STEP = 0.2
VISCOSITY = 1.0
DIFFUSIVITY = 1.0
CORIOLIS = 1.0
MASS_TERM = 0.05
GRAVITY_STEP = 0.5

ROWS = 32
COLS = 256
LANES = 128
WIDE = 512
MESH_IDS = pl.DeviceIdType.MESH

CLASSES = (4, 2, 1, 1)
STEP = (1, 1, 1, 2)
ORIGIN = (48, 32, 24, 16)
HEIGHT = (144, 96, 64, 48)
MASS = tuple(MASS_TERM * 4.0**g for g in range(4))

LAT_MOVES = (1, -1, 2, -2)
EARLY_LEVELS = 5


def east_of(parts, step):
    turned = pltpu.roll(parts[0], LANES - step, 1)
    return list(parts[1:]) + [turned]


def west_of(parts, step):
    turned = pltpu.roll(parts[-1], step, 1)
    return [turned] + list(parts[:-1])


def each_chunk(first, last, body, unroll=5):
    count = (last - first) // 8
    if count <= unroll:
        for i in range(count):
            body(first + 8 * i)
        return
    while count % unroll:
        unroll -= 1

    def step(i, carry):
        for j in range(unroll):
            body(pl.multiple_of(first + (i * unroll + j) * 8, 8))
        return carry

    lax.fori_loop(0, count // unroll, step, 0)


def split_three(values):
    high = values.astype(jnp.bfloat16)
    rest = values - high.astype(jnp.float32)
    middle = rest.astype(jnp.bfloat16)
    low = (rest - middle.astype(jnp.float32)).astype(jnp.bfloat16)
    return jnp.concatenate([high, middle, low], axis=0)


def exact_select(values, choice):
    count = values.shape[0]
    product = jnp.dot(split_three(values), choice, preferred_element_type=jnp.float32)
    return (product[:count] + product[count : 2 * count]) + product[2 * count :]


class Link:
    def __init__(self, copy, leaves, comes):
        self.copy, self.leaves, self.comes = copy, leaves, comes

    def start(self):
        if self.leaves is None:
            self.copy.start()
        else:
            pl.when(self.leaves)(self.copy.start)

    def wait_send(self):
        if self.leaves is None:
            self.copy.wait_send()
        else:
            pl.when(self.leaves)(self.copy.wait_send)

    def wait_recv(self):
        if self.comes is None:
            self.copy.wait_recv()
        else:
            pl.when(self.comes)(self.copy.wait_recv)


def kernel(
    lon_count,
    lat_count,
    u_far,
    v_far,
    t_far,
    depth_far,
    elevation_far,
    u_out,
    v_out,
    t_out,
    p_out,
    u_ref,
    v_ref,
    t_ref,
    depth_ref,
    elevation_ref,
    u_star,
    v_star,
    rows_send,
    rows_got,
    cols_send,
    cols_got,
    mean_send,
    mean_got,
    deep_send,
    deep_got,
    deep_got_far,
    source_send,
    source_got,
    source_got_far,
    close_send,
    close_got,
    weight_send,
    weight_got,
    coarse_send,
    coarse_got,
    choice,
    unchoice,
    deep,
    grid_b,
    grid_p,
    grid_q,
    grid_we,
    grid_ww,
    grid_wn,
    grid_dg,
    grid_iv,
    grid_r,
    grid_s,
    load_sem,
    send_sem,
    recv_sem,
):
    lon = lax.axis_index("lon")
    lat = lax.axis_index("lat")
    sems = iter(range(64))

    def there(lon_move, lat_move):
        return {
            "lon": lax.rem(lon + lon_move + lon_count, lon_count),
            "lat": lax.rem(lat + lat_move + lat_count, lat_count),
        }

    def send(source, target, lon_move, lat_move):
        at = next(sems)
        copy = pltpu.make_async_remote_copy(
            src_ref=source,
            dst_ref=target,
            send_sem=send_sem.at[at],
            recv_sem=recv_sem.at[at],
            device_id=there(lon_move, lat_move),
            device_id_type=MESH_IDS,
        )
        if lat_move == 0:
            return Link(copy, None, None)
        return Link(copy, inside(lat_move), inside(-lat_move))

    def inside(lat_move):
        return (lat + lat_move >= 0) & (lat + lat_move < lat_count)

    def kept(lat_move, values):
        if lat_move == 0:
            return values
        return jnp.where(inside(lat_move), values, jnp.zeros_like(values))

    started = []

    def launch(copies):
        for copy in copies:
            copy.start()
        started.extend(copies)

    barrier = pltpu.get_barrier_semaphore()
    for lon_move in (1, -1):
        pl.semaphore_signal(
            barrier, inc=1, device_id=there(lon_move, 0), device_id_type=MESH_IDS
        )
    beside_count = jnp.int32(2)
    for lat_move in LAT_MOVES:
        beside_count = beside_count + inside(lat_move).astype(jnp.int32)

        @pl.when(inside(lat_move))
        def _(lat_move=lat_move):
            pl.semaphore_signal(
                barrier, inc=1, device_id=there(0, lat_move), device_id_type=MESH_IDS
            )


    loads = [
        pltpu.make_async_copy(far, near, load_sem.at[i])
        for i, (far, near) in enumerate(
            (
                (depth_far, depth_ref),
                (elevation_far, elevation_ref),
                (u_far, u_ref),
                (v_far, v_ref),
                (t_far, t_ref),
            )
        )
    ]
    for load in loads:
        load.start()
    for load in loads:
        load.wait()

    depth = depth_ref[...].astype(jnp.float32)
    lane8 = lax.broadcasted_iota(jnp.int32, (8, LANES), 1)
    fields = (u_ref, v_ref, t_ref)
    for side, row in ((0, ROWS - 1), (1, 0)):
        for f, field in enumerate(fields):
            for k in range(LEVELS):
                rows_send[side, 8 * f + k : 8 * f + k + 1, :] = field[
                    k * ROWS + row : k * ROWS + row + 1, :
                ]
        rows_send[side, pl.ds(24, 8), :] = jnp.broadcast_to(depth[row : row + 1, :], (8, COLS))

    def pack(i, carry):
        at_last, at_first = carry
        rows = pl.ds(pl.multiple_of(8 * i, 8), 8)
        for f, field in enumerate(fields):
            here = lane8 == i + 32 * f
            at_last = jnp.where(here, field[rows, COLS - 1 : COLS], at_last)
            at_first = jnp.where(here, field[rows, 0:1], at_first)
        return at_last, at_first

    zero8 = jnp.zeros((8, LANES), jnp.float32)
    at_last, at_first = lax.fori_loop(0, 32, pack, (zero8, zero8), unroll=4)
    elevation = elevation_ref[...]
    deep_send[0] = depth
    for side, edge, tile in ((0, at_last, 1), (1, at_first, 0)):
        cut = slice(tile * LANES, (tile + 1) * LANES)
        cols_send[side, 0:32, :] = depth[:, cut]
        cols_send[side, 32:64, :] = elevation[:, cut]
        cols_send[side, 64:72, :] = edge

    pl.semaphore_wait(barrier, beside_count)
    row_copies = [
        send(rows_send.at[0], rows_got.at[0], 0, 1),
        send(rows_send.at[1], rows_got.at[1], 0, -1),
    ]
    column_copies = [
        send(cols_send.at[0], cols_got.at[0], 1, 0),
        send(cols_send.at[1], cols_got.at[1], -1, 0),
    ]
    launch(column_copies + row_copies)

    def depth_sends(part):
        source = deep_send.at[part]
        return [
            send(source, deep_got.at[part, 0], 0, 1),
            send(source, deep_got.at[part, 1], 0, -1),
            send(source.at[pl.ds(ROWS - 8, 8)], deep_got_far.at[part, 0], 0, 2),
            send(source.at[pl.ds(0, 8)], deep_got_far.at[part, 1], 0, -2),
        ]

    depth_copies = depth_sends(0)
    launch(depth_copies)

    row_number = lax.broadcasted_iota(jnp.int32, (ROWS, LANES), 0)
    place = (lat * ROWS + row_number).astype(jnp.float32)
    angle = jnp.pi * ((place + 0.5) / (ROWS * lat_count) - 0.5)
    turning = CORIOLIS * jnp.sin(angle)
    rotation = jnp.concatenate([turning, turning], axis=1)

    row = lax.broadcasted_iota(jnp.int32, (ROWS, COLS), 0)
    column = lax.broadcasted_iota(jnp.int32, (ROWS, COLS), 1)
    on_east, on_west = column == COLS - 1, column == 0
    on_north, on_south = row == ROWS - 1, row == 0

    def beside(values, east_edge, west_edge, north_edge, south_edge):
        return (
            jnp.where(on_east, east_edge, pltpu.roll(values, COLS - 1, 1)),
            jnp.where(on_west, west_edge, pltpu.roll(values, 1, 1)),
            jnp.where(on_north, north_edge, pltpu.roll(values, ROWS - 1, 0)),
            jnp.where(on_south, south_edge, pltpu.roll(values, 1, 0)),
        )

    def laplace(faces, values, nearby):
        terms = [jnp.where(face, near - values, 0.0) for face, near in zip(faces, nearby)]
        return (terms[0] + terms[1]) + (terms[2] + terms[3])

    def momentum(faces, u, near_u, v, near_v):
        guess_u = u + TIME_STEP * (VISCOSITY * laplace(faces, u, near_u) + rotation * v)
        guess_v = v + TIME_STEP * (VISCOSITY * laplace(faces, v, near_v) - rotation * u)
        return guess_u, guess_v

    inner_depth = [jnp.minimum(depth, near) for near in beside(depth, 0.0, 0.0, 0.0, 0.0)]

    def inner(k, carry):
        sum_u, sum_v = carry
        level = k.astype(jnp.float32)
        faces = [level < limit for limit in inner_depth]
        rows = pl.ds(pl.multiple_of(k * ROWS, ROWS), ROWS)
        u, v = u_ref[rows, :], v_ref[rows, :]
        near_u, near_v = beside(u, 0.0, 0.0, 0.0, 0.0), beside(v, 0.0, 0.0, 0.0, 0.0)
        guess_u, guess_v = momentum(faces, u, near_u, v, near_v)
        wet = level < depth
        return sum_u + jnp.where(wet, guess_u, 0.0), sum_v + jnp.where(wet, guess_v, 0.0)

    zero = jnp.zeros((ROWS, COLS), jnp.float32)
    sum_u, sum_v = lax.fori_loop(0, LEVELS, inner, (zero, zero))
    gain = TIME_STEP * VISCOSITY / LEVELS

    for copy in row_copies:
        copy.wait_recv()
    north_depth = kept(1, rows_got[1, 24:25, :])
    south_depth = kept(-1, rows_got[0, 24:25, :])
    level8 = lax.broadcasted_iota(jnp.int32, (LEVELS, COLS), 0).astype(jnp.float32)

    def row_flux(f, side, limit):
        step = rows_got[side, 8 * f : 8 * f + 8, :] - rows_send[1 - side, 8 * f : 8 * f + 8, :]
        return gain * jnp.sum(jnp.where(level8 < limit, step, 0.0), axis=0, keepdims=True)

    north_limit = jnp.minimum(depth[ROWS - 1 : ROWS, :], north_depth)
    south_limit = jnp.minimum(depth[0:1, :], south_depth)

    def mean(f, total):
        return (
            total * (1.0 / LEVELS)
            + jnp.where(on_north, row_flux(f, 1, north_limit), 0.0)
            + jnp.where(on_south, row_flux(f, 0, south_limit), 0.0)
        )

    mean_u, mean_v = mean(0, sum_u), mean(1, sum_v)
    for side, tile in ((0, 1), (1, 0)):
        cut = slice(tile * LANES, (tile + 1) * LANES)
        mean_send[side, 0:32, :] = mean_u[:, cut]
        mean_send[side, 32:64, :] = mean_v[:, cut]
    mean_copies = [
        send(mean_send.at[0], mean_got.at[0], 1, 0),
        send(mean_send.at[1], mean_got.at[1], -1, 0),
    ]
    launch(mean_copies)

    def order(n):
        return ((((n & 127) + 32) & 127) << 2) + (n >> 7)

    wanted = order(lax.broadcasted_iota(jnp.int32, (1, WIDE), 1))

    def fill(i, carry):
        rows = pl.ds(pl.multiple_of(32 * i, 32), 32)
        k = lax.broadcasted_iota(jnp.int32, (32, WIDE), 0) + 32 * i
        choice[rows, :] = jnp.where(k == wanted, 1.0, 0.0).astype(jnp.bfloat16)
        n = lax.broadcasted_iota(jnp.int32, (32, COLS), 0) + 32 * i
        column = lax.broadcasted_iota(jnp.int32, (32, COLS), 1) + LANES
        unchoice[rows, :] = jnp.where(order(n) == column, 1.0, 0.0).astype(jnp.bfloat16)
        return carry

    lax.fori_loop(0, WIDE // 32, fill, 0)
    for ref in list(grid_p) + list(grid_q) + list(grid_b) + list(grid_wn) + [deep, grid_s]:
        ref[...] = jnp.zeros_like(ref)
    for copy in column_copies:
        copy.wait_recv()

    west_tile, east_tile = cols_got.at[0], cols_got.at[1]
    deep_send[1, :, 0:LANES] = west_tile[0:32, :]
    deep_send[1, :, LANES:COLS] = east_tile[0:32, :]
    more_depth = depth_sends(1)
    launch(more_depth)
    depth_copies = depth_copies + more_depth

    lane_row = lane8 & 3
    lane_level = ((lane8 >> 2) & 7).astype(jnp.float32)

    def packed(values, column):
        result = zero8
        for g in range(4):
            result = jnp.where(lane_row == g, values[8 * g : 8 * g + 8, column : column + 1], result)
        return result

    def column_flux(own, other, own_depth, other_depth):
        limit = jnp.minimum(own_depth, other_depth)
        flux = jnp.where(lane_level < limit, other - own, 0.0)
        for turn in (4, 8, 16):
            flux = flux + pltpu.roll(flux, turn, 1)
        flux = gain * flux
        return [
            jnp.concatenate([flux[:, at + g : at + g + 1] for g in range(4)], axis=0)
            for at in (28, 60)
        ]

    east_flux = column_flux(
        cols_send[0, 64:72, :],
        east_tile[64:72, :],
        packed(depth, COLS - 1),
        packed(east_tile[0:32, :], 0),
    )
    west_flux = column_flux(
        cols_send[1, 64:72, :],
        west_tile[64:72, :],
        packed(depth, 0),
        packed(west_tile[0:32, :], LANES - 1),
    )

    depth_near = beside(
        depth,
        east_tile[0:32, 0:1],
        west_tile[0:32, LANES - 1 : LANES],
        north_depth,
        south_depth,
    )
    open_depth = [jnp.minimum(depth, near) for near in depth_near]
    east_edges = east_tile[64:72, :]
    west_edges = west_tile[64:72, :]

    def near_field(f, field, k):
        values = field[pl.ds(pl.multiple_of(k * ROWS, ROWS), ROWS), :]
        turn = lax.rem(2 * LANES - 32 * f - 4 * k, LANES)
        east_lanes = pltpu.roll(east_edges, turn, 1)
        west_lanes = pltpu.roll(west_edges, turn, 1)
        east_edge = jnp.concatenate([east_lanes[:, g : g + 1] for g in range(4)], axis=0)
        west_edge = jnp.concatenate([west_lanes[:, g : g + 1] for g in range(4)], axis=0)
        north_edge = kept(1, rows_got[1, pl.ds(8 * f + k, 1), :])
        south_edge = kept(-1, rows_got[0, pl.ds(8 * f + k, 1), :])
        return values, beside(values, east_edge, west_edge, north_edge, south_edge)

    def layer(k, carry):
        level = k.astype(jnp.float32)
        faces = [level < limit for limit in open_depth]
        t, near_t = near_field(2, t_ref, k)
        u, near_u = near_field(0, u_ref, k)
        v, near_v = near_field(1, v_ref, k)
        spread = laplace(faces, t, near_t)
        east = jnp.where(faces[0], (u + near_u[0]) * 0.5, 0.0)
        west = jnp.where(faces[1], (near_u[1] + u) * 0.5, 0.0)
        north = jnp.where(faces[2], (v + near_v[2]) * 0.5, 0.0)
        south = jnp.where(faces[3], (near_v[3] + v) * 0.5, 0.0)
        transport = (east * (t + near_t[0]) - west * (near_t[1] + t)) + (
            north * (t + near_t[2]) - south * (near_t[3] + t)
        )
        result = t + TIME_STEP * (DIFFUSIVITY * spread - 0.5 * transport)
        guess_u, guess_v = momentum(faces, u, near_u, v, near_v)
        wet = level < depth
        rows = pl.ds(pl.multiple_of(k * ROWS, ROWS), ROWS)
        u_star[rows, :] = jnp.where(wet, guess_u, 0.0)
        v_star[rows, :] = jnp.where(wet, guess_v, 0.0)
        t_out[rows, :] = jnp.where(wet, result, 0.0)
        return carry

    lax.fori_loop(0, EARLY_LEVELS, layer, 0)

    for copy in mean_copies:
        copy.wait_recv()
    west_mean, east_mean = mean_got.at[0], mean_got.at[1]
    tile_lane = lax.broadcasted_iota(jnp.int32, (ROWS, LANES), 1)
    tile_first, tile_last = tile_lane == 0, tile_lane == LANES - 1

    def window(f, values):
        cut = slice(32 * f, 32 * f + 32)
        return jnp.concatenate(
            [
                west_mean[cut, :] - jnp.where(tile_last, west_flux[f], 0.0),
                values[:, 0:LANES] + jnp.where(tile_first, west_flux[f], 0.0),
                values[:, LANES:COLS] + jnp.where(tile_last, east_flux[f], 0.0),
                east_mean[cut, :] - jnp.where(tile_first, east_flux[f], 0.0),
            ],
            axis=1,
        )

    wide_u, wide_v = window(0, mean_u), window(1, mean_v)
    wide_eta = jnp.concatenate([west_tile[32:64, :], elevation, east_tile[32:64, :]], axis=1)
    wide_row = lax.broadcasted_iota(jnp.int32, (ROWS, WIDE), 0)
    north_v = jnp.where(wide_row == ROWS - 1, 0.0, pltpu.roll(wide_v, ROWS - 1, 0))
    south_v = jnp.where(wide_row == 0, 0.0, pltpu.roll(wide_v, 1, 0))
    across = pltpu.roll(wide_u, WIDE - 1, 1) - pltpu.roll(wide_u, 1, 1)
    depth_wide = jnp.concatenate([west_tile[0:32, :], depth, east_tile[0:32, :]], axis=1)
    source = jnp.where(
        depth_wide > 0.5, wide_eta - 0.5 * (across + (north_v - south_v)), 0.0
    )
    ends = jnp.where(
        lax.broadcasted_iota(jnp.int32, (16, WIDE), 0) == 0, wide_v[0:1, :], wide_v[31:32, :]
    )
    by_class = exact_select(jnp.concatenate([source, ends], axis=0), choice[...])
    for c in range(4):
        cut = slice(LANES * c, LANES * (c + 1))
        source_send[c] = by_class[0:32, cut]
        close_send[0, c] = by_class[24:32, cut]
        close_send[1, c] = by_class[0:8, cut]
        for side in (0, 1):
            close_send[side, 4, c : c + 1, :] = by_class[32:33, cut]
            close_send[side, 4, 4 + c : 5 + c, :] = by_class[33:34, cut]
    source_copies = [
        send(close_send.at[0], close_got.at[0], 0, 1),
        send(close_send.at[1], close_got.at[1], 0, -1),
    ]
    far_copies = [
        send(close_send.at[0, 4], close_got.at[2, 4], 0, 2),
        send(close_send.at[1, 4], close_got.at[3, 4], 0, -2),
        send(source_send.at[:, pl.ds(0, 24)], source_got.at[0, :, pl.ds(0, 24)], 0, 1),
        send(source_send.at[:, pl.ds(8, 24)], source_got.at[1, :, pl.ds(8, 24)], 0, -1),
        send(source_send.at[:, pl.ds(ROWS - 8, 8)], source_got_far.at[0], 0, 2),
        send(source_send.at[:, pl.ds(0, 8)], source_got_far.at[1], 0, -2),
    ]
    launch(source_copies + far_copies)

    for copy in depth_copies:
        copy.wait_recv()

    def slot_of(lat_move):
        return LAT_MOVES.index(-lat_move)

    def wide_depth(own, halo, move):
        return kept(move, jnp.concatenate([halo[:, 0:LANES], own, halo[:, LANES:COLS]], axis=1))

    blocks = [
        wide_depth(deep_got_far[0, 0], deep_got_far[1, 0], -2),
        wide_depth(deep_got[0, 0], deep_got[1, 0], -1),
        wide_depth(deep_send[0], deep_send[1], 0),
        wide_depth(deep_got[0, 1], deep_got[1, 1], 1),
        wide_depth(deep_got_far[0, 1], deep_got_far[1, 1], 2),
    ]
    by_class = jnp.dot(
        jnp.concatenate(blocks, axis=0).astype(jnp.bfloat16),
        choice[...],
        preferred_element_type=jnp.float32,
    )
    for c in range(4):
        deep[c, pl.ds(ORIGIN[0] - 40, 112), :] = by_class[:, LANES * c : LANES * (c + 1)]

    def finish_weights(g, rows):
        we = [grid_we[g][c, rows, :] for c in range(CLASSES[g])]
        ww = west_of(we, STEP[g])
        grid_ww[g][rows, :] = ww[0]
        before = pl.ds(rows.start - 1, 8)
        for c in range(CLASSES[g]):
            near = (we[c] + ww[c]) + (grid_wn[g][c, rows, :] + grid_wn[g][c, before, :])
            grid_dg[g][c, rows, :] = MASS[g] + near
            grid_iv[g][c, rows, :] = 1.0 / (MASS[g] + 2.0 * near)

    def fine_weights(at):
        rows, after = pl.ds(at, 8), pl.ds(at + 1, 8)
        columns = [deep[c, rows, :] * (1.0 / LEVELS) for c in range(4)]
        for c, near in enumerate(east_of(columns, 1)):
            grid_we[0][c, rows, :] = jnp.minimum(columns[c], near)
            north = deep[c, after, :] * (1.0 / LEVELS)
            grid_wn[0][c, rows, :] = jnp.minimum(columns[c], north)

    def whole(g):
        return tuple(ORIGIN[g] + end for end in ((-40, 72), (-24, 40), (-16, 24), (0, 8))[g])

    def pair_lanes(values):
        even = (lax.broadcasted_iota(jnp.int32, values.shape, 1) & 1) == 0
        return even, pltpu.roll(values, LANES - 1, 1), pltpu.roll(values, 1, 1)

    def finer_rows(g, at):
        return 2 * (at - ORIGIN[g]) + ORIGIN[g - 1]

    each_chunk(*whole(0), fine_weights)
    each_chunk(*whole(0), lambda at: finish_weights(0, pl.ds(at, 8)))
    for g in (1, 2, 3):

        def coarse_weights(at, g=g):
            rows = pl.ds(at, 8)
            above = finer_rows(g, at)
            even_rows, odd_rows = pl.ds(above, 8, stride=2), pl.ds(above + 1, 8, stride=2)
            finer_we, finer_wn = grid_we[g - 1], grid_wn[g - 1]
            if g < 3:
                for c in range(CLASSES[g]):
                    grid_we[g][c, rows, :] = (
                        finer_we[2 * c + 1, even_rows, :] + finer_we[2 * c + 1, odd_rows, :]
                    )
                    grid_wn[g][c, rows, :] = (
                        finer_wn[2 * c, odd_rows, :] + finer_wn[2 * c + 1, odd_rows, :]
                    )
            else:
                we = finer_we[0, even_rows, :] + finer_we[0, odd_rows, :]
                even, east, west = pair_lanes(we)
                grid_we[g][0, rows, :] = jnp.where(even, east, we)
                wn = finer_wn[0, odd_rows, :]
                even, east, west = pair_lanes(wn)
                grid_wn[g][0, rows, :] = wn + jnp.where(even, east, west)

        each_chunk(*whole(g), coarse_weights)
        if g < 3:
            each_chunk(*whole(g), lambda at, g=g: finish_weights(g, pl.ds(at, 8)))

    upper = lax.broadcasted_iota(jnp.int32, (8, LANES), 0) >= 4

    def around(held, own, got, moves):
        def block(move):
            return kept(move, got[moves.index(-move)][...])

        held[0, pl.ds(ORIGIN[3], 8), :] = jnp.where(upper, pltpu.roll(block(1), 4, 0), own)
        lower = pltpu.roll(block(-1), 4, 0)
        if len(moves) == 4:
            lower = jnp.where(upper, lower, block(-2))
            held[0, pl.ds(ORIGIN[3] + 8, 8), :] = block(2)
        held[0, pl.ds(ORIGIN[3] - 8, 8), :] = lower

    weight_send[0:8, :] = grid_we[3][0, pl.ds(ORIGIN[3], 8), :]
    weight_send[8:16, :] = grid_wn[3][0, pl.ds(ORIGIN[3], 8), :]
    weight_copies = [
        send(weight_send, weight_got.at[i], 0, move) for i, move in enumerate(LAT_MOVES)
    ]
    launch(weight_copies)

    lax.fori_loop(EARLY_LEVELS, LEVELS, layer, 0)
    for copy in source_copies:
        copy.wait_recv()

    rows32 = lax.broadcasted_iota(jnp.int32, (ROWS, LANES), 0)

    def ends(move, spot):
        held = close_send.at[0, 4] if move == 0 else close_got.at[slot_of(move), 4]
        return 0.5 * kept(move, held[spot : spot + 1, :])

    def place_source(move, low, high, held):
        at = rows32[: high - low] + low
        for c in range(4):
            rows = pl.ds(ORIGIN[0] + 32 * move + low, high - low)
            values = held[c]
            if move < 2 and high == ROWS:
                values = values - jnp.where(at == ROWS - 1, ends(move + 1, c), 0.0)
            if move > -2 and low == 0:
                values = values + jnp.where(at == 0, ends(move - 1, 4 + c), 0.0)
            grid_b[0][c, rows, :] = jnp.where(deep[c, rows, :] > 0.5, values, 0.0)

    place_source(-1, 24, 32, close_got.at[0])
    place_source(0, 0, 32, source_send)
    place_source(1, 0, 8, close_got.at[1])

    def place_far_source():
        for copy in far_copies:
            copy.wait_recv()
        place_source(-2, 24, 32, source_got_far.at[0])
        place_source(-1, 0, 24, source_got.at[0, :, pl.ds(0, 24)])
        place_source(1, 8, 32, source_got.at[1, :, pl.ds(8, 24)])
        place_source(2, 0, 8, source_got_far.at[1])

    def operator(g, held, at):
        rows, after, before = pl.ds(at, 8), pl.ds(at + 1, 8), pl.ds(at - 1, 8)
        count = CLASSES[g]
        p = [held[c, rows, :] for c in range(count)]
        we = [grid_we[g][c, rows, :] for c in range(count)]
        ww = [grid_ww[g][rows, :]] + we[:-1]
        pe, pw = east_of(p, STEP[g]), west_of(p, STEP[g])
        residual = []
        for c in range(count):
            pull = (we[c] * pe[c] + ww[c] * pw[c]) + (
                grid_wn[g][c, rows, :] * held[c, after, :]
                + grid_wn[g][c, before, :] * held[c, before, :]
            )
            image = grid_dg[g][c, rows, :] * p[c] - pull
            residual.append(grid_b[g][c, rows, :] - image)
        return p, residual

    def span(g, low, high):
        return ORIGIN[g] + low, ORIGIN[g] + high

    def from_zero(g, low, high, held):
        def body(at):
            rows = pl.ds(at, 8)
            for c in range(CLASSES[g]):
                held[c, rows, :] = grid_b[g][c, rows, :] * grid_iv[g][c, rows, :]

        each_chunk(*span(g, low, high), body)

    def sweep(g, low, high, held, result):
        def body(at):
            rows = pl.ds(at, 8)
            p, residual = operator(g, held, at)
            for c in range(CLASSES[g]):
                result[c, rows, :] = p[c] + residual[c] * grid_iv[g][c, rows, :]

        each_chunk(*span(g, low, high), body)

    def restricted(g, low, high, held):
        def residual_rows(at):
            rows = pl.ds(at, 8)
            _, residual = operator(g, held, at)
            if g < 2:
                for c in range(CLASSES[g] // 2):
                    grid_r[g][c, rows, :] = residual[2 * c] + residual[2 * c + 1]
            else:
                even, east, west = pair_lanes(residual[0])
                grid_r[g][0, rows, :] = residual[0] + jnp.where(even, east, west)

        each_chunk(*span(g, low, high), residual_rows)

        def pair_rows(at):
            above = finer_rows(g + 1, at)
            for c in range(CLASSES[g + 1]):
                grid_b[g + 1][c, pl.ds(at, 8), :] = (
                    grid_r[g][c, pl.ds(above, 8, stride=2), :]
                    + grid_r[g][c, pl.ds(above + 1, 8, stride=2), :]
                )

        top = (high // 2 + 7) // 8 * 8
        each_chunk(*span(g + 1, low // 2 // 8 * 8, top), pair_rows)

    def corrected(g, low, high, held, correction):
        first, last = low // 2 // 8 * 8, (high // 2 + 7) // 8 * 8

        def body(at):
            above = finer_rows(g + 1, at)
            for c in range(CLASSES[g]):
                change = correction[c // 2, pl.ds(at, 8), :]
                for odd in (0, 1):
                    rows = pl.ds(above + odd, 8, stride=2)
                    held[c, rows, :] = held[c, rows, :] + change

        each_chunk(*span(g + 1, first, last), body)

    def coarse_links(cycle, reach):
        coarse_send[cycle] = grid_b[3][0, pl.ds(ORIGIN[3], 8), :]
        moves = LAT_MOVES[: 2 * reach]
        copies = [
            send(coarse_send.at[cycle], coarse_got.at[4 * cycle + i], 0, move)
            for i, move in enumerate(moves)
        ]
        launch(copies)
        return copies, moves

    def coarse_weights_around():
        for copy in weight_copies:
            copy.wait_recv()
        for held, first in ((grid_we[3], 0), (grid_wn[3], 8)):
            cut = pl.ds(first, 8)
            around(held, weight_send[cut, :], [weight_got.at[i, cut] for i in range(4)], LAT_MOVES)
        each_chunk(ORIGIN[3] - 8, ORIGIN[3] + 16, lambda at: finish_weights(3, pl.ds(at, 8)))

    def coarse_source(cycle, copies, moves):
        for copy in copies:
            copy.wait_recv()
        got = [coarse_got.at[4 * cycle + i] for i in range(len(moves))]
        around(grid_b[3], coarse_send[cycle], got, moves)

    reach_before = (
        ((-40, 72), (-24, 40), (-16, 24)),
        ((-24, 56), (-16, 32), (-8, 16)),
        ((-16, 48), (-8, 24), (-8, 16)),
    )
    reach_after = ((-24, 56), (-16, 48), (-8, 40))
    up_rows = ((-16, 32), (-8, 24), (-8, 24))
    smoothed = (grid_q[0], grid_s, grid_q[0])
    pressure = grid_p[0]

    def descend(cycle, ranges):
        for low, high in ranges[0]:
            restricted(0, low, high, smoothed[cycle])
        for low, high in ranges[1]:
            from_zero(1, low, high, grid_q[1])
        for low, high in ranges[1]:
            restricted(1, low, high, grid_q[1])
        for low, high in ranges[2]:
            from_zero(2, low, high, grid_q[2])

    def send_coarse(cycle):
        descend(cycle, (((-8, 40),), ((-8, 24),), ((-8, 16),)))
        restricted(2, -8, 16, grid_q[2])
        return coarse_links(cycle, 1 if cycle == 2 else 2)

    def outer(cycle):
        parts = [((low, 0), (32 >> g, high)) for g, (low, high) in enumerate(reach_before[cycle])]
        if cycle == 0:
            for low, high in parts[0]:
                from_zero(0, low, high, smoothed[0])
        else:
            for low, high in parts[0]:
                sweep(0, low, high, pressure, smoothed[cycle])
        descend(cycle, parts)

    from_zero(0, -8, 40, smoothed[0])
    links = send_coarse(0)
    place_far_source()
    outer(0)
    coarse_weights_around()
    for cycle in range(CYCLES):
        coarse_source(cycle, *links)
        from_zero(3, -8, 16, grid_q[3])
        here, there_ = grid_q[3], grid_p[3]
        for _ in range(SWEEPS - 1):
            sweep(3, -8, 16, here, there_)
            here, there_ = there_, here
        corrected(2, -8, 16, grid_q[2], here)
        sweep(2, -8, 16, grid_q[2], grid_p[2])
        corrected(1, *up_rows[cycle], grid_q[1], grid_p[2])
        sweep(1, *up_rows[cycle], grid_q[1], grid_p[1])
        corrected(0, -16, 48, smoothed[cycle], grid_p[1])
        sweep(0, -8, 40, smoothed[cycle], pressure)
        if cycle + 1 < CYCLES:
            sweep(0, -8, 40, pressure, smoothed[cycle + 1])
            links = send_coarse(cycle + 1)
            low, high = reach_after[cycle]
            if cycle == 0:
                corrected(0, -32, -16, smoothed[0], grid_p[1])
                corrected(0, 48, 64, smoothed[0], grid_p[1])
            sweep(0, low, -8, smoothed[cycle], pressure)
            sweep(0, 40, high, smoothed[cycle], pressure)
            outer(cycle + 1)

    own = pl.ds(ORIGIN[0], ROWS)
    p = [pressure[c, own, :] for c in range(4)]
    slope_east = [0.5 * (e - w) for e, w in zip(east_of(p, 1), west_of(p, 1))]
    slope_north = [
        0.5 * (pressure[c, pl.ds(ORIGIN[0] + 1, ROWS), :] - pressure[c, pl.ds(ORIGIN[0] - 1, ROWS), :])
        for c in range(4)
    ]
    stacked = jnp.concatenate(
        [jnp.concatenate(parts, axis=1) for parts in (p, slope_east, slope_north)], axis=0
    )
    ordered = exact_select(stacked, unchoice[...])
    p_out[...] = ordered[0:32]
    push_u = GRAVITY_STEP * ordered[32:64]
    push_v = GRAVITY_STEP * ordered[64:96]
    for k in range(LEVELS):
        rows = slice(k * ROWS, (k + 1) * ROWS)
        wet = depth > k
        u_out[rows, :] = jnp.where(wet, u_star[rows, :] - push_u, 0.0)
        v_out[rows, :] = jnp.where(wet, v_star[rows, :] - push_v, 0.0)
    for copy in started:
        copy.wait_send()


def deliver(*refs):
    held, outs, sem = refs[:4], refs[4:8], refs[8]
    copies = [pltpu.make_async_copy(held[i], outs[i], sem.at[i]) for i in range(4)]
    for copy in copies:
        copy.start()
    for copy in copies:
        copy.wait()


def shards(lon_count, lat_count, u, v, t, depth, elevation):
    f32 = jnp.float32
    flat = (LEVELS * ROWS, COLS)
    block = pl.BlockSpec(memory_space=pltpu.VMEM)

    def grids(classes=CLASSES):
        return [pltpu.VMEM((c, h, LANES), f32) for c, h in zip(classes, HEIGHT)]

    shapes = [flat] * 3 + [(ROWS, COLS)]
    anywhere = pl.BlockSpec(memory_space=pl.ANY)
    held = pl.pallas_call(
        functools.partial(kernel, lon_count, lat_count),
        out_shape=[pltpu.VMEM(shape, f32) for shape in shapes],
        in_specs=[anywhere] * 5,
        out_specs=[block] * 4,
        scratch_shapes=[
            pltpu.VMEM(flat, f32),
            pltpu.VMEM(flat, f32),
            pltpu.VMEM(flat, f32),
            pltpu.VMEM((ROWS, COLS), jnp.int32),
            pltpu.VMEM((ROWS, COLS), f32),
            pltpu.VMEM(flat, f32),
            pltpu.VMEM(flat, f32),
            pltpu.VMEM((2, 32, COLS), f32),
            pltpu.VMEM((2, 32, COLS), f32),
            pltpu.VMEM((2, 72, LANES), f32),
            pltpu.VMEM((2, 72, LANES), f32),
            pltpu.VMEM((2, 64, LANES), f32),
            pltpu.VMEM((2, 64, LANES), f32),
            pltpu.VMEM((2, ROWS, COLS), f32),
            pltpu.VMEM((2, 2, ROWS, COLS), f32),
            pltpu.VMEM((2, 2, 8, COLS), f32),
            pltpu.VMEM((4, ROWS, LANES), f32),
            pltpu.VMEM((2, 4, ROWS, LANES), f32),
            pltpu.VMEM((2, 4, 8, LANES), f32),
            pltpu.VMEM((2, 5, 8, LANES), f32),
            pltpu.VMEM((4, 5, 8, LANES), f32),
            pltpu.VMEM((16, LANES), f32),
            pltpu.VMEM((4, 16, LANES), f32),
            pltpu.VMEM((CYCLES, 8, LANES), f32),
            pltpu.VMEM((10, 8, LANES), f32),
            pltpu.VMEM((WIDE, WIDE), jnp.bfloat16),
            pltpu.VMEM((WIDE, COLS), jnp.bfloat16),
            pltpu.VMEM((4, HEIGHT[0], LANES), f32),
            grids(),
            grids(),
            grids(),
            grids(),
            [pltpu.VMEM((h, LANES), f32) for h in HEIGHT],
            grids(),
            grids(),
            grids(),
            grids(),
            pltpu.VMEM((4, HEIGHT[0], LANES), f32),
            pltpu.SemaphoreType.DMA((5,)),
            pltpu.SemaphoreType.DMA((40,)),
            pltpu.SemaphoreType.DMA((40,)),
        ],
        compiler_params=pltpu.CompilerParams(
            collective_id=0, has_side_effects=True, vmem_limit_bytes=32 << 20
        ),
    )(
        *[
            pltpu.with_memory_space_constraint(x, pltpu.HBM)
            for x in (u.reshape(flat), v.reshape(flat), t.reshape(flat), depth, elevation)
        ]
    )
    outs = pl.pallas_call(
        deliver,
        out_shape=[jax.ShapeDtypeStruct(shape, f32) for shape in shapes],
        in_specs=[block] * 4,
        out_specs=[anywhere] * 4,
        scratch_shapes=[pltpu.SemaphoreType.DMA((4,))],
    )(*[pltpu.with_memory_space_constraint(x, pltpu.VMEM) for x in held])
    shape = (LEVELS, ROWS, COLS)
    return outs[0].reshape(shape), outs[1].reshape(shape), outs[2].reshape(shape), outs[3]


def solution(mesh):
    spec3, spec2 = P(None, "lat", "lon"), P("lat", "lon")
    return jax.shard_map(
        functools.partial(shards, mesh.shape["lon"], mesh.shape["lat"]),
        mesh=mesh,
        in_specs=(spec3, spec3, spec3, spec2, spec2),
        out_specs=(spec3, spec3, spec3, spec2),
        check_vma=False,
    )
```

```python
import functools

import jax
import jax.numpy as jnp
from jax import lax
from jax.experimental import pallas as pl
from jax.experimental.pallas import tpu as pltpu
from jax.sharding import PartitionSpec as P

LEVELS = 8
CYCLES = 3
SWEEPS = 4
TIME_STEP = 0.2
VISCOSITY = 1.0
DIFFUSIVITY = 1.0
CORIOLIS = 1.0
MASS_TERM = 0.05
GRAVITY_STEP = 0.5

ROWS = 32
COLS = 256
LANES = 128
WIDE = 512
MESH_IDS = pl.DeviceIdType.MESH

CLASSES = (4, 2, 1, 1)
STEP = (1, 1, 1, 2)
ORIGIN = (48, 32, 24, 16)
HEIGHT = (144, 96, 64, 48)
MASS = tuple(MASS_TERM * 4.0**g for g in range(4))

LAT_MOVES = (1, -1, 2, -2)
EARLY_LEVELS = 5


def east_of(parts, step):
    turned = pltpu.roll(parts[0], LANES - step, 1)
    return list(parts[1:]) + [turned]


def west_of(parts, step):
    turned = pltpu.roll(parts[-1], step, 1)
    return [turned] + list(parts[:-1])


def each_chunk(first, last, body, unroll=6):
    count = (last - first) // 8
    if count <= unroll:
        for i in range(count):
            body(first + 8 * i)
        return
    while count % unroll:
        unroll -= 1

    def step(i, carry):
        for j in range(unroll):
            body(pl.multiple_of(first + (i * unroll + j) * 8, 8))
        return carry

    lax.fori_loop(0, count // unroll, step, 0)


def split_three(values):
    high = values.astype(jnp.bfloat16)
    rest = values - high.astype(jnp.float32)
    middle = rest.astype(jnp.bfloat16)
    low = (rest - middle.astype(jnp.float32)).astype(jnp.bfloat16)
    return jnp.concatenate([high, middle, low], axis=0)


def exact_select(values, choice):
    count = values.shape[0]
    product = jnp.dot(split_three(values), choice, preferred_element_type=jnp.float32)
    return (product[:count] + product[count : 2 * count]) + product[2 * count :]


class Link:
    def __init__(self, copy, leaves, comes):
        self.copy, self.leaves, self.comes = copy, leaves, comes

    def start(self):
        if self.leaves is None:
            self.copy.start()
        else:
            pl.when(self.leaves)(self.copy.start)

    def wait_send(self):
        if self.leaves is None:
            self.copy.wait_send()
        else:
            pl.when(self.leaves)(self.copy.wait_send)

    def wait_recv(self):
        if self.comes is None:
            self.copy.wait_recv()
        else:
            pl.when(self.comes)(self.copy.wait_recv)


def kernel(
    lon_count,
    lat_count,
    u_far,
    v_far,
    t_far,
    depth_far,
    elevation_far,
    u_out,
    v_out,
    t_out,
    p_out,
    u_ref,
    v_ref,
    t_ref,
    depth_ref,
    elevation_ref,
    u_star,
    v_star,
    rows_send,
    rows_got,
    cols_send,
    cols_got,
    mean_send,
    mean_got,
    deep_send,
    deep_got,
    deep_got_far,
    source_send,
    source_got,
    source_got_far,
    close_send,
    close_got,
    weight_send,
    weight_got,
    coarse_send,
    coarse_got,
    choice,
    unchoice,
    deep,
    grid_b,
    grid_p,
    grid_q,
    grid_we,
    grid_ww,
    grid_wn,
    grid_dg,
    grid_iv,
    grid_r,
    grid_s,
    load_sem,
    send_sem,
    recv_sem,
):
    lon = lax.axis_index("lon")
    lat = lax.axis_index("lat")
    sems = iter(range(64))

    def there(lon_move, lat_move):
        return {
            "lon": lax.rem(lon + lon_move + lon_count, lon_count),
            "lat": lax.rem(lat + lat_move + lat_count, lat_count),
        }

    def send(source, target, lon_move, lat_move):
        at = next(sems)
        copy = pltpu.make_async_remote_copy(
            src_ref=source,
            dst_ref=target,
            send_sem=send_sem.at[at],
            recv_sem=recv_sem.at[at],
            device_id=there(lon_move, lat_move),
            device_id_type=MESH_IDS,
        )
        if lat_move == 0:
            return Link(copy, None, None)
        return Link(copy, inside(lat_move), inside(-lat_move))

    def inside(lat_move):
        return (lat + lat_move >= 0) & (lat + lat_move < lat_count)

    def kept(lat_move, values):
        if lat_move == 0:
            return values
        return jnp.where(inside(lat_move), values, jnp.zeros_like(values))

    started = []

    def launch(copies):
        for copy in copies:
            copy.start()
        started.extend(copies)

    barrier = pltpu.get_barrier_semaphore()
    for lon_move in (1, -1):
        pl.semaphore_signal(
            barrier, inc=1, device_id=there(lon_move, 0), device_id_type=MESH_IDS
        )
    beside_count = jnp.int32(2)
    for lat_move in LAT_MOVES:
        beside_count = beside_count + inside(lat_move).astype(jnp.int32)

        @pl.when(inside(lat_move))
        def _(lat_move=lat_move):
            pl.semaphore_signal(
                barrier, inc=1, device_id=there(0, lat_move), device_id_type=MESH_IDS
            )


    loads = [
        pltpu.make_async_copy(far, near, load_sem.at[i])
        for i, (far, near) in enumerate(
            (
                (depth_far, depth_ref),
                (elevation_far, elevation_ref),
                (u_far, u_ref),
                (v_far, v_ref),
                (t_far, t_ref),
            )
        )
    ]
    for load in loads:
        load.start()
    for load in loads:
        load.wait()

    depth = depth_ref[...].astype(jnp.float32)
    lane8 = lax.broadcasted_iota(jnp.int32, (8, LANES), 1)
    fields = (u_ref, v_ref, t_ref)
    for side, row in ((0, ROWS - 1), (1, 0)):
        for f, field in enumerate(fields):
            for k in range(LEVELS):
                rows_send[side, 8 * f + k : 8 * f + k + 1, :] = field[
                    k * ROWS + row : k * ROWS + row + 1, :
                ]
        rows_send[side, pl.ds(24, 8), :] = jnp.broadcast_to(depth[row : row + 1, :], (8, COLS))

    def pack(i, carry):
        at_last, at_first = carry
        rows = pl.ds(pl.multiple_of(8 * i, 8), 8)
        for f, field in enumerate(fields):
            here = lane8 == i + 32 * f
            at_last = jnp.where(here, field[rows, COLS - 1 : COLS], at_last)
            at_first = jnp.where(here, field[rows, 0:1], at_first)
        return at_last, at_first

    zero8 = jnp.zeros((8, LANES), jnp.float32)
    at_last, at_first = lax.fori_loop(0, 32, pack, (zero8, zero8), unroll=4)
    elevation = elevation_ref[...]
    deep_send[0] = depth
    for side, edge, tile in ((0, at_last, 1), (1, at_first, 0)):
        cut = slice(tile * LANES, (tile + 1) * LANES)
        cols_send[side, 0:32, :] = depth[:, cut]
        cols_send[side, 32:64, :] = elevation[:, cut]
        cols_send[side, 64:72, :] = edge

    pl.semaphore_wait(barrier, beside_count)
    row_copies = [
        send(rows_send.at[0], rows_got.at[0], 0, 1),
        send(rows_send.at[1], rows_got.at[1], 0, -1),
    ]
    column_copies = [
        send(cols_send.at[0], cols_got.at[0], 1, 0),
        send(cols_send.at[1], cols_got.at[1], -1, 0),
    ]
    launch(column_copies + row_copies)

    def depth_sends(part):
        source = deep_send.at[part]
        return [
            send(source, deep_got.at[part, 0], 0, 1),
            send(source, deep_got.at[part, 1], 0, -1),
            send(source.at[pl.ds(ROWS - 8, 8)], deep_got_far.at[part, 0], 0, 2),
            send(source.at[pl.ds(0, 8)], deep_got_far.at[part, 1], 0, -2),
        ]

    depth_copies = depth_sends(0)
    launch(depth_copies)

    row_number = lax.broadcasted_iota(jnp.int32, (ROWS, LANES), 0)
    place = (lat * ROWS + row_number).astype(jnp.float32)
    angle = jnp.pi * ((place + 0.5) / (ROWS * lat_count) - 0.5)
    turning = CORIOLIS * jnp.sin(angle)
    rotation = jnp.concatenate([turning, turning], axis=1)

    row = lax.broadcasted_iota(jnp.int32, (ROWS, COLS), 0)
    column = lax.broadcasted_iota(jnp.int32, (ROWS, COLS), 1)
    on_east, on_west = column == COLS - 1, column == 0
    on_north, on_south = row == ROWS - 1, row == 0

    def beside(values, east_edge, west_edge, north_edge, south_edge):
        return (
            jnp.where(on_east, east_edge, pltpu.roll(values, COLS - 1, 1)),
            jnp.where(on_west, west_edge, pltpu.roll(values, 1, 1)),
            jnp.where(on_north, north_edge, pltpu.roll(values, ROWS - 1, 0)),
            jnp.where(on_south, south_edge, pltpu.roll(values, 1, 0)),
        )

    def laplace(faces, values, nearby):
        terms = [jnp.where(face, near - values, 0.0) for face, near in zip(faces, nearby)]
        return (terms[0] + terms[1]) + (terms[2] + terms[3])

    def momentum(faces, u, near_u, v, near_v):
        guess_u = u + TIME_STEP * (VISCOSITY * laplace(faces, u, near_u) + rotation * v)
        guess_v = v + TIME_STEP * (VISCOSITY * laplace(faces, v, near_v) - rotation * u)
        return guess_u, guess_v

    inner_depth = [jnp.minimum(depth, near) for near in beside(depth, 0.0, 0.0, 0.0, 0.0)]

    def inner(k, carry):
        sum_u, sum_v = carry
        level = k.astype(jnp.float32)
        faces = [level < limit for limit in inner_depth]
        rows = pl.ds(pl.multiple_of(k * ROWS, ROWS), ROWS)
        u, v = u_ref[rows, :], v_ref[rows, :]
        near_u, near_v = beside(u, 0.0, 0.0, 0.0, 0.0), beside(v, 0.0, 0.0, 0.0, 0.0)
        guess_u, guess_v = momentum(faces, u, near_u, v, near_v)
        wet = level < depth
        return sum_u + jnp.where(wet, guess_u, 0.0), sum_v + jnp.where(wet, guess_v, 0.0)

    zero = jnp.zeros((ROWS, COLS), jnp.float32)
    sum_u, sum_v = lax.fori_loop(0, LEVELS, inner, (zero, zero))
    gain = TIME_STEP * VISCOSITY / LEVELS

    for copy in row_copies:
        copy.wait_recv()
    north_depth = kept(1, rows_got[1, 24:25, :])
    south_depth = kept(-1, rows_got[0, 24:25, :])
    level8 = lax.broadcasted_iota(jnp.int32, (LEVELS, COLS), 0).astype(jnp.float32)

    def row_flux(f, side, limit):
        step = rows_got[side, 8 * f : 8 * f + 8, :] - rows_send[1 - side, 8 * f : 8 * f + 8, :]
        return gain * jnp.sum(jnp.where(level8 < limit, step, 0.0), axis=0, keepdims=True)

    north_limit = jnp.minimum(depth[ROWS - 1 : ROWS, :], north_depth)
    south_limit = jnp.minimum(depth[0:1, :], south_depth)

    def mean(f, total):
        return (
            total * (1.0 / LEVELS)
            + jnp.where(on_north, row_flux(f, 1, north_limit), 0.0)
            + jnp.where(on_south, row_flux(f, 0, south_limit), 0.0)
        )

    mean_u, mean_v = mean(0, sum_u), mean(1, sum_v)
    for side, tile in ((0, 1), (1, 0)):
        cut = slice(tile * LANES, (tile + 1) * LANES)
        mean_send[side, 0:32, :] = mean_u[:, cut]
        mean_send[side, 32:64, :] = mean_v[:, cut]
    mean_copies = [
        send(mean_send.at[0], mean_got.at[0], 1, 0),
        send(mean_send.at[1], mean_got.at[1], -1, 0),
    ]
    launch(mean_copies)

    def order(n):
        return ((((n & 127) + 32) & 127) << 2) + (n >> 7)

    wanted = order(lax.broadcasted_iota(jnp.int32, (1, WIDE), 1))

    def fill(i, carry):
        rows = pl.ds(pl.multiple_of(32 * i, 32), 32)
        k = lax.broadcasted_iota(jnp.int32, (32, WIDE), 0) + 32 * i
        choice[rows, :] = jnp.where(k == wanted, 1.0, 0.0).astype(jnp.bfloat16)
        n = lax.broadcasted_iota(jnp.int32, (32, COLS), 0) + 32 * i
        column = lax.broadcasted_iota(jnp.int32, (32, COLS), 1) + LANES
        unchoice[rows, :] = jnp.where(order(n) == column, 1.0, 0.0).astype(jnp.bfloat16)
        return carry

    lax.fori_loop(0, WIDE // 32, fill, 0)
    for ref in list(grid_p) + list(grid_q) + list(grid_b) + list(grid_wn) + [deep, grid_s]:
        ref[...] = jnp.zeros_like(ref)
    for copy in column_copies:
        copy.wait_recv()

    west_tile, east_tile = cols_got.at[0], cols_got.at[1]
    deep_send[1, :, 0:LANES] = west_tile[0:32, :]
    deep_send[1, :, LANES:COLS] = east_tile[0:32, :]
    more_depth = depth_sends(1)
    launch(more_depth)
    depth_copies = depth_copies + more_depth

    lane_row = lane8 & 3
    lane_level = ((lane8 >> 2) & 7).astype(jnp.float32)

    def packed(values, column):
        result = zero8
        for g in range(4):
            result = jnp.where(lane_row == g, values[8 * g : 8 * g + 8, column : column + 1], result)
        return result

    def column_flux(own, other, own_depth, other_depth):
        limit = jnp.minimum(own_depth, other_depth)
        flux = jnp.where(lane_level < limit, other - own, 0.0)
        for turn in (4, 8, 16):
            flux = flux + pltpu.roll(flux, turn, 1)
        flux = gain * flux
        return [
            jnp.concatenate([flux[:, at + g : at + g + 1] for g in range(4)], axis=0)
            for at in (28, 60)
        ]

    east_flux = column_flux(
        cols_send[0, 64:72, :],
        east_tile[64:72, :],
        packed(depth, COLS - 1),
        packed(east_tile[0:32, :], 0),
    )
    west_flux = column_flux(
        cols_send[1, 64:72, :],
        west_tile[64:72, :],
        packed(depth, 0),
        packed(west_tile[0:32, :], LANES - 1),
    )

    depth_near = beside(
        depth,
        east_tile[0:32, 0:1],
        west_tile[0:32, LANES - 1 : LANES],
        north_depth,
        south_depth,
    )
    open_depth = [jnp.minimum(depth, near) for near in depth_near]
    east_edges = east_tile[64:72, :]
    west_edges = west_tile[64:72, :]

    def near_field(f, field, k):
        values = field[pl.ds(pl.multiple_of(k * ROWS, ROWS), ROWS), :]
        turn = lax.rem(2 * LANES - 32 * f - 4 * k, LANES)
        east_lanes = pltpu.roll(east_edges, turn, 1)
        west_lanes = pltpu.roll(west_edges, turn, 1)
        east_edge = jnp.concatenate([east_lanes[:, g : g + 1] for g in range(4)], axis=0)
        west_edge = jnp.concatenate([west_lanes[:, g : g + 1] for g in range(4)], axis=0)
        north_edge = kept(1, rows_got[1, pl.ds(8 * f + k, 1), :])
        south_edge = kept(-1, rows_got[0, pl.ds(8 * f + k, 1), :])
        return values, beside(values, east_edge, west_edge, north_edge, south_edge)

    def layer(k, carry):
        level = k.astype(jnp.float32)
        faces = [level < limit for limit in open_depth]
        t, near_t = near_field(2, t_ref, k)
        u, near_u = near_field(0, u_ref, k)
        v, near_v = near_field(1, v_ref, k)
        spread = laplace(faces, t, near_t)
        east = jnp.where(faces[0], (u + near_u[0]) * 0.5, 0.0)
        west = jnp.where(faces[1], (near_u[1] + u) * 0.5, 0.0)
        north = jnp.where(faces[2], (v + near_v[2]) * 0.5, 0.0)
        south = jnp.where(faces[3], (near_v[3] + v) * 0.5, 0.0)
        transport = (east * (t + near_t[0]) - west * (near_t[1] + t)) + (
            north * (t + near_t[2]) - south * (near_t[3] + t)
        )
        result = t + TIME_STEP * (DIFFUSIVITY * spread - 0.5 * transport)
        guess_u, guess_v = momentum(faces, u, near_u, v, near_v)
        wet = level < depth
        rows = pl.ds(pl.multiple_of(k * ROWS, ROWS), ROWS)
        u_star[rows, :] = jnp.where(wet, guess_u, 0.0)
        v_star[rows, :] = jnp.where(wet, guess_v, 0.0)
        t_out[rows, :] = jnp.where(wet, result, 0.0)
        return carry

    lax.fori_loop(0, EARLY_LEVELS, layer, 0)

    for copy in mean_copies:
        copy.wait_recv()
    west_mean, east_mean = mean_got.at[0], mean_got.at[1]
    tile_lane = lax.broadcasted_iota(jnp.int32, (ROWS, LANES), 1)
    tile_first, tile_last = tile_lane == 0, tile_lane == LANES - 1

    def window(f, values):
        cut = slice(32 * f, 32 * f + 32)
        return jnp.concatenate(
            [
                west_mean[cut, :] - jnp.where(tile_last, west_flux[f], 0.0),
                values[:, 0:LANES] + jnp.where(tile_first, west_flux[f], 0.0),
                values[:, LANES:COLS] + jnp.where(tile_last, east_flux[f], 0.0),
                east_mean[cut, :] - jnp.where(tile_first, east_flux[f], 0.0),
            ],
            axis=1,
        )

    wide_u, wide_v = window(0, mean_u), window(1, mean_v)
    wide_eta = jnp.concatenate([west_tile[32:64, :], elevation, east_tile[32:64, :]], axis=1)
    wide_row = lax.broadcasted_iota(jnp.int32, (ROWS, WIDE), 0)
    north_v = jnp.where(wide_row == ROWS - 1, 0.0, pltpu.roll(wide_v, ROWS - 1, 0))
    south_v = jnp.where(wide_row == 0, 0.0, pltpu.roll(wide_v, 1, 0))
    across = pltpu.roll(wide_u, WIDE - 1, 1) - pltpu.roll(wide_u, 1, 1)
    depth_wide = jnp.concatenate([west_tile[0:32, :], depth, east_tile[0:32, :]], axis=1)
    source = jnp.where(
        depth_wide > 0.5, wide_eta - 0.5 * (across + (north_v - south_v)), 0.0
    )
    ends = jnp.where(
        lax.broadcasted_iota(jnp.int32, (16, WIDE), 0) == 0, wide_v[0:1, :], wide_v[31:32, :]
    )
    by_class = exact_select(jnp.concatenate([source, ends], axis=0), choice[...])
    for c in range(4):
        cut = slice(LANES * c, LANES * (c + 1))
        source_send[c] = by_class[0:32, cut]
        close_send[0, c] = by_class[24:32, cut]
        close_send[1, c] = by_class[0:8, cut]
        for side in (0, 1):
            close_send[side, 4, c : c + 1, :] = by_class[32:33, cut]
            close_send[side, 4, 4 + c : 5 + c, :] = by_class[33:34, cut]
    source_copies = [
        send(close_send.at[0], close_got.at[0], 0, 1),
        send(close_send.at[1], close_got.at[1], 0, -1),
    ]
    far_copies = [
        send(close_send.at[0, 4], close_got.at[2, 4], 0, 2),
        send(close_send.at[1, 4], close_got.at[3, 4], 0, -2),
        send(source_send.at[:, pl.ds(0, 24)], source_got.at[0, :, pl.ds(0, 24)], 0, 1),
        send(source_send.at[:, pl.ds(8, 24)], source_got.at[1, :, pl.ds(8, 24)], 0, -1),
        send(source_send.at[:, pl.ds(ROWS - 8, 8)], source_got_far.at[0], 0, 2),
        send(source_send.at[:, pl.ds(0, 8)], source_got_far.at[1], 0, -2),
    ]
    launch(source_copies + far_copies)

    for copy in depth_copies:
        copy.wait_recv()

    def slot_of(lat_move):
        return LAT_MOVES.index(-lat_move)

    def wide_depth(own, halo, move):
        return kept(move, jnp.concatenate([halo[:, 0:LANES], own, halo[:, LANES:COLS]], axis=1))

    blocks = [
        wide_depth(deep_got_far[0, 0], deep_got_far[1, 0], -2),
        wide_depth(deep_got[0, 0], deep_got[1, 0], -1),
        wide_depth(deep_send[0], deep_send[1], 0),
        wide_depth(deep_got[0, 1], deep_got[1, 1], 1),
        wide_depth(deep_got_far[0, 1], deep_got_far[1, 1], 2),
    ]
    by_class = jnp.dot(
        jnp.concatenate(blocks, axis=0).astype(jnp.bfloat16),
        choice[...],
        preferred_element_type=jnp.float32,
    )
    for c in range(4):
        deep[c, pl.ds(ORIGIN[0] - 40, 112), :] = by_class[:, LANES * c : LANES * (c + 1)]

    def finish_weights(g, rows):
        we = [grid_we[g][c, rows, :] for c in range(CLASSES[g])]
        ww = west_of(we, STEP[g])
        grid_ww[g][rows, :] = ww[0]
        before = pl.ds(rows.start - 1, 8)
        for c in range(CLASSES[g]):
            near = (we[c] + ww[c]) + (grid_wn[g][c, rows, :] + grid_wn[g][c, before, :])
            grid_dg[g][c, rows, :] = MASS[g] + near
            grid_iv[g][c, rows, :] = 1.0 / (MASS[g] + 2.0 * near)

    def fine_weights(at):
        rows, after = pl.ds(at, 8), pl.ds(at + 1, 8)
        columns = [deep[c, rows, :] * (1.0 / LEVELS) for c in range(4)]
        for c, near in enumerate(east_of(columns, 1)):
            grid_we[0][c, rows, :] = jnp.minimum(columns[c], near)
            north = deep[c, after, :] * (1.0 / LEVELS)
            grid_wn[0][c, rows, :] = jnp.minimum(columns[c], north)

    def whole(g):
        return tuple(ORIGIN[g] + end for end in ((-40, 72), (-24, 40), (-16, 24), (0, 8))[g])

    def pair_lanes(values):
        even = (lax.broadcasted_iota(jnp.int32, values.shape, 1) & 1) == 0
        return even, pltpu.roll(values, LANES - 1, 1), pltpu.roll(values, 1, 1)

    def finer_rows(g, at):
        return 2 * (at - ORIGIN[g]) + ORIGIN[g - 1]

    each_chunk(*whole(0), fine_weights)
    each_chunk(*whole(0), lambda at: finish_weights(0, pl.ds(at, 8)))
    for g in (1, 2, 3):

        def coarse_weights(at, g=g):
            rows = pl.ds(at, 8)
            above = finer_rows(g, at)
            even_rows, odd_rows = pl.ds(above, 8, stride=2), pl.ds(above + 1, 8, stride=2)
            finer_we, finer_wn = grid_we[g - 1], grid_wn[g - 1]
            if g < 3:
                for c in range(CLASSES[g]):
                    grid_we[g][c, rows, :] = (
                        finer_we[2 * c + 1, even_rows, :] + finer_we[2 * c + 1, odd_rows, :]
                    )
                    grid_wn[g][c, rows, :] = (
                        finer_wn[2 * c, odd_rows, :] + finer_wn[2 * c + 1, odd_rows, :]
                    )
            else:
                we = finer_we[0, even_rows, :] + finer_we[0, odd_rows, :]
                even, east, west = pair_lanes(we)
                grid_we[g][0, rows, :] = jnp.where(even, east, we)
                wn = finer_wn[0, odd_rows, :]
                even, east, west = pair_lanes(wn)
                grid_wn[g][0, rows, :] = wn + jnp.where(even, east, west)

        each_chunk(*whole(g), coarse_weights)
        if g < 3:
            each_chunk(*whole(g), lambda at, g=g: finish_weights(g, pl.ds(at, 8)))

    upper = lax.broadcasted_iota(jnp.int32, (8, LANES), 0) >= 4

    def around(held, own, got, moves):
        def block(move):
            return kept(move, got[moves.index(-move)][...])

        held[0, pl.ds(ORIGIN[3], 8), :] = jnp.where(upper, pltpu.roll(block(1), 4, 0), own)
        lower = pltpu.roll(block(-1), 4, 0)
        if len(moves) == 4:
            lower = jnp.where(upper, lower, block(-2))
            held[0, pl.ds(ORIGIN[3] + 8, 8), :] = block(2)
        held[0, pl.ds(ORIGIN[3] - 8, 8), :] = lower

    weight_send[0:8, :] = grid_we[3][0, pl.ds(ORIGIN[3], 8), :]
    weight_send[8:16, :] = grid_wn[3][0, pl.ds(ORIGIN[3], 8), :]
    weight_copies = [
        send(weight_send, weight_got.at[i], 0, move) for i, move in enumerate(LAT_MOVES)
    ]
    launch(weight_copies)

    lax.fori_loop(EARLY_LEVELS, LEVELS, layer, 0)
    for copy in source_copies:
        copy.wait_recv()

    rows32 = lax.broadcasted_iota(jnp.int32, (ROWS, LANES), 0)

    def ends(move, spot):
        held = close_send.at[0, 4] if move == 0 else close_got.at[slot_of(move), 4]
        return 0.5 * kept(move, held[spot : spot + 1, :])

    def place_source(move, low, high, held):
        at = rows32[: high - low] + low
        for c in range(4):
            rows = pl.ds(ORIGIN[0] + 32 * move + low, high - low)
            values = held[c]
            if move < 2 and high == ROWS:
                values = values - jnp.where(at == ROWS - 1, ends(move + 1, c), 0.0)
            if move > -2 and low == 0:
                values = values + jnp.where(at == 0, ends(move - 1, 4 + c), 0.0)
            grid_b[0][c, rows, :] = jnp.where(deep[c, rows, :] > 0.5, values, 0.0)

    place_source(-1, 24, 32, close_got.at[0])
    place_source(0, 0, 32, source_send)
    place_source(1, 0, 8, close_got.at[1])

    def place_far_source():
        for copy in far_copies:
            copy.wait_recv()
        place_source(-2, 24, 32, source_got_far.at[0])
        place_source(-1, 0, 24, source_got.at[0, :, pl.ds(0, 24)])
        place_source(1, 8, 32, source_got.at[1, :, pl.ds(8, 24)])
        place_source(2, 0, 8, source_got_far.at[1])

    def operator(g, held, at):
        rows, after, before = pl.ds(at, 8), pl.ds(at + 1, 8), pl.ds(at - 1, 8)
        count = CLASSES[g]
        p = [held[c, rows, :] for c in range(count)]
        we = [grid_we[g][c, rows, :] for c in range(count)]
        ww = [grid_ww[g][rows, :]] + we[:-1]
        pe, pw = east_of(p, STEP[g]), west_of(p, STEP[g])
        residual = []
        for c in range(count):
            pull = (we[c] * pe[c] + ww[c] * pw[c]) + (
                grid_wn[g][c, rows, :] * held[c, after, :]
                + grid_wn[g][c, before, :] * held[c, before, :]
            )
            image = grid_dg[g][c, rows, :] * p[c] - pull
            residual.append(grid_b[g][c, rows, :] - image)
        return p, residual

    def span(g, low, high):
        return ORIGIN[g] + low, ORIGIN[g] + high

    def from_zero(g, low, high, held):
        def body(at):
            rows = pl.ds(at, 8)
            for c in range(CLASSES[g]):
                held[c, rows, :] = grid_b[g][c, rows, :] * grid_iv[g][c, rows, :]

        each_chunk(*span(g, low, high), body)

    def sweep(g, low, high, held, result):
        def body(at):
            rows = pl.ds(at, 8)
            p, residual = operator(g, held, at)
            for c in range(CLASSES[g]):
                result[c, rows, :] = p[c] + residual[c] * grid_iv[g][c, rows, :]

        each_chunk(*span(g, low, high), body)

    def restricted(g, low, high, held):
        def residual_rows(at):
            rows = pl.ds(at, 8)
            _, residual = operator(g, held, at)
            if g < 2:
                for c in range(CLASSES[g] // 2):
                    grid_r[g][c, rows, :] = residual[2 * c] + residual[2 * c + 1]
            else:
                even, east, west = pair_lanes(residual[0])
                grid_r[g][0, rows, :] = residual[0] + jnp.where(even, east, west)

        each_chunk(*span(g, low, high), residual_rows)

        def pair_rows(at):
            above = finer_rows(g + 1, at)
            for c in range(CLASSES[g + 1]):
                grid_b[g + 1][c, pl.ds(at, 8), :] = (
                    grid_r[g][c, pl.ds(above, 8, stride=2), :]
                    + grid_r[g][c, pl.ds(above + 1, 8, stride=2), :]
                )

        top = (high // 2 + 7) // 8 * 8
        each_chunk(*span(g + 1, low // 2 // 8 * 8, top), pair_rows)

    def corrected(g, low, high, held, correction):
        first, last = low // 2 // 8 * 8, (high // 2 + 7) // 8 * 8

        def body(at):
            above = finer_rows(g + 1, at)
            for c in range(CLASSES[g]):
                change = correction[c // 2, pl.ds(at, 8), :]
                for odd in (0, 1):
                    rows = pl.ds(above + odd, 8, stride=2)
                    held[c, rows, :] = held[c, rows, :] + change

        each_chunk(*span(g + 1, first, last), body)

    def coarse_links(cycle, reach):
        coarse_send[cycle] = grid_b[3][0, pl.ds(ORIGIN[3], 8), :]
        moves = LAT_MOVES[: 2 * reach]
        copies = [
            send(coarse_send.at[cycle], coarse_got.at[4 * cycle + i], 0, move)
            for i, move in enumerate(moves)
        ]
        launch(copies)
        return copies, moves

    def coarse_weights_around():
        for copy in weight_copies:
            copy.wait_recv()
        for held, first in ((grid_we[3], 0), (grid_wn[3], 8)):
            cut = pl.ds(first, 8)
            around(held, weight_send[cut, :], [weight_got.at[i, cut] for i in range(4)], LAT_MOVES)
        each_chunk(ORIGIN[3] - 8, ORIGIN[3] + 16, lambda at: finish_weights(3, pl.ds(at, 8)))

    def coarse_source(cycle, copies, moves):
        for copy in copies:
            copy.wait_recv()
        got = [coarse_got.at[4 * cycle + i] for i in range(len(moves))]
        around(grid_b[3], coarse_send[cycle], got, moves)

    reach_before = (
        ((-40, 72), (-24, 40), (-16, 24)),
        ((-24, 56), (-16, 32), (-8, 16)),
        ((-16, 48), (-8, 24), (-8, 16)),
    )
    reach_after = ((-24, 56), (-16, 48), (-8, 40))
    up_rows = ((-16, 32), (-8, 24), (-8, 24))
    smoothed = (grid_q[0], grid_s, grid_q[0])
    pressure = grid_p[0]

    def descend(cycle, ranges):
        for low, high in ranges[0]:
            restricted(0, low, high, smoothed[cycle])
        for low, high in ranges[1]:
            from_zero(1, low, high, grid_q[1])
        for low, high in ranges[1]:
            restricted(1, low, high, grid_q[1])
        for low, high in ranges[2]:
            from_zero(2, low, high, grid_q[2])

    def send_coarse(cycle):
        descend(cycle, (((-8, 40),), ((-8, 24),), ((-8, 16),)))
        restricted(2, -8, 16, grid_q[2])
        return coarse_links(cycle, 1 if cycle == 2 else 2)

    def outer(cycle):
        parts = [((low, 0), (32 >> g, high)) for g, (low, high) in enumerate(reach_before[cycle])]
        if cycle == 0:
            for low, high in parts[0]:
                from_zero(0, low, high, smoothed[0])
        else:
            for low, high in parts[0]:
                sweep(0, low, high, pressure, smoothed[cycle])
        descend(cycle, parts)

    from_zero(0, -8, 40, smoothed[0])
    links = send_coarse(0)
    place_far_source()
    outer(0)
    coarse_weights_around()
    for cycle in range(CYCLES):
        coarse_source(cycle, *links)
        from_zero(3, -8, 16, grid_q[3])
        here, there_ = grid_q[3], grid_p[3]
        for _ in range(SWEEPS - 1):
            sweep(3, -8, 16, here, there_)
            here, there_ = there_, here
        corrected(2, -8, 16, grid_q[2], here)
        sweep(2, -8, 16, grid_q[2], grid_p[2])
        corrected(1, *up_rows[cycle], grid_q[1], grid_p[2])
        sweep(1, *up_rows[cycle], grid_q[1], grid_p[1])
        corrected(0, -16, 48, smoothed[cycle], grid_p[1])
        sweep(0, -8, 40, smoothed[cycle], pressure)
        if cycle + 1 < CYCLES:
            sweep(0, -8, 40, pressure, smoothed[cycle + 1])
            links = send_coarse(cycle + 1)
            low, high = reach_after[cycle]
            if cycle == 0:
                corrected(0, -32, -16, smoothed[0], grid_p[1])
                corrected(0, 48, 64, smoothed[0], grid_p[1])
            sweep(0, low, -8, smoothed[cycle], pressure)
            sweep(0, 40, high, smoothed[cycle], pressure)
            outer(cycle + 1)

    own = pl.ds(ORIGIN[0], ROWS)
    p = [pressure[c, own, :] for c in range(4)]
    slope_east = [0.5 * (e - w) for e, w in zip(east_of(p, 1), west_of(p, 1))]
    slope_north = [
        0.5 * (pressure[c, pl.ds(ORIGIN[0] + 1, ROWS), :] - pressure[c, pl.ds(ORIGIN[0] - 1, ROWS), :])
        for c in range(4)
    ]
    stacked = jnp.concatenate(
        [jnp.concatenate(parts, axis=1) for parts in (p, slope_east, slope_north)], axis=0
    )
    ordered = exact_select(stacked, unchoice[...])
    p_out[...] = ordered[0:32]
    push_u = GRAVITY_STEP * ordered[32:64]
    push_v = GRAVITY_STEP * ordered[64:96]
    for k in range(LEVELS):
        rows = slice(k * ROWS, (k + 1) * ROWS)
        wet = depth > k
        u_out[rows, :] = jnp.where(wet, u_star[rows, :] - push_u, 0.0)
        v_out[rows, :] = jnp.where(wet, v_star[rows, :] - push_v, 0.0)
    for copy in started:
        copy.wait_send()


def deliver(*refs):
    held, outs, sem = refs[:4], refs[4:8], refs[8]
    copies = [pltpu.make_async_copy(held[i], outs[i], sem.at[i]) for i in range(4)]
    for copy in copies:
        copy.start()
    for copy in copies:
        copy.wait()


def shards(lon_count, lat_count, u, v, t, depth, elevation):
    f32 = jnp.float32
    flat = (LEVELS * ROWS, COLS)
    block = pl.BlockSpec(memory_space=pltpu.VMEM)

    def grids(classes=CLASSES):
        return [pltpu.VMEM((c, h, LANES), f32) for c, h in zip(classes, HEIGHT)]

    shapes = [flat] * 3 + [(ROWS, COLS)]
    anywhere = pl.BlockSpec(memory_space=pl.ANY)
    held = pl.pallas_call(
        functools.partial(kernel, lon_count, lat_count),
        out_shape=[pltpu.VMEM(shape, f32) for shape in shapes],
        in_specs=[anywhere] * 5,
        out_specs=[block] * 4,
        scratch_shapes=[
            pltpu.VMEM(flat, f32),
            pltpu.VMEM(flat, f32),
            pltpu.VMEM(flat, f32),
            pltpu.VMEM((ROWS, COLS), jnp.int32),
            pltpu.VMEM((ROWS, COLS), f32),
            pltpu.VMEM(flat, f32),
            pltpu.VMEM(flat, f32),
            pltpu.VMEM((2, 32, COLS), f32),
            pltpu.VMEM((2, 32, COLS), f32),
            pltpu.VMEM((2, 72, LANES), f32),
            pltpu.VMEM((2, 72, LANES), f32),
            pltpu.VMEM((2, 64, LANES), f32),
            pltpu.VMEM((2, 64, LANES), f32),
            pltpu.VMEM((2, ROWS, COLS), f32),
            pltpu.VMEM((2, 2, ROWS, COLS), f32),
            pltpu.VMEM((2, 2, 8, COLS), f32),
            pltpu.VMEM((4, ROWS, LANES), f32),
            pltpu.VMEM((2, 4, ROWS, LANES), f32),
            pltpu.VMEM((2, 4, 8, LANES), f32),
            pltpu.VMEM((2, 5, 8, LANES), f32),
            pltpu.VMEM((4, 5, 8, LANES), f32),
            pltpu.VMEM((16, LANES), f32),
            pltpu.VMEM((4, 16, LANES), f32),
            pltpu.VMEM((CYCLES, 8, LANES), f32),
            pltpu.VMEM((10, 8, LANES), f32),
            pltpu.VMEM((WIDE, WIDE), jnp.bfloat16),
            pltpu.VMEM((WIDE, COLS), jnp.bfloat16),
            pltpu.VMEM((4, HEIGHT[0], LANES), f32),
            grids(),
            grids(),
            grids(),
            grids(),
            [pltpu.VMEM((h, LANES), f32) for h in HEIGHT],
            grids(),
            grids(),
            grids(),
            grids(),
            pltpu.VMEM((4, HEIGHT[0], LANES), f32),
            pltpu.SemaphoreType.DMA((5,)),
            pltpu.SemaphoreType.DMA((40,)),
            pltpu.SemaphoreType.DMA((40,)),
        ],
        compiler_params=pltpu.CompilerParams(
            collective_id=0, has_side_effects=True, vmem_limit_bytes=32 << 20
        ),
    )(
        *[
            pltpu.with_memory_space_constraint(x, pltpu.HBM)
            for x in (u.reshape(flat), v.reshape(flat), t.reshape(flat), depth, elevation)
        ]
    )
    outs = pl.pallas_call(
        deliver,
        out_shape=[jax.ShapeDtypeStruct(shape, f32) for shape in shapes],
        in_specs=[block] * 4,
        out_specs=[anywhere] * 4,
        scratch_shapes=[pltpu.SemaphoreType.DMA((4,))],
    )(*[pltpu.with_memory_space_constraint(x, pltpu.VMEM) for x in held])
    shape = (LEVELS, ROWS, COLS)
    return outs[0].reshape(shape), outs[1].reshape(shape), outs[2].reshape(shape), outs[3]


def solution(mesh):
    spec3, spec2 = P(None, "lat", "lon"), P("lat", "lon")
    return jax.shard_map(
        functools.partial(shards, mesh.shape["lon"], mesh.shape["lat"]),
        mesh=mesh,
        in_specs=(spec3, spec3, spec3, spec2, spec2),
        out_specs=(spec3, spec3, spec3, spec2),
        check_vma=False,
    )
```
